32 devices in a mesh: section: 2 (over x), dp: 16 (over z, y, core).
Axes of the slice: x: 2, y: 2, z: 4, core: 2. Of those that a mesh axis runs over, the one named last changes fastest.
Arguments:
- entering_tokens: bfloat16 [4, 16, 256, 384], P(None, 'dp'), may hold values from -6 to 6
- output_sensitivity: bfloat16 [4, 16, 256, 384], P(None, 'dp'), may hold values from -6 to 6
- picture_tile_extents: int32 [4, 16, 2], P(None, 'dp'), may hold values from 8 to 16
- pointwise_enlarge: bfloat16 [384, 1536], replicated, may hold values from -0.3125 to 0.3125
- enlarge_bias: float32 [1536], replicated, may hold values from -3 to 3
- channelwise_kernel: float32 [9, 1536], replicated, may hold values from -2 to 2
- channelwise_conv_bias: float32 [1536], replicated, may hold values from -3 to 3
- pointwise_contract: bfloat16 [1536, 384], replicated, may hold values from -0.15625 to 0.15625
- convblock_scale: float32 [384], replicated, may hold values from 0.1 to 1.9
- convblock_offset: float32 [384], replicated, may hold values from -3 to 3
- attend_scale: float32 [384], replicated, may hold values from 0.1 to 1.9
- attend_offset: float32 [384], replicated, may hold values from -3 to 3
- query_key_proj: bfloat16 [384, 1152], replicated, may hold values from -0.3125 to 0.3125
- heads_output_proj: bfloat16 [384, 384], replicated, may hold values from -3.5 to 3.5
- heads_output_bias: float32 [384], replicated, may hold values from -3 to 3
- feedforward_scale: float32 [384], replicated, may hold values from 0.1 to 1.9
- feedforward_offset: float32 [384], replicated, may hold values from -3 to 3
- feedforward_enlarge: bfloat16 [384, 1536], replicated, may hold values from -0.3125 to 0.3125
- feedforward_enlarge_bias: float32 [1536], replicated, may hold values from -3 to 3
- feedforward_contract: bfloat16 [1536, 384], replicated, may hold values from -0.15625 to 0.15625
- contract_bias: float32 [384], replicated, may hold values from -3 to 3
Outputs:
- section_ends: bfloat16 [2, 4, 16, 256, 384], P('section', None, 'dp')
- root_means: float32 [2, 4, 16], P('section', None, 'dp')
- expander_grad: float32 [384, 1536], replicated
- upshift_grad: float32 [1536], replicated
- depthwise_grad: float32 [9, 1536], replicated
- depthshift_grad: float32 [1536], replicated
- projector_grad: float32 [1536, 384], replicated
- postgain_grad: float32 [384], replicated
- postshift_grad: float32 [384], replicated
- pregain_grad: float32 [384], replicated
- preshift_grad: float32 [384], replicated
- attention_grad: float32 [384, 1152], replicated
- mixing_grad: float32 [384, 384], replicated
- mixshift_grad: float32 [384], replicated
- midgain_grad: float32 [384], replicated
- midshift_grad: float32 [384], replicated
- widener_grad: float32 [384, 1536], replicated
- wideshift_grad: float32 [1536], replicated
- narrower_grad: float32 [1536, 384], replicated
- narrowshift_grad: float32 [384], replicated
The draws below stay inside these ranges and needn't reach their ends.
Inputs may be any that keep to these rules, and one draw needn't show every extreme that they name: Image (m, i) occupies the slots of the first picture_tile_extents[m, i, 0] rows and first picture_tile_extents[m, i, 1] columns of its 16 x 16 grid.
All inputs are finite; a program needn't handle non-finite values.
Results may differ from the reference program's by a relative error of at most 0.015.
Values may be sent and summed in bfloat16 or wider, within the bound.
No kernel may reach another device: no remote copies, remote signals or barrier semaphores. Data moves between devices by JAX's collectives and lax.ppermute only.
A program may use at most 256 MiB of HBM per device.

```python
import math
import jax
import jax.numpy as jnp
from jax import lax

EMBED_DIMENSION = 384
FF = 1536
HEADS = 6
HEAD = 64
SIDE = 16
SLOT = 256
MICRO = 4
IMAGES = 16


def plant(values, rng, least, high):
    longest = values.shape.index(max(values.shape))
    spots = []
    for shift in (0, 1):
        where = [jax.random.randint(jax.random.fold_in(rng, axis), (), 0, length) for axis, length in enumerate(values.shape)]
        where[longest] = (where[longest] + shift) % values.shape[longest]
        spots.append(tuple(where))
    return values.at[spots[0]].set(least).at[spots[1]].set(high)


def level_of(stream_key, extent, shards, low, largest):
    def one(position, parts):
        steps = jax.random.uniform(jax.random.fold_in(jax.random.fold_in(stream_key, 6), position), (parts,), jnp.float32, low / len(shards), largest / len(shards))
        return jnp.repeat(jnp.exp(steps), extent[position] // parts).reshape((-1,) + (1,) * (len(extent) - position - 1))

    gain = one(*shards[0])
    for cut in shards[1:]:
        gain = gain * one(*cut)
    return gain


def gaussian(key, dims, spread, bound, shards=(), kind=jnp.bfloat16):
    loudness = level_of(key, dims, shards, -0.22, 0.18) if shards else 1.0
    values = jax.random.normal(key, dims, jnp.float32) * spread * loudness
    return jnp.minimum(jnp.maximum(values, -bound), bound).astype(kind)


def setup_inputs(seed: int = 0) -> dict:
    streams_of = jax.random.split(jax.random.key(seed), 22)
    entering_tokens = gaussian(streams_of[0], (MICRO, IMAGES, SLOT, EMBED_DIMENSION), 1.0, 6.0, ((1, 16),))
    output_sensitivity = gaussian(streams_of[1], (MICRO, IMAGES, SLOT, EMBED_DIMENSION), 1.0, 6.0, ((1, 16),))
    picture_tile_extents = plant(jax.random.randint(streams_of[2], (MICRO, IMAGES, 2), SIDE // 2, SIDE + 1), jax.random.fold_in(streams_of[2], 1), SIDE // 2, SIDE).astype(jnp.int32)
    pointwise_enlarge = gaussian(streams_of[3], (EMBED_DIMENSION, FF), EMBED_DIMENSION ** -0.5, 0.3125)
    enlarge_bias = gaussian(streams_of[4], (FF,), 0.5, 3.0, (), jnp.float32)
    channelwise_kernel = gaussian(streams_of[5], (9, FF), 9 ** -0.5, 2.0, (), jnp.float32)
    channelwise_conv_bias = gaussian(streams_of[6], (FF,), 0.5, 3.0, (), jnp.float32)
    pointwise_contract = gaussian(streams_of[7], (FF, EMBED_DIMENSION), FF ** -0.5, 0.15625)
    convblock_scale = jnp.clip(1.0 + 0.18 * jax.random.normal(streams_of[8], (EMBED_DIMENSION,), jnp.float32), 0.1, 1.9)
    convblock_offset = gaussian(streams_of[9], (EMBED_DIMENSION,), 0.5, 3.0, (), jnp.float32)
    attend_scale = jnp.clip(1.0 + 0.18 * jax.random.normal(streams_of[10], (EMBED_DIMENSION,), jnp.float32), 0.1, 1.9)
    attend_offset = gaussian(streams_of[11], (EMBED_DIMENSION,), 0.5, 3.0, (), jnp.float32)
    query_key_proj = gaussian(streams_of[12], (EMBED_DIMENSION, 3 * EMBED_DIMENSION), EMBED_DIMENSION ** -0.5, 0.3125)
    heads_output_proj = gaussian(streams_of[13], (EMBED_DIMENSION, EMBED_DIMENSION), (max(EMBED_DIMENSION // 128, 2)) ** -0.5, 3.5)
    heads_output_bias = gaussian(streams_of[14], (EMBED_DIMENSION,), 0.5, 3.0, (), jnp.float32)
    feedforward_scale = jnp.clip(1.0 + 0.18 * jax.random.normal(streams_of[15], (EMBED_DIMENSION,), jnp.float32), 0.1, 1.9)
    feedforward_offset = gaussian(streams_of[16], (EMBED_DIMENSION,), 0.5, 3.0, (), jnp.float32)
    feedforward_enlarge = gaussian(streams_of[17], (EMBED_DIMENSION, FF), EMBED_DIMENSION ** -0.5, 0.3125)
    feedforward_enlarge_bias = gaussian(streams_of[18], (FF,), 0.5, 3.0, (), jnp.float32)
    feedforward_contract = gaussian(streams_of[19], (FF, EMBED_DIMENSION), FF ** -0.5, 0.15625)
    contract_bias = gaussian(streams_of[20], (EMBED_DIMENSION,), 0.5, 3.0, (), jnp.float32)
    return dict(entering_tokens=entering_tokens, output_sensitivity=output_sensitivity, picture_tile_extents=picture_tile_extents, pointwise_enlarge=pointwise_enlarge, enlarge_bias=enlarge_bias, channelwise_kernel=channelwise_kernel, channelwise_conv_bias=channelwise_conv_bias, pointwise_contract=pointwise_contract, convblock_scale=convblock_scale, convblock_offset=convblock_offset, attend_scale=attend_scale, attend_offset=attend_offset, query_key_proj=query_key_proj, heads_output_proj=heads_output_proj, heads_output_bias=heads_output_bias, feedforward_scale=feedforward_scale, feedforward_offset=feedforward_offset, feedforward_enlarge=feedforward_enlarge, feedforward_enlarge_bias=feedforward_enlarge_bias, feedforward_contract=feedforward_contract, contract_bias=contract_bias)


@jax.custom_vjp
def collapsed_quantity(v):
    return lax.optimization_barrier(v.astype(jnp.bfloat16)).astype(jnp.float32)

@jax.custom_vjp
def low_back(v):
    return v

def low_keep(v):
    return (collapsed_quantity(v), None)

def low_pass(kept, grad):
    return (grad,)

def back_keep(v):
    return (v, None)

def back_low(kept, grad):
    return (collapsed_quantity(grad),)
collapsed_quantity.defvjp(low_keep, low_pass)
low_back.defvjp(back_keep, back_low)
HIGHEST = lax.Precision.HIGHEST
EPSILON = 1e-05
BLOCKED = -1000000000.0

def matmul(left, right):
    return jnp.dot(left, right, precision=HIGHEST)

def both_ways(values):
    return low_back(collapsed_quantity(values))

def standardize_features(values, norm_gain, norm_shift):
    centered = values - lax.optimization_barrier(jnp.mean(values, axis=-1, keepdims=True))
    scaled = centered * lax.rsqrt(lax.optimization_barrier(jnp.mean(centered * centered, axis=-1, keepdims=True)) + EPSILON)
    return scaled * norm_gain + norm_shift

def grid_mask(picture_tile_extents):
    places = jnp.arange(SIDE, dtype=jnp.int32)
    inside = (places[None, :, None] < picture_tile_extents[:, 0, None, None]) & (places[None, None, :] < picture_tile_extents[:, 1, None, None])
    return inside.reshape(picture_tile_extents.shape[0], SIDE * SIDE).astype(jnp.float32)

def depth_conv(expanded, channelwise_kernel, channelwise_conv_bias):
    padded = jnp.pad(expanded, ((0, 0), (1, 1), (1, 1), (0, 0)))
    result = channelwise_conv_bias + jnp.zeros_like(expanded)
    for tap_index in range(9):
        row_off = tap_index // 3
        col_off = tap_index % 3
        result = result + padded[:, row_off:row_off + SIDE, col_off:col_off + SIDE, :] * channelwise_kernel[tap_index]
    return result

def mbconv_block(weights_one, entering_tokens, valid):
    pointwise_enlarge, enlarge_bias, channelwise_kernel, channelwise_conv_bias, pointwise_contract, convblock_scale, convblock_offset = weights_one
    images = entering_tokens.shape[0]
    unrolled_entries = entering_tokens.reshape(-1, EMBED_DIMENSION)
    expanded = low_back(matmul(unrolled_entries, pointwise_enlarge)) + enlarge_bias
    expanded = expanded.reshape(images, SIDE, SIDE, FF) * valid.reshape(images, SIDE, SIDE, 1)
    convolved = depth_conv(expanded, channelwise_kernel, channelwise_conv_bias)
    active = collapsed_quantity(jax.nn.silu(convolved).reshape(-1, FF))
    projected = low_back(matmul(active, pointwise_contract))
    return (unrolled_entries + standardize_features(projected, convblock_scale, convblock_offset)).reshape(images, SLOT, EMBED_DIMENSION)

def transformer_block(latter_coefficients, sent, valid):
    attend_scale, attend_offset, query_key_proj, heads_output_proj, heads_output_bias, feedforward_scale, feedforward_offset, feedforward_enlarge, feedforward_enlarge_bias, feedforward_contract, contract_bias = latter_coefficients
    images = sent.shape[0]
    unrolled_entries = sent.reshape(-1, EMBED_DIMENSION)
    standardized_entries = collapsed_quantity(standardize_features(unrolled_entries, attend_scale, attend_offset))
    mixed_all = matmul(standardized_entries, query_key_proj).reshape(images, SLOT, 3, HEADS, HEAD)
    queries = both_ways(mixed_all[:, :, 0])
    keys_all = both_ways(mixed_all[:, :, 1])
    values_all = both_ways(mixed_all[:, :, 2])
    raw_scores = jnp.einsum('nqhe,nkhe->nhqk', queries, keys_all, precision=HIGHEST) * (1.0 / math.sqrt(HEAD))
    scores = low_back(jnp.where(valid[:, None, None, :] > 0.5, raw_scores, BLOCKED))
    weights_soft = jax.nn.softmax(scores, axis=-1)
    context = both_ways(jnp.einsum('nhqk,nkhe->nqhe', collapsed_quantity(weights_soft), values_all, precision=HIGHEST)).reshape(-1, EMBED_DIMENSION)
    middle = unrolled_entries + low_back(matmul(context, heads_output_proj)) + heads_output_bias
    hidden = collapsed_quantity(standardize_features(middle, feedforward_scale, feedforward_offset))
    widened = low_back(matmul(hidden, feedforward_enlarge)) + feedforward_enlarge_bias
    activated = collapsed_quantity(jax.nn.gelu(widened, approximate=False))
    result = middle + low_back(matmul(activated, feedforward_contract)) + contract_bias
    return result.reshape(images, SLOT, EMBED_DIMENSION) * valid[:, :, None]

def both_blocks(weights_one, latter_coefficients, entering_tokens, valid):
    sent = both_ways(mbconv_block(weights_one, entering_tokens, valid))
    return transformer_block(latter_coefficients, sent, valid)

def root_mean(values, valid):
    squares = lax.optimization_barrier(jnp.sum(values * values * valid[:, :, None], axis=(1, 2)))
    return jnp.sqrt(squares / (lax.optimization_barrier(jnp.sum(valid, axis=1)) * EMBED_DIMENSION))

def reference(entering_tokens, output_sensitivity, picture_tile_extents, pointwise_enlarge, enlarge_bias, channelwise_kernel, channelwise_conv_bias, pointwise_contract, convblock_scale, convblock_offset, attend_scale, attend_offset, query_key_proj, heads_output_proj, heads_output_bias, feedforward_scale, feedforward_offset, feedforward_enlarge, feedforward_enlarge_bias, feedforward_contract, contract_bias):
    weights_one = tuple((coefficient_array.astype(jnp.float32) for coefficient_array in (pointwise_enlarge, enlarge_bias, channelwise_kernel, channelwise_conv_bias, pointwise_contract, convblock_scale, convblock_offset)))
    latter_coefficients = tuple((coefficient_array.astype(jnp.float32) for coefficient_array in (attend_scale, attend_offset, query_key_proj, heads_output_proj, heads_output_bias, feedforward_scale, feedforward_offset, feedforward_enlarge, feedforward_enlarge_bias, feedforward_contract, contract_bias)))
    group_size = math.gcd(MICRO * IMAGES, 16)
    blocks = MICRO * IMAGES // group_size
    stacked_in = entering_tokens.astype(jnp.float32).reshape(blocks, group_size, SLOT, EMBED_DIMENSION)
    stacked_cot = output_sensitivity.astype(jnp.float32).reshape(blocks, group_size, SLOT, EMBED_DIMENSION)
    stacked_sides = picture_tile_extents.reshape(blocks, group_size, 2)

    def visit_block(totals, block_item):
        block_in, block_cot, block_sides = block_item
        valid = grid_mask(block_sides)
        output, pullback = jax.vjp(lambda first_set, second_set, start_rows: both_blocks(first_set, second_set, start_rows, valid), weights_one, latter_coefficients, block_in)
        grad_first, grad_second, grad_input = pullback(block_cot)
        totals = jax.tree.map(lambda running, addend: running + addend, totals, grad_first + grad_second)
        return (totals, (grad_input.astype(jnp.bfloat16), output.astype(jnp.bfloat16), root_mean(grad_input, valid), root_mean(output, valid)))
    initial = tuple((jnp.zeros_like(coefficient_array) for coefficient_array in weights_one + latter_coefficients))
    totals, (grad_inputs, outputs, rms_in, rms_out) = lax.scan(visit_block, initial, (stacked_in, stacked_cot, stacked_sides))
    section_ends = jnp.stack([grad_inputs.reshape(MICRO, IMAGES, SLOT, EMBED_DIMENSION), outputs.reshape(MICRO, IMAGES, SLOT, EMBED_DIMENSION)])
    root_means = jnp.stack([rms_in.reshape(MICRO, IMAGES), rms_out.reshape(MICRO, IMAGES)])
    return (section_ends, root_means, totals[0], totals[1], totals[2], totals[3], totals[4], totals[5], totals[6], totals[7], totals[8], totals[9], totals[10], totals[11], totals[12], totals[13], totals[14], totals[15], totals[16], totals[17])
```

```python
import functools
import math

import jax
import jax.numpy as jnp
from jax import lax
from jax.experimental import pallas as pl
from jax.experimental.pallas import tpu as pltpu
from jax.sharding import PartitionSpec as P

HEADS = 6
SIDE = 16
SLOTS = SIDE * SIDE
EPSILON = 1e-05
BLOCKED = -1000000000.0
LANES = 128
BLOCK = 256
BF16 = jnp.bfloat16
F32 = jnp.float32


def dot_nn(left, right):
    return jnp.dot(left, right, preferred_element_type=F32)


def dot_nt(left, right):
    return lax.dot_general(left, right, (((1,), (1,)), ((), ())), preferred_element_type=F32)


def dot_tn(left, right):
    return lax.dot_general(left, right, (((0,), (0,)), ((), ())), preferred_element_type=F32)


def norm_parts(values):
    centered = values - jnp.mean(values, axis=-1, keepdims=True)
    inverse = lax.rsqrt(jnp.mean(centered * centered, axis=-1, keepdims=True) + EPSILON)
    return centered * inverse, inverse


def norm_reverse(upstream, scaled, inverse, gain):
    lifted = upstream * gain
    return inverse * (
        lifted
        - jnp.mean(lifted, axis=-1, keepdims=True)
        - scaled * jnp.mean(lifted * scaled, axis=-1, keepdims=True)
    )


def total_rows(values):
    return jnp.sum(values, axis=0, keepdims=True)


def valid_column(numbers, image):
    slot = lax.broadcasted_iota(jnp.int32, (SLOTS, 1), 0)
    inside = (slot // SIDE < numbers[1 + 2 * image]) & (slot % SIDE < numbers[2 + 2 * image])
    return inside.astype(F32)


def valid_rows(numbers, images):
    return jnp.concatenate([valid_column(numbers, image) for image in range(images)], axis=0)


def column_shifts(row, first_column, last_column):
    before = jnp.where(first_column, 0.0, pltpu.roll(row, 1, 0))
    after = jnp.where(last_column, 0.0, pltpu.roll(row, SIDE - 1, 0))
    return before, after


def conv_ahead_kernel(
    numbers, tokens, enlarge, enlarge_bias, taps, taps_bias, contract, gain, shift,
    sent, expanded, slope, active, projected, grid_cells,
):
    rows = sent.shape[0]
    images = rows // SLOTS
    width = sent.shape[1]
    channels = enlarge.shape[1]
    local_in = tokens[...].reshape(rows, width)
    valid = valid_rows(numbers, images)
    column = lax.broadcasted_iota(jnp.int32, (SIDE, BLOCK), 0)
    first_column, last_column = column == 0, column == SIDE - 1
    total = jnp.zeros((rows, width), F32)
    for start in range(0, channels, BLOCK):
        part = slice(start, start + BLOCK)
        cells = (dot_nn(local_in, enlarge[:, part]) + enlarge_bias[:, part]) * valid
        grid_cells[...] = cells
        expanded[:, part] = cells.astype(BF16)
        kernel = [taps[tap : tap + 1, part] for tap in range(9)]
        bias = taps_bias[:, part]
        for image in range(images):
            base = image * SLOTS
            above = here = None
            for line in range(SIDE + 1):
                if line < SIDE:
                    row = grid_cells[base + line * SIDE : base + (line + 1) * SIDE, :]
                    before, after = column_shifts(row, first_column, last_column)
                    sums = [
                        before * kernel[3 * a] + row * kernel[3 * a + 1] + after * kernel[3 * a + 2]
                        for a in range(3)
                    ]
                if line > 0:
                    convolved = above + sums[2] if line < SIDE else above
                    gate = jax.nn.sigmoid(convolved)
                    lit = convolved * gate
                    place = slice(base + (line - 1) * SIDE, base + line * SIDE)
                    active[place, part] = lit.astype(BF16)
                    slope[place, part] = (gate + lit * (1.0 - gate)).astype(BF16)
                if line < SIDE:
                    above = (here if line > 0 else bias) + sums[1]
                    here = bias + sums[0]
        total = total + dot_nn(active[:, part], contract[part, :])
    projected[...] = total
    scaled, _ = norm_parts(total)
    sent[...] = (local_in.astype(F32) + scaled * gain[...] + shift[...]).astype(BF16)


def head_lanes(width):
    return lax.broadcasted_iota(jnp.int32, (1, width), 1)


def attend_ahead_kernel(
    numbers, sent, gain, shift, mixing_in, mixing_out, mixing_bias,
    qkv, weights, context, middle,
):
    rows, width = sent.shape
    images = rows // SLOTS
    head = width // HEADS
    factor = 1.0 / math.sqrt(head)
    entering = sent[...].astype(F32)
    scaled, _ = norm_parts(entering)
    normed = (scaled * gain[...] + shift[...]).astype(BF16)
    for start in range(0, 3 * width, width):
        part = slice(start, start + width)
        qkv[:, part] = dot_nn(normed, mixing_in[:, part]).astype(BF16)
    pair = 2 * head
    lane = head_lanes(pair)
    for image in range(images):
        valid = valid_column(numbers, image) > 0.5
        place = slice(image * SLOTS, (image + 1) * SLOTS)
        for couple in range(HEADS // 2):
            at = couple * pair
            queries = qkv[place, at : at + pair]
            keys = qkv[place, width + at : width + at + pair]
            values = qkv[place, 2 * width + at : 2 * width + at + pair]
            gathered = []
            for side in range(2):
                own = (lane >= side * head) & (lane < (side + 1) * head)
                scores = dot_nt(jnp.where(own, keys, jnp.zeros_like(keys)), queries) * factor
                scores = jnp.where(valid, scores, BLOCKED)
                powers = jnp.exp(scores - jnp.max(scores, axis=0, keepdims=True))
                soft = powers * (1.0 / jnp.sum(powers, axis=0, keepdims=True))
                low = soft.astype(BF16)
                weights[image * HEADS + couple * 2 + side] = low
                gathered.append(dot_tn(low, values))
            context[place, at : at + pair] = jnp.where(lane < head, *gathered).astype(BF16)
    middle[...] = entering + dot_nn(context[...], mixing_out[...]) + mixing_bias[...]


def mlp_kernel(
    numbers, middle, sensitivity, gain, shift, enlarge, enlarge_bias, contract, contract_bias,
    output, grad_middle, narrower, widener, small, wide_small,
):
    rows, width = middle.shape
    images = rows // SLOTS
    hidden_width = enlarge.shape[1]
    valid = valid_rows(numbers, images)
    center = middle[...]
    scaled, inverse = norm_parts(center)
    hidden = (scaled * gain[...] + shift[...]).astype(BF16)
    grad_out = sensitivity[...].reshape(rows, width).astype(F32) * valid
    out_low = grad_out.astype(BF16)
    total = jnp.zeros((rows, width), F32)
    grad_hidden = jnp.zeros((rows, width), F32)
    for start in range(0, hidden_width, BLOCK):
        part = slice(start, start + BLOCK)
        widened = dot_nn(hidden, enlarge[:, part]) + enlarge_bias[:, part]
        normal_cdf = 0.5 * (1.0 + lax.erf(widened * (1.0 / math.sqrt(2.0))))
        normal_pdf = jnp.exp(-0.5 * widened * widened) * (1.0 / math.sqrt(2.0 * math.pi))
        activated = (widened * normal_cdf).astype(BF16)
        total = total + dot_nn(activated, contract[part, :])
        grad_wide = dot_nt(out_low, contract[part, :]) * (normal_cdf + widened * normal_pdf)
        wide_small[:, part] = total_rows(grad_wide)
        wide_low = grad_wide.astype(BF16)
        grad = dot_tn(activated, out_low).astype(BF16)
        for lanes in range(width // LANES):
            narrower[lanes, part, :] = grad[:, lanes * LANES : (lanes + 1) * LANES]
        grad = dot_tn(hidden, wide_low).astype(BF16)
        for lanes in range(BLOCK // LANES):
            widener[start // LANES + lanes] = grad[:, lanes * LANES : (lanes + 1) * LANES]
        grad_hidden = grad_hidden + dot_nt(wide_low, enlarge[:, part])
    output[...] = ((center + total + contract_bias[...]) * valid).astype(BF16)
    gradient = grad_out + norm_reverse(grad_hidden, scaled, inverse, gain[...])
    grad_middle[...] = gradient
    small[0:1, :] = total_rows(grad_out)
    small[1:2, :] = total_rows(grad_hidden * scaled)
    small[2:3, :] = total_rows(grad_hidden)
    small[3:4, :] = total_rows(gradient)


def attend_back_kernel(
    sent, grad_middle, qkv, weights, context, gain, shift, mixing_in, mixing_out,
    grad_sent, mixed, small, grad_qkv,
):
    rows, width = sent.shape
    images = rows // SLOTS
    head = width // HEADS
    factor = 1.0 / math.sqrt(head)
    gradient = grad_middle[...]
    middle_low = gradient.astype(BF16)
    blocks = width // LANES
    grad = dot_tn(context[...], middle_low).astype(BF16)
    for lanes in range(blocks):
        mixed[3 * blocks + lanes] = grad[:, lanes * LANES : (lanes + 1) * LANES]
    grad_context = dot_nt(middle_low, mixing_out[...]).astype(BF16)
    pair = 2 * head
    lane = head_lanes(pair)
    for image in range(images):
        place = slice(image * SLOTS, (image + 1) * SLOTS)
        for couple in range(HEADS // 2):
            at = couple * pair
            queries = qkv[place, at : at + pair]
            keys = qkv[place, width + at : width + at + pair]
            values = qkv[place, 2 * width + at : 2 * width + at + pair]
            upstream = grad_context[place, at : at + pair]
            parts = []
            for side in range(2):
                own = (lane >= side * head) & (lane < (side + 1) * head)
                low = weights[image * HEADS + couple * 2 + side]
                soft = low.astype(F32)
                grad_values = dot_nn(low, upstream)
                lifted = soft * dot_nt(jnp.where(own, values, jnp.zeros_like(values)), upstream)
                scores_low = (lifted - soft * jnp.sum(lifted, axis=0, keepdims=True)).astype(BF16)
                parts.append(
                    (
                        dot_tn(scores_low, keys) * factor,
                        dot_nn(scores_low, queries) * factor,
                        grad_values,
                    )
                )
            for which in range(3):
                merged = jnp.where(lane < head, parts[0][which], parts[1][which])
                grad_qkv[place, which * width + at : which * width + at + pair] = merged.astype(
                    BF16
                )
    entering = sent[...].astype(F32)
    scaled, inverse = norm_parts(entering)
    normed = (scaled * gain[...] + shift[...]).astype(BF16)
    lifted = jnp.zeros((rows, width), F32)
    for which in range(3):
        part = slice(which * width, (which + 1) * width)
        piece = grad_qkv[:, part]
        grad = dot_tn(normed, piece).astype(BF16)
        for lanes in range(blocks):
            mixed[which * blocks + lanes] = grad[:, lanes * LANES : (lanes + 1) * LANES]
        lifted = lifted + dot_nt(piece, mixing_in[:, part])
    grad_sent[...] = (gradient + norm_reverse(lifted, scaled, inverse, gain[...])).astype(BF16)
    small[0:1, :] = total_rows(lifted * scaled)
    small[1:2, :] = total_rows(lifted)


def conv_back_kernel(
    numbers, tokens, grad_sent, projected, expanded, slope, active, gain, enlarge, taps, contract,
    grad_in, projector, expander, small, wide_small, grad_cells,
):
    rows, width = projected.shape
    images = rows // SLOTS
    channels = enlarge.shape[1]
    incoming = grad_sent[...].astype(F32)
    scaled, inverse = norm_parts(projected[...])
    proj_low = norm_reverse(incoming, scaled, inverse, gain[...]).astype(BF16)
    small[0:1, :] = total_rows(incoming * scaled)
    small[1:2, :] = total_rows(incoming)
    for start in range(0, channels, BLOCK):
        part = slice(start, start + BLOCK)
        grad = dot_tn(active[:, part], proj_low).astype(BF16)
        for lanes in range(width // LANES):
            projector[lanes, part, :] = grad[:, lanes * LANES : (lanes + 1) * LANES]
    local_in = tokens[...].reshape(rows, width)
    valid = valid_rows(numbers, images)
    column = lax.broadcasted_iota(jnp.int32, (SIDE, LANES), 0)
    first_column, last_column = column == 0, column == SIDE - 1
    total = incoming
    for start in range(0, channels, BLOCK):
        part = slice(start, start + BLOCK)
        grad_conv = dot_nt(proj_low, contract[part, :]) * slope[:, part].astype(F32)
        wide_small[9:10, part] = total_rows(grad_conv)
        grad_cells[...] = grad_conv
        pieces = []
        for lanes in range(0, BLOCK, LANES):
            chans = slice(start + lanes, start + lanes + LANES)
            kernel = [taps[tap : tap + 1, chans] for tap in range(9)]
            sums = [jnp.zeros((SIDE, LANES), F32) for _ in range(9)]
            outcome = []
            for image in range(images):
                base = image * SLOTS
                shifted = {}
                for line in range(SIDE):
                    for ahead in (line, line + 1):
                        if ahead < SIDE and ahead not in shifted:
                            row = grad_cells[
                                base + ahead * SIDE : base + (ahead + 1) * SIDE,
                                lanes : lanes + LANES,
                            ]
                            before, after = column_shifts(row, first_column, last_column)
                            shifted[ahead] = (after, row, before)
                    place = slice(base + line * SIDE, base + (line + 1) * SIDE)
                    cells = expanded[place, chans].astype(F32)
                    grid = jnp.zeros((SIDE, LANES), F32)
                    for a in range(3):
                        if 0 <= line + 1 - a < SIDE:
                            for b in range(3):
                                moved = shifted[line + 1 - a][b]
                                sums[3 * a + b] = sums[3 * a + b] + cells * moved
                                grid = grid + moved * kernel[3 * a + b]
                    outcome.append(grid)
            for tap in range(9):
                wide_small[tap : tap + 1, chans] = total_rows(sums[tap])
            pieces.append(jnp.concatenate(outcome, axis=0) * valid)
        grad_expanded = jnp.concatenate(pieces, axis=1)
        wide_small[10:11, part] = total_rows(grad_expanded)
        expanded_low = grad_expanded.astype(BF16)
        grad = dot_tn(local_in, expanded_low).astype(BF16)
        for lanes in range(BLOCK // LANES):
            expander[start // LANES + lanes] = grad[:, lanes * LANES : (lanes + 1) * LANES]
        total = total + dot_nt(expanded_low, enlarge[:, part])
    grad_in[...] = total.astype(BF16)


WHOLE = pl.BlockSpec(memory_space=pltpu.VMEM)


def call(kernel, name, numbers, ins, outs, scratch=(), tokens=()):
    specs = []
    for place, value in enumerate(ins):
        if place in tokens:
            share = value.shape[0] // 2
            specs.append(
                pl.BlockSpec(
                    (share,) + value.shape[1:], lambda step, numbers: (numbers[0], 0, 0, 0)
                )
            )
        else:
            specs.append(WHOLE)
    return pl.pallas_call(
        kernel if numbers is not None else kernel,
        out_shape=outs,
        grid_spec=pltpu.PrefetchScalarGridSpec(
            num_scalar_prefetch=1,
            grid=(1,),
            in_specs=specs,
            out_specs=[WHOLE] * len(outs),
            scratch_shapes=list(scratch),
        ),
        compiler_params=pltpu.CompilerParams(vmem_limit_bytes=56 * 1024 * 1024),
        name=name,
    )(numbers, *ins)


def shape(dims, kind):
    return jax.ShapeDtypeStruct(dims, kind)


def unpacked(blocks, axis_blocks):
    return jnp.concatenate([blocks[i] for i in range(axis_blocks)], axis=1)


def shards(
    entering_tokens,
    output_sensitivity,
    picture_tile_extents,
    pointwise_enlarge,
    enlarge_bias,
    channelwise_kernel,
    channelwise_conv_bias,
    pointwise_contract,
    convblock_scale,
    convblock_offset,
    attend_scale,
    attend_offset,
    query_key_proj,
    heads_output_proj,
    heads_output_bias,
    feedforward_scale,
    feedforward_offset,
    feedforward_enlarge,
    feedforward_enlarge_bias,
    feedforward_contract,
    contract_bias,
):
    micro_count, local_images, slots, width = entering_tokens.shape
    channels = pointwise_enlarge.shape[1]
    section = lax.axis_index("section")
    share = micro_count // 2
    images = share * local_images
    rows = images * slots
    mine = lax.dynamic_slice_in_dim(picture_tile_extents, section * share, share, 0)
    numbers = jnp.concatenate([section[None].astype(jnp.int32), mine.reshape(-1)])
    line = lambda vector: vector.reshape(1, -1)
    blocks = width // LANES
    wide_blocks = channels // LANES

    sent, expanded, slope, active, projected = call(
        conv_ahead_kernel, "conv_ahead", numbers,
        (entering_tokens, pointwise_enlarge, line(enlarge_bias), channelwise_kernel,
         line(channelwise_conv_bias), pointwise_contract, line(convblock_scale),
         line(convblock_offset)),
        (shape((rows, width), BF16), shape((rows, channels), BF16), shape((rows, channels), BF16),
         shape((rows, channels), BF16), shape((rows, width), F32)),
        [pltpu.VMEM((rows, BLOCK), F32)], (0,),
    )
    qkv, weights, context, middle = call(
        attend_ahead_kernel, "attend_ahead", numbers,
        (sent, line(attend_scale), line(attend_offset), query_key_proj, heads_output_proj,
         line(heads_output_bias)),
        (shape((rows, 3 * width), BF16), shape((images * HEADS, slots, slots), BF16),
         shape((rows, width), BF16), shape((rows, width), F32)),
    )
    output, grad_middle, narrower, widener, mlp_small, mlp_wide = call(
        mlp_kernel, "mlp", numbers,
        (middle, output_sensitivity, line(feedforward_scale), line(feedforward_offset),
         feedforward_enlarge, line(feedforward_enlarge_bias), feedforward_contract,
         line(contract_bias)),
        (shape((rows, width), BF16), shape((rows, width), F32),
         shape((blocks, channels, LANES), BF16), shape((wide_blocks, width, LANES), BF16),
         shape((8, width), F32), shape((1, channels), F32)),
        (), (1,),
    )
    grad_sent, mixed, attend_small = call(
        lambda numbers, *refs: attend_back_kernel(*refs), "attend_back", numbers,
        (sent, grad_middle, qkv, weights, context, line(attend_scale), line(attend_offset),
         query_key_proj, heads_output_proj),
        (shape((rows, width), BF16), shape((4 * blocks, width, LANES), BF16),
         shape((8, width), F32)),
        [pltpu.VMEM((rows, 3 * width), BF16)],
    )
    grad_in, projector, expander, conv_small, conv_wide = call(
        conv_back_kernel, "conv_back", numbers,
        (entering_tokens, grad_sent, projected, expanded, slope, active, line(convblock_scale),
         pointwise_enlarge, channelwise_kernel, pointwise_contract),
        (shape((rows, width), BF16), shape((blocks, channels, LANES), BF16),
         shape((wide_blocks, width, LANES), BF16), shape((8, width), F32),
         shape((16, channels), F32)),
        [pltpu.VMEM((rows, BLOCK), F32)], (0,),
    )

    grads = lax.psum(
        (narrower, widener, mixed, projector, expander, mlp_small, mlp_wide, attend_small,
         conv_small, conv_wide), ("section", "dp")
    )
    narrower, widener, mixed, projector, expander = [g.astype(F32) for g in grads[:5]]
    mlp_small, mlp_wide, attend_small, conv_small, conv_wide = grads[5:]

    own = jnp.stack([grad_in, output]).reshape(2, share, local_images, slots, width)
    first = section == 0
    other = lax.ppermute(jnp.where(first, own[1], own[0]), "section", [(0, 1), (1, 0)])
    ends = jnp.where(
        first,
        jnp.concatenate([own[0], other], axis=0),
        jnp.concatenate([other, own[1]], axis=0),
    )
    squares = jnp.sum(jnp.square(ends.astype(F32)), axis=(2, 3))
    filled = (picture_tile_extents[..., 0] * picture_tile_extents[..., 1]).astype(F32)
    means = jnp.sqrt(squares / (filled * width))
    return (
        ends[None],
        means[None],
        unpacked(expander, wide_blocks),
        conv_wide[10],
        conv_wide[:9],
        conv_wide[9],
        unpacked(projector, blocks),
        conv_small[0],
        conv_small[1],
        attend_small[0],
        attend_small[1],
        unpacked(mixed[: 3 * blocks], 3 * blocks),
        unpacked(mixed[3 * blocks :], blocks),
        mlp_small[3],
        mlp_small[1],
        mlp_small[2],
        unpacked(widener, wide_blocks),
        mlp_wide[0],
        unpacked(narrower, blocks),
        mlp_small[0],
    )


def solution(mesh):
    tokens = P(None, "dp", None, None)
    placed = (tokens, tokens, P(None, "dp", None)) + (P(),) * 18
    return jax.shard_map(
        shards,
        mesh=mesh,
        in_specs=placed,
        out_specs=(P("section", None, "dp", None, None), P("section", None, "dp")) + (P(),) * 18,
        check_vma=False,
    )
```

```python
import functools
import math

import jax
import jax.numpy as jnp
from jax import lax
from jax.experimental import pallas as pl
from jax.experimental.pallas import tpu as pltpu
from jax.sharding import PartitionSpec as P

HEADS = 6
SIDE = 16
SLOTS = SIDE * SIDE
EPSILON = 1e-05
BLOCKED = -1000000000.0
LANES = 128
BLOCK = 256
FIXED = 4
SQUARE = 4
TALL = 576
ROW = 4
BF16 = jnp.bfloat16
F32 = jnp.float32


def dot_nn(left, right):
    return jnp.dot(left, right, preferred_element_type=F32)


def dot_nt(left, right):
    return lax.dot_general(left, right, (((1,), (1,)), ((), ())), preferred_element_type=F32)


def dot_tn(left, right):
    return lax.dot_general(left, right, (((0,), (0,)), ((), ())), preferred_element_type=F32)


def norm_parts(values):
    centered = values - jnp.mean(values, axis=-1, keepdims=True)
    inverse = lax.rsqrt(jnp.mean(centered * centered, axis=-1, keepdims=True) + EPSILON)
    return centered * inverse, inverse


def norm_reverse(upstream, scaled, inverse, gain):
    lifted = upstream * gain
    return inverse * (
        lifted
        - jnp.mean(lifted, axis=-1, keepdims=True)
        - scaled * jnp.mean(lifted * scaled, axis=-1, keepdims=True)
    )


def across(vector):
    return vector[...].reshape(1, -1)


def total_rows(values):
    return jnp.sum(values, axis=0, keepdims=True)


def valid_column(numbers, image):
    slot = lax.broadcasted_iota(jnp.int32, (SLOTS, 1), 0)
    inside = (slot // SIDE < numbers[FIXED + 2 * image]) & (slot % SIDE < numbers[FIXED + 1 + 2 * image])
    return inside.astype(F32)


def valid_rows(numbers, images):
    return jnp.concatenate([valid_column(numbers, image) for image in range(images)], axis=0)


def column_shifts(row, first_column, last_column):
    before = jnp.where(first_column, 0.0, pltpu.roll(row, 1, 0))
    after = jnp.where(last_column, 0.0, pltpu.roll(row, SIDE - 1, 0))
    return before, after


def conv_ahead_kernel(
    numbers, tokens, enlarge, enlarge_bias, taps, taps_bias, contract, gain, shift,
    sent, expanded, slope, active, projected, grid_cells,
):
    rows = sent.shape[0]
    images = rows // SLOTS
    width = sent.shape[1]
    channels = enlarge.shape[1]
    local_in = tokens[...].reshape(rows, width)
    valid = valid_rows(numbers, images)
    column = lax.broadcasted_iota(jnp.int32, (SIDE, BLOCK), 0)
    first_column, last_column = column == 0, column == SIDE - 1
    total = jnp.zeros((rows, width), F32)
    for start in range(0, channels, BLOCK):
        part = slice(start, start + BLOCK)
        cells = (dot_nn(local_in, enlarge[:, part]) + enlarge_bias[part].reshape(1, -1)) * valid
        grid_cells[...] = cells
        expanded[:, part] = cells.astype(BF16)
        kernel = [taps[tap : tap + 1, part] for tap in range(9)]
        bias = taps_bias[part].reshape(1, -1)
        for image in range(images):
            base = image * SLOTS
            above = here = None
            for line in range(SIDE + 1):
                if line < SIDE:
                    row = grid_cells[base + line * SIDE : base + (line + 1) * SIDE, :]
                    before, after = column_shifts(row, first_column, last_column)
                    sums = [
                        before * kernel[3 * a] + row * kernel[3 * a + 1] + after * kernel[3 * a + 2]
                        for a in range(3)
                    ]
                if line > 0:
                    convolved = above + sums[2] if line < SIDE else above
                    gate = jax.nn.sigmoid(convolved)
                    lit = convolved * gate
                    place = slice(base + (line - 1) * SIDE, base + line * SIDE)
                    active[place, part] = lit.astype(BF16)
                    slope[place, part] = (gate + lit * (1.0 - gate)).astype(BF16)
                if line < SIDE:
                    above = (here if line > 0 else bias) + sums[1]
                    here = bias + sums[0]
        total = total + dot_nn(active[:, part], contract[part, :])
    projected[...] = total
    scaled, _ = norm_parts(total)
    sent[...] = (local_in.astype(F32) + scaled * across(gain) + across(shift)).astype(BF16)


def head_lanes(width):
    return lax.broadcasted_iota(jnp.int32, (1, width), 1)


def attend_ahead_kernel(
    numbers, sent, gain, shift, mixing_in, mixing_out, mixing_bias,
    qkv, weights, context, middle,
):
    rows, width = sent.shape
    images = rows // SLOTS
    head = width // HEADS
    factor = 1.0 / math.sqrt(head)
    entering = sent[...].astype(F32)
    scaled, _ = norm_parts(entering)
    normed = (scaled * across(gain) + across(shift)).astype(BF16)
    for start in range(0, 3 * width, width):
        part = slice(start, start + width)
        qkv[:, part] = dot_nn(normed, mixing_in[:, part]).astype(BF16)
    pair = 2 * head
    lane = head_lanes(pair)
    for image in range(images):
        valid = valid_column(numbers, image) > 0.5
        place = slice(image * SLOTS, (image + 1) * SLOTS)
        for couple in range(HEADS // 2):
            at = couple * pair
            queries = qkv[place, at : at + pair]
            keys = qkv[place, width + at : width + at + pair]
            values = qkv[place, 2 * width + at : 2 * width + at + pair]
            gathered = []
            for side in range(2):
                own = (lane >= side * head) & (lane < (side + 1) * head)
                scores = dot_nt(jnp.where(own, keys, jnp.zeros_like(keys)), queries) * factor
                scores = jnp.where(valid, scores, BLOCKED)
                powers = jnp.exp(scores - jnp.max(scores, axis=0, keepdims=True))
                soft = powers * (1.0 / jnp.sum(powers, axis=0, keepdims=True))
                low = soft.astype(BF16)
                weights[image * HEADS + couple * 2 + side] = low
                gathered.append(dot_tn(low, values))
            context[place, at : at + pair] = jnp.where(lane < head, *gathered).astype(BF16)
    middle[...] = entering + dot_nn(context[...], mixing_out[...]) + across(mixing_bias)


def place_tall(blocks, grad, first_row, offset):
    count = blocks.shape[0] * blocks.shape[1]
    lanes = grad.shape[1] // LANES
    for block in range(count):
        height = TALL // lanes
        low = max(first_row, block * height)
        high = min(first_row + grad.shape[0], (block + 1) * height)
        if low < high:
            for lane in range(lanes):
                at = offset + lane * height + low - block * height
                blocks[block // SQUARE, block % SQUARE, at : at + high - low, :] = grad[
                    low - first_row : high - first_row, lane * LANES : (lane + 1) * LANES
                ]


def place_wide(blocks, grad, first_lane, offset):
    count = blocks.shape[0] * blocks.shape[1]
    height = grad.shape[0] // count
    for block in range(count):
        for lane in range(grad.shape[1] // LANES):
            at = offset + (first_lane + lane) * height
            blocks[block // SQUARE, block % SQUARE, at : at + height, :] = grad[
                block * height : (block + 1) * height, lane * LANES : (lane + 1) * LANES
            ]


def mlp_kernel(
    numbers, middle, sensitivity, gain, shift, enlarge, enlarge_bias, contract, contract_bias,
    output, grad_middle, keep, send, small, wide_small, blocks,
):
    rows, width = middle.shape
    images = rows // SLOTS
    hidden_width = enlarge.shape[1]
    valid = valid_rows(numbers, images)
    center = middle[...]
    scaled, inverse = norm_parts(center)
    hidden = (scaled * across(gain) + across(shift)).astype(BF16)
    grad_out = sensitivity[...].reshape(rows, width).astype(F32) * valid
    out_low = grad_out.astype(BF16)
    total = jnp.zeros((rows, width), F32)
    grad_hidden = jnp.zeros((rows, width), F32)
    for start in range(0, hidden_width, BLOCK):
        part = slice(start, start + BLOCK)
        widened = dot_nn(hidden, enlarge[:, part]) + enlarge_bias[part].reshape(1, -1)
        normal_cdf = 0.5 * (1.0 + lax.erf(widened * (1.0 / math.sqrt(2.0))))
        normal_pdf = jnp.exp(-0.5 * widened * widened) * (1.0 / math.sqrt(2.0 * math.pi))
        activated = (widened * normal_cdf).astype(BF16)
        total = total + dot_nn(activated, contract[part, :])
        grad_wide = dot_nt(out_low, contract[part, :]) * (normal_cdf + widened * normal_pdf)
        wide_small[:, part] = total_rows(grad_wide)
        wide_low = grad_wide.astype(BF16)
        place_tall(blocks, dot_tn(activated, out_low).astype(BF16), start, 0)
        place_wide(blocks, dot_tn(hidden, wide_low).astype(BF16), start // LANES, TALL)
        grad_hidden = grad_hidden + dot_nt(wide_low, enlarge[:, part])
    output[...] = ((center + total + across(contract_bias)) * valid).astype(BF16)
    gradient = grad_out + norm_reverse(grad_hidden, scaled, inverse, across(gain))
    grad_middle[...] = gradient
    small[0:1, :] = total_rows(grad_out)
    small[1:2, :] = total_rows(grad_hidden * scaled)
    small[2:3, :] = total_rows(grad_hidden)
    small[3:4, :] = total_rows(gradient)
    core = numbers[1]
    keep[...] = blocks[core]
    send[...] = blocks[1 - core]


def heads_back_kernel(
    grad_middle, qkv, weights, mixing_out, grad_qkv,
):
    rows, width = grad_middle.shape
    images = rows // SLOTS
    head = width // HEADS
    factor = 1.0 / math.sqrt(head)
    grad_context = dot_nt(grad_middle[...].astype(BF16), mixing_out[...]).astype(BF16)
    pair = 2 * head
    lane = head_lanes(pair)
    for image in range(images):
        place = slice(image * SLOTS, (image + 1) * SLOTS)
        for couple in range(HEADS // 2):
            at = couple * pair
            queries = qkv[place, at : at + pair]
            keys = qkv[place, width + at : width + at + pair]
            values = qkv[place, 2 * width + at : 2 * width + at + pair]
            upstream = grad_context[place, at : at + pair]
            parts = []
            for side in range(2):
                own = (lane >= side * head) & (lane < (side + 1) * head)
                low = weights[image * HEADS + couple * 2 + side]
                soft = low.astype(F32)
                grad_values = dot_nn(low, upstream)
                lifted = soft * dot_nt(jnp.where(own, values, jnp.zeros_like(values)), upstream)
                scores_low = (lifted - soft * jnp.sum(lifted, axis=0, keepdims=True)).astype(BF16)
                parts.append(
                    (
                        dot_tn(scores_low, keys) * factor,
                        dot_nn(scores_low, queries) * factor,
                        grad_values,
                    )
                )
            for which in range(3):
                merged = jnp.where(lane < head, parts[0][which], parts[1][which])
                grad_qkv[place, which * width + at : which * width + at + pair] = merged.astype(
                    BF16
                )


def sent_back_kernel(
    numbers, sent, grad_middle, grad_qkv, context, projected, active, gain, shift, mixing_in,
    conv_gain, grad_sent, proj_low, keep, send, small, blocks,
):
    rows, width = sent.shape
    gradient = grad_middle[...]
    entering = sent[...].astype(F32)
    scaled, inverse = norm_parts(entering)
    normed = (scaled * across(gain) + across(shift)).astype(BF16)
    lifted = jnp.zeros((rows, width), F32)
    for which in range(3):
        part = slice(which * width, (which + 1) * width)
        piece = grad_qkv[:, part]
        place_wide(blocks, dot_tn(normed, piece).astype(BF16), which * width // LANES, 0)
        lifted = lifted + dot_nt(piece, mixing_in[:, part])
    mixing = dot_tn(context[...], gradient.astype(BF16)).astype(BF16)
    place_wide(blocks, mixing, 3 * width // LANES, 0)
    grad_low = (gradient + norm_reverse(lifted, scaled, inverse, across(gain))).astype(BF16)
    grad_sent[...] = grad_low
    small[0:1, :] = total_rows(lifted * scaled)
    small[1:2, :] = total_rows(lifted)
    incoming = grad_low.astype(F32)
    scaled, inverse = norm_parts(projected[...])
    low = norm_reverse(incoming, scaled, inverse, across(conv_gain)).astype(BF16)
    proj_low[...] = low
    small[2:3, :] = total_rows(incoming * scaled)
    small[3:4, :] = total_rows(incoming)
    for start in range(0, active.shape[1], BLOCK):
        part = slice(start, start + BLOCK)
        place_tall(blocks, dot_tn(active[:, part], low).astype(BF16), start, TALL)
    core = numbers[1]
    keep[...] = blocks[core]
    send[...] = blocks[1 - core]


def conv_part(
    numbers, local_in, proj_low, expanded, slope, enlarge, taps, contract, wide_small, grad_cells,
    blocks, total, first, last,
):
    rows = local_in.shape[0]
    images = rows // SLOTS
    valid = valid_rows(numbers, images)
    column = lax.broadcasted_iota(jnp.int32, (SIDE, LANES), 0)
    first_column, last_column = column == 0, column == SIDE - 1
    for start in range(first, last, BLOCK):
        part = slice(start, start + BLOCK)
        grad_conv = dot_nt(proj_low, contract[part, :]) * slope[:, part].astype(F32)
        wide_small[9:10, part] = total_rows(grad_conv)
        grad_cells[...] = grad_conv
        pieces = []
        for lanes in range(0, BLOCK, LANES):
            chans = slice(start + lanes, start + lanes + LANES)
            kernel = [taps[tap : tap + 1, chans] for tap in range(9)]
            sums = [jnp.zeros((SIDE, LANES), F32) for _ in range(9)]
            outcome = []
            for image in range(images):
                base = image * SLOTS
                shifted = {}
                for line in range(SIDE):
                    for ahead in (line, line + 1):
                        if ahead < SIDE and ahead not in shifted:
                            row = grad_cells[
                                base + ahead * SIDE : base + (ahead + 1) * SIDE,
                                lanes : lanes + LANES,
                            ]
                            before, after = column_shifts(row, first_column, last_column)
                            shifted[ahead] = (after, row, before)
                    place = slice(base + line * SIDE, base + (line + 1) * SIDE)
                    cells = expanded[place, chans].astype(F32)
                    grid = jnp.zeros((SIDE, LANES), F32)
                    for a in range(3):
                        if 0 <= line + 1 - a < SIDE:
                            for b in range(3):
                                moved = shifted[line + 1 - a][b]
                                sums[3 * a + b] = sums[3 * a + b] + cells * moved
                                grid = grid + moved * kernel[3 * a + b]
                    outcome.append(grid)
            for tap in range(9):
                wide_small[tap : tap + 1, chans] = total_rows(sums[tap])
            pieces.append(jnp.concatenate(outcome, axis=0) * valid)
        grad_expanded = jnp.concatenate(pieces, axis=1)
        wide_small[10:11, part] = total_rows(grad_expanded)
        expanded_low = grad_expanded.astype(BF16)
        place_wide(
            blocks, dot_tn(local_in, expanded_low).astype(BF16), (start - first) // LANES, 0
        )
        total = total + dot_nt(expanded_low, enlarge[:, part])
    return total


def conv_back_kernel(
    numbers, tokens, grad_sent, proj_low, expanded, slope, enlarge, taps, contract,
    total, early, early_wide, grad_cells,
):
    rows, width = grad_sent.shape
    total[...] = conv_part(
        numbers, tokens[...].reshape(rows, width), proj_low[...], expanded, slope, enlarge, taps,
        contract, early_wide, grad_cells, early, grad_sent[...].astype(F32), 0,
        enlarge.shape[1] // 2,
    )


def small_rows(small, wide):
    mlp, sent = small
    mlp_wide, conv_wide = wide
    found = []
    for source, rows in ((mlp, 4), (sent, 4), (mlp_wide, 1), (conv_wide, 11)):
        for row in range(rows):
            for at in range(0, source.shape[1], LANES):
                found.append((source, row, at))
    return found


def conv_end_kernel(
    numbers, tokens, total, proj_low, expanded, slope, enlarge, taps, contract, early, early_wide,
    mlp_small, sent_small, mlp_wide, grad_in, keep, send, blocks, conv_wide, grad_cells, short,
):
    rows, width = total.shape
    channels = enlarge.shape[1]
    half = channels // 2
    conv_wide[:, 0:half] = early_wide[:, 0:half]
    gradient = conv_part(
        numbers, tokens[...].reshape(rows, width), proj_low[...], expanded, slope, enlarge, taps,
        contract, conv_wide, grad_cells, blocks, total[...], half, channels,
    )
    grad_in[...] = gradient.astype(BF16)
    short[...] = jnp.zeros_like(short)
    places = small_rows((mlp_small, sent_small), (mlp_wide, conv_wide))
    for number, (source, row, at) in enumerate(places):
        short[number : number + 1, :] = source[row : row + 1, at : at + LANES]
    core = numbers[1]
    for target, half_of in ((keep, core), (send, 1 - core)):
        target[:, 0 : TALL // 2, :] = early[half_of]
        target[:, TALL // 2 : TALL, :] = blocks[half_of]
        for block in range(SQUARE):
            for row in range(ROW):
                at = pl.multiple_of(((half_of * SQUARE + block) * ROW + row) * 8, 8)
                value = short[pl.ds(at, 8), :]
                high = value.astype(BF16).astype(F32)
                pair = jnp.concatenate([high, value - high], axis=0).astype(BF16)
                target[block, TALL + row * 16 : TALL + (row + 1) * 16, :] = pair


def summed(parts, short):
    total = parts[0].astype(F32)
    for part in parts[1:]:
        total = total + part.astype(F32)
    main = total[: total.shape[0] - short].astype(BF16)
    if not short:
        return main
    pieces = [main]
    for at in range(total.shape[0] - short, total.shape[0], 16):
        value = total[at : at + 8] + total[at + 8 : at + 16]
        high = value.astype(BF16).astype(F32)
        pieces.append(jnp.concatenate([high, value - high], axis=0).astype(BF16))
    return jnp.concatenate(pieces, axis=0)


def square_kernel(short, numbers, keep, arrived, *out):
    for step in range(SQUARE):
        block = numbers[2] ^ step
        out[step][...] = summed((keep[block], arrived[block]), short)


def row_kernel(short, numbers, *refs):
    parts, out, scratch = refs[:SQUARE], refs[SQUARE : SQUARE + ROW], refs[SQUARE + ROW]
    value = summed([part[...] for part in parts], short * ROW)
    main = TALL_OF(value.shape[0], short * ROW) // ROW
    for row in range(ROW):
        scratch[row, 0:main, :] = value[row * main : (row + 1) * main]
        if short:
            at = ROW * main + row * short
            scratch[row, main : main + short, :] = value[at : at + short]
    for step in range(ROW):
        out[step][...] = scratch[numbers[3] ^ step]


def TALL_OF(rows, short):
    return rows - short


def shard_kernel(short, numbers, *refs):
    refs[-1][...] = summed([part[...] for part in refs[:-1]], short)


def joined_kernel(short, numbers, *refs):
    parts, out, scratch = refs[:ROW], refs[ROW], refs[ROW + 1]
    for step in range(ROW):
        scratch[numbers[3] ^ step] = parts[step][...]
    main = parts[0].shape[0] - short
    for row in range(ROW):
        out[row * main : (row + 1) * main, :] = scratch[row, 0:main, :]
        if short:
            at = ROW * main + row * short
            out[at : at + short, :] = scratch[row, main : main + short, :]


def blocks_of(numbers, parts):
    for step in range(SQUARE):
        for side in range(2):
            core = numbers[1] if side == 0 else 1 - numbers[1]
            yield core * SQUARE + (numbers[2] ^ step), parts[side * SQUARE + step]


def write_tall(target, block, part, offset):
    lanes = target.shape[1] // LANES
    height = TALL // lanes
    at = pl.multiple_of(block * height, 16)
    for lane in range(lanes):
        target[pl.ds(at, height), lane * LANES : (lane + 1) * LANES] = part[
            offset + lane * height : offset + (lane + 1) * height, :
        ].astype(F32)


def write_wide(target, block, part, offset, first_lane=0):
    height = target.shape[0] // (2 * SQUARE)
    at = pl.multiple_of(block * height, 16)
    for lane in range(target.shape[1] // LANES):
        low = offset + (first_lane + lane) * height
        target[pl.ds(at, height), lane * LANES : (lane + 1) * LANES] = part[
            low : low + height, :
        ].astype(F32)


def mlp_end_kernel(numbers, *refs):
    narrower, widener = refs[2 * SQUARE :]
    for block, part in blocks_of(numbers, refs):
        write_tall(narrower, block, part, 0)
        write_wide(widener, block, part, TALL)


def sent_end_kernel(numbers, *refs):
    attention, mixing, projector = refs[2 * SQUARE :]
    for block, part in blocks_of(numbers, refs):
        write_wide(attention, block, part, 0)
        write_wide(mixing, block, part, 0, attention.shape[1] // LANES)
        write_tall(projector, block, part, TALL)


def conv_all_kernel(numbers, *refs):
    expander = refs[2 * SQUARE]
    shorts = refs[2 * SQUARE + 1 : -1]
    short = refs[-1]
    for block, part in blocks_of(numbers, refs):
        height = expander.shape[0] // (2 * SQUARE)
        at = pl.multiple_of(block * height, 16)
        for lane in range(expander.shape[1] // LANES):
            expander[pl.ds(at, height), lane * LANES : (lane + 1) * LANES] = part[
                lane * height : (lane + 1) * height, :
            ].astype(F32)
        for row in range(ROW):
            pair = part[TALL + row * 16 : TALL + (row + 1) * 16, :].astype(F32)
            at = pl.multiple_of((block * ROW + row) * 8, 8)
            short[pl.ds(at, 8), :] = pair[0:8] + pair[8:16]
    (upshift, depthwise, depthshift, postgain, postshift, pregain, preshift, mixshift, midgain,
     midshift, wideshift, narrowshift) = shorts
    lanes = narrowshift.shape[0] // LANES
    wide_lanes = upshift.shape[0] // LANES
    number = 0
    for target in (narrowshift, midgain, midshift, mixshift, pregain, preshift, postgain, postshift):
        for lane in range(lanes):
            target[lane * LANES : (lane + 1) * LANES] = short[number, :]
            number += 1
    for target in (wideshift,) + (depthwise,) * 9 + (depthshift, upshift):
        for lane in range(wide_lanes):
            value = short[number : number + 1, :]
            if target is depthwise:
                tap = number // wide_lanes - 3
                target[tap : tap + 1, lane * LANES : (lane + 1) * LANES] = value
            else:
                target[lane * LANES : (lane + 1) * LANES] = value.reshape(LANES)
            number += 1


WHOLE = pl.BlockSpec(memory_space=pltpu.VMEM)
ANYWHERE = pl.BlockSpec(memory_space=pl.ANY)
BOTH = ("section", "dp")


def shape(dims, kind):
    return jax.ShapeDtypeStruct(dims, kind)


def call(kernel, name, numbers, ins, outs, scratch=(), tokens=(), after=(), us=1, plain=False):
    specs = []
    for place, value in enumerate(ins):
        if place in tokens:
            block = (value.shape[0] // 2,) + value.shape[1:]
            specs.append(pl.BlockSpec(block, lambda step, numbers: (numbers[0], 0, 0, 0)))
        else:
            specs.append(WHOLE)
    count = len(ins)

    def body(numbers, *refs):
        refs = refs[:count] + refs[count + len(after) :]
        return kernel(*refs) if plain else kernel(numbers, *refs)

    result = pl.pallas_call(
        body,
        out_shape=outs,
        grid_spec=pltpu.PrefetchScalarGridSpec(
            num_scalar_prefetch=1,
            grid=(1,),
            in_specs=specs + [ANYWHERE] * len(after),
            out_specs=[WHOLE] * len(outs),
            scratch_shapes=list(scratch),
        ),
        cost_estimate=pl.CostEstimate(
            flops=int(us * 1e9), bytes_accessed=int(us * 3e6), transcendentals=0
        ),
        compiler_params=pltpu.CompilerParams(vmem_limit_bytes=56 * 1024 * 1024),
        name=name,
    )(numbers, *ins, *after)
    return result


def swapped(value, digit, step):
    sections, members = (lax.axis_size(axis) for axis in BOTH)
    pairs = []
    for section in range(sections):
        for member in range(members):
            if digit == "square":
                other = (section ^ (step >> 1)) * members + (member ^ ((step & 1) * 2))
            else:
                other = section * members + (member ^ (step * digit))
            pairs.append((section * members + member, other))
    return lax.ppermute(value, BOTH, pairs)


class Group:
    def __init__(self, name, numbers, keep, send, short=0):
        self.name, self.numbers, self.keep, self.short = name, numbers, keep, short
        self.rows = keep.shape[1]
        self.arrived = swapped(send, 1, 1)

    def call(self, kernel, what, ins, outs, scratch=(), after=()):
        return call(
            functools.partial(kernel, self.short), f"{self.name}_{what}", self.numbers, ins,
            [shape((rows, LANES), BF16) for rows in outs],
            [pltpu.VMEM(dims, BF16) for dims in scratch], after=after,
        )

    def square(self, after=()):
        short, self.short = self.short, self.short * ROW
        parts = self.call(square_kernel, "square", (self.keep, self.arrived), [self.rows] * SQUARE, (), after)
        self.short = short
        self.parts = [parts[0]] + [swapped(parts[step], "square", step) for step in range(1, SQUARE)]
        return parts[0]

    def row(self, after=()):
        rows = self.rows // ROW
        parts = self.call(row_kernel, "row", self.parts, [rows] * ROW, [(ROW, rows, LANES)], after)
        self.parts = [parts[0]] + [swapped(parts[step], 4, step) for step in range(1, ROW)]
        return parts[0]

    def shard(self, after=()):
        (self.own,) = self.call(shard_kernel, "shard", self.parts, [self.rows // ROW], (), after)
        rest, stride = lax.axis_size("dp") // (4 * ROW), 4 * ROW
        while rest > 1:
            radix = 4 if rest % 4 == 0 else 2
            parts = [self.own] + [swapped(self.own, stride, step) for step in range(1, radix)]
            (self.own,) = self.call(shard_kernel, "more", parts, [self.rows // ROW])
            rest, stride = rest // radix, stride * radix
        self.parts = [self.own] + [swapped(self.own, 4, step) for step in range(1, ROW)]
        return self.own

    def joined(self, after=()):
        (block,) = self.call(
            joined_kernel, "joined", self.parts, [self.rows], [(ROW, self.rows // ROW, LANES)], after
        )
        blocks = [block] + [swapped(block, "square", step) for step in range(1, SQUARE)]
        self.blocks = blocks + [swapped(part, 1, 1) for part in blocks]
        return block


def shards(
    entering_tokens,
    output_sensitivity,
    picture_tile_extents,
    pointwise_enlarge,
    enlarge_bias,
    channelwise_kernel,
    channelwise_conv_bias,
    pointwise_contract,
    convblock_scale,
    convblock_offset,
    attend_scale,
    attend_offset,
    query_key_proj,
    heads_output_proj,
    heads_output_bias,
    feedforward_scale,
    feedforward_offset,
    feedforward_enlarge,
    feedforward_enlarge_bias,
    feedforward_contract,
    contract_bias,
):
    micro_count, local_images, slots, width = entering_tokens.shape
    channels = pointwise_enlarge.shape[1]
    section, member = lax.axis_index("section"), lax.axis_index("dp")
    share = micro_count // 2
    images = share * local_images
    rows = images * slots
    mine = lax.dynamic_slice_in_dim(picture_tile_extents, section * share, share, 0)
    fixed = jnp.stack(
        [section, member % 2, section * 2 + member // 2 % 2, member // 4 % ROW]
    ).astype(jnp.int32)
    numbers = jnp.concatenate([fixed, mine.reshape(-1)])

    sent, expanded, slope, active, projected = call(
        conv_ahead_kernel, "conv_ahead", numbers,
        (entering_tokens, pointwise_enlarge, enlarge_bias, channelwise_kernel,
         channelwise_conv_bias, pointwise_contract, convblock_scale, convblock_offset),
        (shape((rows, width), BF16), shape((rows, channels), BF16), shape((rows, channels), BF16),
         shape((rows, channels), BF16), shape((rows, width), F32)),
        [pltpu.VMEM((rows, BLOCK), F32)], (0,), us=10,
    )
    qkv, weights, context, middle = call(
        attend_ahead_kernel, "attend_ahead", numbers,
        (sent, attend_scale, attend_offset, query_key_proj, heads_output_proj, heads_output_bias),
        (shape((rows, 3 * width), BF16), shape((images * HEADS, slots, slots), BF16),
         shape((rows, width), BF16), shape((rows, width), F32)), us=6,
    )
    halves = [shape((SQUARE, 2 * TALL, LANES), BF16)] * 2
    whole = [pltpu.VMEM((2, SQUARE, 2 * TALL, LANES), BF16)]
    output, grad_middle, keep, send, mlp_small, mlp_wide = call(
        mlp_kernel, "mlp", numbers,
        (middle, output_sensitivity, feedforward_scale, feedforward_offset, feedforward_enlarge,
         feedforward_enlarge_bias, feedforward_contract, contract_bias),
        [shape((rows, width), BF16), shape((rows, width), F32)] + halves
        + [shape((8, width), F32), shape((1, channels), F32)],
        whole, (1,), us=10,
    )
    mlp = Group("mlp", numbers, keep, send)
    (grad_qkv,) = call(
        heads_back_kernel, "heads_back", numbers, (grad_middle, qkv, weights, heads_output_proj),
        [shape((rows, 3 * width), BF16)], us=6, plain=True,
    )
    done = mlp.square(after=(grad_qkv,))
    grad_sent, proj_low, keep, send, sent_small = call(
        sent_back_kernel, "sent_back", numbers,
        (sent, grad_middle, grad_qkv, context, projected, active, attend_scale, attend_offset,
         query_key_proj, convblock_scale),
        [shape((rows, width), BF16), shape((rows, width), BF16)] + halves
        + [shape((8, width), F32)],
        whole, after=(done,), us=6,
    )
    sent_group = Group("sent", numbers, keep, send)
    done = mlp.row(after=(grad_sent,))
    quarter = shape((2, SQUARE, TALL // 2, LANES), BF16)
    total, early, early_wide = call(
        conv_back_kernel, "conv_back", numbers,
        (entering_tokens, grad_sent, proj_low, expanded, slope, pointwise_enlarge,
         channelwise_kernel, pointwise_contract),
        [shape((rows, width), F32), quarter, shape((16, channels), F32)],
        [pltpu.VMEM((rows, BLOCK), F32)], (0,), after=(done,), us=6,
    )
    done = mlp.shard(after=(total,))
    done = sent_group.square(after=(done,))
    halves = [shape((SQUARE, TALL + ROW * 16, LANES), BF16)] * 2
    grad_in, keep, send = call(
        conv_end_kernel, "conv_end", numbers,
        (entering_tokens, total, proj_low, expanded, slope, pointwise_enlarge, channelwise_kernel,
         pointwise_contract, early, early_wide, mlp_small, sent_small, mlp_wide),
        [shape((rows, width), BF16)] + halves,
        [pltpu.VMEM(quarter.shape, BF16), pltpu.VMEM((16, channels), F32),
         pltpu.VMEM((rows, BLOCK), F32), pltpu.VMEM((2 * SQUARE * ROW * 8, LANES), F32)],
        (0,), after=(done,), us=7,
    )
    conv = Group("conv", numbers, keep, send, 16)
    sent_group.row(after=(grad_in,))
    conv.square()
    mlp.joined()
    sent_group.shard()
    conv.row()
    sent_group.joined()
    conv.shard()
    conv.joined()

    line, wide_line = shape((width,), F32), shape((channels,), F32)
    tall, wide = shape((channels, width), F32), shape((width, channels), F32)
    narrower, widener = call(mlp_end_kernel, "mlp_end", numbers, mlp.blocks, [tall, wide])
    attention, mixing, projector = call(
        sent_end_kernel, "sent_end", numbers, sent_group.blocks,
        [shape((width, 3 * width), F32), shape((width, width), F32), tall],
    )
    (expander, upshift, depthwise, depthshift, postgain, postshift, pregain, preshift, mixshift,
     midgain, midshift, wideshift, narrowshift) = call(
        conv_all_kernel, "conv_all", numbers, conv.blocks,
        [wide, wide_line, shape((9, channels), F32), wide_line] + [line] * 7 + [wide_line, line],
        [pltpu.VMEM((2 * SQUARE * ROW * 8, LANES), F32)],
    )

    first = section == 0
    dims = (share, local_images, slots, width)
    arrived_out = lax.ppermute(output, "section", [(0, 1)])
    arrived_in = lax.ppermute(grad_in, "section", [(1, 0)])
    ends = jnp.where(
        first,
        jnp.concatenate([grad_in, arrived_in], axis=0),
        jnp.concatenate([arrived_out, output], axis=0),
    ).reshape((micro_count,) + dims[1:])
    squares = jnp.sum(jnp.square(ends.astype(F32)), axis=(2, 3))
    filled = (picture_tile_extents[..., 0] * picture_tile_extents[..., 1]).astype(F32)
    means = jnp.sqrt(squares / (filled * width))
    return (
        ends[None], means[None], expander, upshift, depthwise, depthshift, projector, postgain,
        postshift, pregain, preshift, attention, mixing, mixshift, midgain, midshift, widener,
        wideshift, narrower, narrowshift,
    )


def solution(mesh):
    tokens = P(None, "dp", None, None)
    placed = (tokens, tokens, P(None, "dp", None)) + (P(),) * 18
    return jax.shard_map(
        shards,
        mesh=mesh,
        in_specs=placed,
        out_specs=(P("section", None, "dp", None, None), P("section", None, "dp")) + (P(),) * 18,
        check_vma=False,
    )
```

```python
import functools
import math

import jax
import jax.numpy as jnp
from jax import lax
from jax.experimental import pallas as pl
from jax.experimental.pallas import tpu as pltpu
from jax.sharding import PartitionSpec as P

HEADS = 6
SIDE = 16
SLOTS = SIDE * SIDE
EPSILON = 1e-05
BLOCKED = -1000000000.0
LANES = 128
BLOCK = 256
FIXED = 4
SQUARE = 4
ROW = 4
PIECE = 144
HEIGHT = 48
ACROSS = PIECE // HEIGHT
SWAPPED = (0, 2, 1, 3)
BF16 = jnp.bfloat16
F32 = jnp.float32


def dot_nn(left, right):
    return jnp.dot(left, right, preferred_element_type=F32)


def dot_nt(left, right):
    return lax.dot_general(left, right, (((1,), (1,)), ((), ())), preferred_element_type=F32)


def dot_tn(left, right):
    return lax.dot_general(left, right, (((0,), (0,)), ((), ())), preferred_element_type=F32)


def norm_parts(values):
    centered = values - jnp.mean(values, axis=-1, keepdims=True)
    inverse = lax.rsqrt(jnp.mean(centered * centered, axis=-1, keepdims=True) + EPSILON)
    return centered * inverse, inverse


def norm_reverse(upstream, scaled, inverse, gain):
    lifted = upstream * gain
    return inverse * (
        lifted
        - jnp.mean(lifted, axis=-1, keepdims=True)
        - scaled * jnp.mean(lifted * scaled, axis=-1, keepdims=True)
    )


def across(vector):
    return vector[...].reshape(1, -1)


def own_share(tokens, numbers, rows):
    share = rows // (tokens.shape[1] * tokens.shape[2])
    return tokens[pl.ds(numbers[0, 0] * share, share)].reshape(rows, tokens.shape[3])


def total_rows(values):
    return jnp.sum(values, axis=0, keepdims=True)


def extent(numbers, image, local, side):
    micros, images = numbers.shape[1] - FIXED, numbers.shape[0] // 2
    first = numbers[0, 0] * (micros // 2) if local else 0
    return numbers[image % images * 2 + side, FIXED + first + image // images]


def valid_column(numbers, image):
    slot = lax.broadcasted_iota(jnp.int32, (SLOTS, 1), 0)
    height, width = (extent(numbers, image, True, side) for side in range(2))
    inside = (slot // SIDE < height) & (slot % SIDE < width)
    return inside.astype(F32)


def valid_rows(numbers, images):
    return jnp.concatenate([valid_column(numbers, image) for image in range(images)], axis=0)


def column_shifts(row, first_column, last_column):
    before = jnp.where(first_column, 0.0, pltpu.roll(row, 1, 0))
    after = jnp.where(last_column, 0.0, pltpu.roll(row, SIDE - 1, 0))
    return before, after


def conv_ahead_kernel(
    numbers, tokens, enlarge, enlarge_bias, taps, taps_bias, contract, gain, shift,
    sent, expanded, slope, active, projected, grid_cells,
):
    rows = sent.shape[0]
    images = rows // SLOTS
    width = sent.shape[1]
    channels = enlarge.shape[1]
    local_in = own_share(tokens, numbers, rows)
    valid = valid_rows(numbers, images)
    column = lax.broadcasted_iota(jnp.int32, (SIDE, BLOCK), 0)
    first_column, last_column = column == 0, column == SIDE - 1
    total = jnp.zeros((rows, width), F32)
    for start in range(0, channels, BLOCK):
        part = slice(start, start + BLOCK)
        cells = (dot_nn(local_in, enlarge[:, part]) + enlarge_bias[part].reshape(1, -1)) * valid
        grid_cells[...] = cells
        expanded[:, part] = cells.astype(BF16)
        kernel = [taps[tap : tap + 1, part] for tap in range(9)]
        bias = taps_bias[part].reshape(1, -1)
        for image in range(images):
            base = image * SLOTS
            above = here = None
            for line in range(SIDE + 1):
                if line < SIDE:
                    row = grid_cells[base + line * SIDE : base + (line + 1) * SIDE, :]
                    before, after = column_shifts(row, first_column, last_column)
                    sums = [
                        before * kernel[3 * a] + row * kernel[3 * a + 1] + after * kernel[3 * a + 2]
                        for a in range(3)
                    ]
                if line > 0:
                    convolved = above + sums[2] if line < SIDE else above
                    gate = jax.nn.sigmoid(convolved)
                    lit = convolved * gate
                    place = slice(base + (line - 1) * SIDE, base + line * SIDE)
                    active[place, part] = lit.astype(BF16)
                    slope[place, part] = (gate + lit * (1.0 - gate)).astype(BF16)
                if line < SIDE:
                    above = (here if line > 0 else bias) + sums[1]
                    here = bias + sums[0]
        total = total + dot_nn(active[:, part], contract[part, :])
    projected[...] = total
    scaled, _ = norm_parts(total)
    sent[...] = (local_in.astype(F32) + scaled * across(gain) + across(shift)).astype(BF16)


def head_lanes(width):
    return lax.broadcasted_iota(jnp.int32, (1, width), 1)


def attend_ahead_kernel(
    numbers, sent, gain, shift, mixing_in, mixing_out, mixing_bias,
    qkv, weights, context, middle,
):
    rows, width = sent.shape
    images = rows // SLOTS
    head = width // HEADS
    factor = 1.0 / math.sqrt(head)
    entering = sent[...].astype(F32)
    scaled, _ = norm_parts(entering)
    normed = (scaled * across(gain) + across(shift)).astype(BF16)
    for start in range(0, 3 * width, width):
        part = slice(start, start + width)
        qkv[:, part] = dot_nn(normed, mixing_in[:, part]).astype(BF16)
    pair = 2 * head
    lane = head_lanes(pair)
    for image in range(images):
        valid = valid_column(numbers, image) > 0.5
        place = slice(image * SLOTS, (image + 1) * SLOTS)
        for couple in range(HEADS // 2):
            at = couple * pair
            queries = qkv[place, at : at + pair]
            keys = qkv[place, width + at : width + at + pair]
            values = qkv[place, 2 * width + at : 2 * width + at + pair]
            gathered = []
            for side in range(2):
                own = (lane >= side * head) & (lane < (side + 1) * head)
                scores = dot_nt(jnp.where(own, keys, jnp.zeros_like(keys)), queries) * factor
                scores = jnp.where(valid, scores, BLOCKED)
                powers = jnp.exp(scores - jnp.max(scores, axis=0, keepdims=True))
                soft = powers * (1.0 / jnp.sum(powers, axis=0, keepdims=True))
                low = soft.astype(BF16)
                weights[image * HEADS + couple * 2 + side] = low
                gathered.append(dot_tn(low, values))
            context[place, at : at + pair] = jnp.where(lane < head, *gathered).astype(BF16)
    middle[...] = entering + dot_nn(context[...], mixing_out[...]) + across(mixing_bias)


def place_tall(pieces, grad, first_row, offset):
    for low in range(first_row, first_row + grad.shape[0], 16):
        piece, inside = low // HEIGHT, low % HEIGHT
        core, square, row = piece // (SQUARE * ROW), piece // ROW % SQUARE, piece % ROW
        for lane in range(ACROSS):
            at = offset + lane * HEIGHT + inside
            pieces[core, square, row, at : at + 16, :] = grad[
                low - first_row : low - first_row + 16, lane * LANES : (lane + 1) * LANES
            ]


def place_wide(pieces, grad, first_lane, offset, first_row=0):
    for block in range(grad.shape[0] // HEIGHT):
        for lane in range(grad.shape[1] // LANES):
            row, inside = (first_lane + lane) // ACROSS, (first_lane + lane) % ACROSS
            at = offset + inside * HEIGHT
            pieces[block // SQUARE, block % SQUARE, row - first_row, at : at + HEIGHT, :] = grad[
                block * HEIGHT : (block + 1) * HEIGHT, lane * LANES : (lane + 1) * LANES
            ]


def square_at(numbers, core, step):
    return numbers[0, 2] ^ jnp.where(core == 0, step, SWAPPED[step])


def row_at(numbers, step):
    return step % 2 * 2 + (numbers[0, 3] % 2 ^ step // 2)


def hand_out(numbers, pieces, keep, send):
    for target, core in ((keep, numbers[0, 1]), (send, 1 - numbers[0, 1])):
        for step in range(SQUARE):
            square = square_at(numbers, core, step)
            for along in range(ROW):
                target[step * ROW + along] = pieces[core, square, row_at(numbers, along)]


def mlp_kernel(
    numbers, middle, sensitivity, gain, shift, enlarge, enlarge_bias, contract, contract_bias,
    output, grad_middle, keep, send, small, wide_small, blocks,
):
    rows, width = middle.shape
    images = rows // SLOTS
    hidden_width = enlarge.shape[1]
    valid = valid_rows(numbers, images)
    center = middle[...]
    scaled, inverse = norm_parts(center)
    hidden = (scaled * across(gain) + across(shift)).astype(BF16)
    grad_out = own_share(sensitivity, numbers, rows).astype(F32) * valid
    out_low = grad_out.astype(BF16)
    total = jnp.zeros((rows, width), F32)
    grad_hidden = jnp.zeros((rows, width), F32)
    for start in range(0, hidden_width, BLOCK):
        part = slice(start, start + BLOCK)
        widened = dot_nn(hidden, enlarge[:, part]) + enlarge_bias[part].reshape(1, -1)
        normal_cdf = 0.5 * (1.0 + lax.erf(widened * (1.0 / math.sqrt(2.0))))
        normal_pdf = jnp.exp(-0.5 * widened * widened) * (1.0 / math.sqrt(2.0 * math.pi))
        activated = (widened * normal_cdf).astype(BF16)
        total = total + dot_nn(activated, contract[part, :])
        grad_wide = dot_nt(out_low, contract[part, :]) * (normal_cdf + widened * normal_pdf)
        wide_small[:, part] = total_rows(grad_wide)
        wide_low = grad_wide.astype(BF16)
        place_tall(blocks, dot_tn(activated, out_low).astype(BF16), start, 0)
        place_wide(blocks, dot_tn(hidden, wide_low).astype(BF16), start // LANES, PIECE)
        grad_hidden = grad_hidden + dot_nt(wide_low, enlarge[:, part])
    output[...] = ((center + total + across(contract_bias)) * valid).astype(BF16)
    gradient = grad_out + norm_reverse(grad_hidden, scaled, inverse, across(gain))
    grad_middle[...] = gradient
    small[0:1, :] = total_rows(grad_out)
    small[1:2, :] = total_rows(grad_hidden * scaled)
    small[2:3, :] = total_rows(grad_hidden)
    small[3:4, :] = total_rows(gradient)
    hand_out(numbers, blocks, keep, send)


def heads_back_kernel(
    grad_middle, qkv, weights, mixing_out, grad_qkv,
):
    rows, width = grad_middle.shape
    images = rows // SLOTS
    head = width // HEADS
    factor = 1.0 / math.sqrt(head)
    grad_context = dot_nt(grad_middle[...].astype(BF16), mixing_out[...]).astype(BF16)
    pair = 2 * head
    lane = head_lanes(pair)
    for image in range(images):
        place = slice(image * SLOTS, (image + 1) * SLOTS)
        for couple in range(HEADS // 2):
            at = couple * pair
            queries = qkv[place, at : at + pair]
            keys = qkv[place, width + at : width + at + pair]
            values = qkv[place, 2 * width + at : 2 * width + at + pair]
            upstream = grad_context[place, at : at + pair]
            parts = []
            for side in range(2):
                own = (lane >= side * head) & (lane < (side + 1) * head)
                low = weights[image * HEADS + couple * 2 + side]
                soft = low.astype(F32)
                grad_values = dot_nn(low, upstream)
                lifted = soft * dot_nt(jnp.where(own, values, jnp.zeros_like(values)), upstream)
                scores_low = (lifted - soft * jnp.sum(lifted, axis=0, keepdims=True)).astype(BF16)
                parts.append(
                    (
                        dot_tn(scores_low, keys) * factor,
                        dot_nn(scores_low, queries) * factor,
                        grad_values,
                    )
                )
            for which in range(3):
                merged = jnp.where(lane < head, parts[0][which], parts[1][which])
                grad_qkv[place, which * width + at : which * width + at + pair] = merged.astype(
                    BF16
                )


def sent_back_kernel(
    numbers, sent, grad_middle, grad_qkv, context, projected, active, gain, shift, mixing_in,
    conv_gain, grad_sent, proj_low, keep, send, small, blocks,
):
    rows, width = sent.shape
    gradient = grad_middle[...]
    entering = sent[...].astype(F32)
    scaled, inverse = norm_parts(entering)
    normed = (scaled * across(gain) + across(shift)).astype(BF16)
    lifted = jnp.zeros((rows, width), F32)
    for which in range(3):
        part = slice(which * width, (which + 1) * width)
        piece = grad_qkv[:, part]
        place_wide(blocks, dot_tn(normed, piece).astype(BF16), which * width // LANES, 0)
        lifted = lifted + dot_nt(piece, mixing_in[:, part])
    mixing = dot_tn(context[...], gradient.astype(BF16)).astype(BF16)
    place_wide(blocks, mixing, 3 * width // LANES, 0)
    grad_low = (gradient + norm_reverse(lifted, scaled, inverse, across(gain))).astype(BF16)
    grad_sent[...] = grad_low
    small[0:1, :] = total_rows(lifted * scaled)
    small[1:2, :] = total_rows(lifted)
    incoming = grad_low.astype(F32)
    scaled, inverse = norm_parts(projected[...])
    low = norm_reverse(incoming, scaled, inverse, across(conv_gain)).astype(BF16)
    proj_low[...] = low
    small[2:3, :] = total_rows(incoming * scaled)
    small[3:4, :] = total_rows(incoming)
    for start in range(0, active.shape[1], BLOCK):
        part = slice(start, start + BLOCK)
        place_tall(blocks, dot_tn(active[:, part], low).astype(BF16), start, PIECE)
    hand_out(numbers, blocks, keep, send)


def conv_part(
    numbers, local_in, proj_low, expanded, slope, enlarge, taps, contract, wide_small, grad_cells,
    blocks, total, first, last, first_row=0,
):
    rows = local_in.shape[0]
    images = rows // SLOTS
    valid = valid_rows(numbers, images)
    column = lax.broadcasted_iota(jnp.int32, (SIDE, LANES), 0)
    first_column, last_column = column == 0, column == SIDE - 1
    for start in range(first, last, BLOCK):
        part = slice(start, start + BLOCK)
        grad_conv = dot_nt(proj_low, contract[part, :]) * slope[:, part].astype(F32)
        wide_small[9:10, part] = total_rows(grad_conv)
        grad_cells[...] = grad_conv
        pieces = []
        for lanes in range(0, BLOCK, LANES):
            chans = slice(start + lanes, start + lanes + LANES)
            kernel = [taps[tap : tap + 1, chans] for tap in range(9)]
            sums = [jnp.zeros((SIDE, LANES), F32) for _ in range(9)]
            outcome = []
            for image in range(images):
                base = image * SLOTS
                shifted = {}
                for line in range(SIDE):
                    for ahead in (line, line + 1):
                        if ahead < SIDE and ahead not in shifted:
                            row = grad_cells[
                                base + ahead * SIDE : base + (ahead + 1) * SIDE,
                                lanes : lanes + LANES,
                            ]
                            before, after = column_shifts(row, first_column, last_column)
                            shifted[ahead] = (after, row, before)
                    place = slice(base + line * SIDE, base + (line + 1) * SIDE)
                    cells = expanded[place, chans].astype(F32)
                    grid = jnp.zeros((SIDE, LANES), F32)
                    for a in range(3):
                        if 0 <= line + 1 - a < SIDE:
                            for b in range(3):
                                moved = shifted[line + 1 - a][b]
                                sums[3 * a + b] = sums[3 * a + b] + cells * moved
                                grid = grid + moved * kernel[3 * a + b]
                    outcome.append(grid)
            for tap in range(9):
                wide_small[tap : tap + 1, chans] = total_rows(sums[tap])
            pieces.append(jnp.concatenate(outcome, axis=0) * valid)
        grad_expanded = jnp.concatenate(pieces, axis=1)
        wide_small[10:11, part] = total_rows(grad_expanded)
        expanded_low = grad_expanded.astype(BF16)
        place_wide(
            blocks, dot_tn(local_in, expanded_low).astype(BF16), start // LANES, 0, first_row
        )
        total = total + dot_nt(expanded_low, enlarge[:, part])
    return total


def conv_back_kernel(
    numbers, tokens, grad_sent, proj_low, expanded, slope, enlarge, taps, contract,
    total, early, early_wide, grad_cells,
):
    rows, width = grad_sent.shape
    total[...] = conv_part(
        numbers, own_share(tokens, numbers, rows), proj_low[...], expanded, slope, enlarge, taps,
        contract, early_wide, grad_cells, early, grad_sent[...].astype(F32), 0,
        enlarge.shape[1] // 2,
    )


def small_rows(small, wide):
    mlp, sent = small
    mlp_wide, conv_wide = wide
    found = []
    for source, rows in ((mlp, 4), (sent, 4), (mlp_wide, 1), (conv_wide, 11)):
        for row in range(rows):
            for at in range(0, source.shape[1], LANES):
                found.append((source, row, at))
    return found


def conv_end_kernel(
    numbers, tokens, total, proj_low, expanded, slope, enlarge, taps, contract, early, early_wide,
    mlp_small, sent_small, mlp_wide, output, own, give, keep, send, pieces, conv_wide, grad_cells,
    short,
):
    rows, width = total.shape
    channels = enlarge.shape[1]
    half = channels // 2
    conv_wide[:, 0:half] = early_wide[:, 0:half]
    pieces[:, :, 0 : ROW // 2, 0:PIECE, :] = early[...]
    gradient = conv_part(
        numbers, own_share(tokens, numbers, rows), proj_low[...], expanded, slope, enlarge, taps,
        contract, conv_wide, grad_cells, pieces, total[...], half, channels,
    ).astype(BF16)
    first = numbers[0, 0] == 0
    own[...] = jnp.where(first, gradient, output[...])
    give[...] = jnp.where(first, output[...], gradient)
    short[...] = jnp.zeros_like(short)
    places = small_rows((mlp_small, sent_small), (mlp_wide, conv_wide))
    for number, (source, row, at) in enumerate(places):
        piece, inside = number // 8, number % 8
        short[piece, inside : inside + 1, :] = source[row : row + 1, at : at + LANES]
    for piece in range(2 * SQUARE * ROW):
        value = short[piece]
        high = value.astype(BF16).astype(F32)
        pair = jnp.concatenate([high, value - high], axis=0).astype(BF16)
        core, square, row = piece // (SQUARE * ROW), piece // ROW % SQUARE, piece % ROW
        pieces[core, square, row, PIECE : PIECE + 16, :] = pair
    hand_out(numbers, pieces, keep, send)


def summed(parts, short):
    total = parts[0].astype(F32)
    for part in parts[1:]:
        total = total + part.astype(F32)
    if not short:
        return total.astype(BF16)
    main = total.shape[0] - short
    value = total[main : main + 8] + total[main + 8 : main + 16]
    high = value.astype(BF16).astype(F32)
    return jnp.concatenate([total[:main], high, value - high], axis=0).astype(BF16)


def halve_kernel(short, keep, arrived, kept, send):
    half = kept.shape[0]
    for step in range(half):
        kept[step] = summed((keep[step], arrived[step]), short)
        send[step] = summed((keep[half + step], arrived[half + step]), short)


def sum_kernel(short, keep, arrived, out):
    for step in range(out.shape[0]):
        out[step] = summed((keep[step], arrived[step]), short)


def join_kernel(short, own, arrived, out):
    half = own.shape[0]
    out[0:half] = own[...]
    out[half:] = arrived[...]


def pieces_of(numbers, parts):
    half = SQUARE * ROW // 2
    for side in range(2):
        core = numbers[0, 1] if side == 0 else 1 - numbers[0, 1]
        for step in range(2 * half):
            square = square_at(numbers, core, step // ROW)
            yield core * SQUARE + square, row_at(numbers, step % ROW), parts[2 * side + step // half], step % half


def write_tall(target, block, row, part, step, offset):
    at = pl.multiple_of((block * ROW + row) * HEIGHT, 16)
    for lane in range(ACROSS):
        low = offset + lane * HEIGHT
        target[pl.ds(at, HEIGHT), lane * LANES : (lane + 1) * LANES] = part[
            step, low : low + HEIGHT, :
        ].astype(F32)


def write_wide(target, block, row, part, step, offset):
    at = pl.multiple_of(block * HEIGHT, 16)
    for lane in range(ACROSS):
        low = offset + lane * HEIGHT
        column = pl.multiple_of((row * ACROSS + lane) * LANES, LANES)
        target[pl.ds(at, HEIGHT), pl.ds(column, LANES)] = part[step, low : low + HEIGHT, :].astype(
            F32
        )


def mlp_end_kernel(numbers, *refs):
    narrower, widener = refs[4:]
    for block, row, part, step in pieces_of(numbers, refs):
        write_tall(narrower, block, row, part, step, 0)
        write_wide(widener, block, row, part, step, PIECE)


def sent_end_kernel(numbers, *refs):
    attention, mixing, projector, joint = refs[4:]
    for block, row, part, step in pieces_of(numbers, refs):
        write_wide(joint, block, row, part, step, 0)
        write_tall(projector, block, row, part, step, PIECE)
    attention[...] = joint[:, : attention.shape[1]]
    mixing[...] = joint[:, attention.shape[1] :]


def conv_all_kernel(numbers, *refs):
    expander, shorts, short = refs[4], refs[5:-1], refs[-1]
    for block, row, part, step in pieces_of(numbers, refs):
        write_wide(expander, block, row, part, step, 0)
        pair = part[step, PIECE : PIECE + 16, :].astype(F32)
        short[pl.ds(pl.multiple_of((block * ROW + row) * 8, 8), 8), :] = pair[0:8] + pair[8:16]
    (upshift, depthwise, depthshift, postgain, postshift, pregain, preshift, mixshift, midgain,
     midshift, wideshift, narrowshift) = shorts
    lanes = narrowshift.shape[0] // LANES
    wide_lanes = upshift.shape[0] // LANES
    number = 0
    for target in (narrowshift, midgain, midshift, mixshift, pregain, preshift, postgain, postshift):
        for lane in range(lanes):
            target[lane * LANES : (lane + 1) * LANES] = short[number, :]
            number += 1
    for target in (wideshift,) + (depthwise,) * 9 + (depthshift, upshift):
        for lane in range(wide_lanes):
            value = short[number : number + 1, :]
            if target is depthwise:
                tap = number // wide_lanes - 3
                target[tap : tap + 1, lane * LANES : (lane + 1) * LANES] = value
            else:
                target[lane * LANES : (lane + 1) * LANES] = value.reshape(LANES)
            number += 1


def ends_kernel(numbers, own, arrived, ends, means):
    share = ends.shape[0] // 2
    local, slots, width = ends.shape[1:]
    first = numbers[0, 0]
    ends[pl.ds(first * share, share)] = own[...].reshape(share, local, slots, width)
    ends[pl.ds((1 - first) * share, share)] = arrived[...].reshape(share, local, slots, width)
    for micro in range(ends.shape[0]):
        for image in range(local):
            value = ends[micro, image].astype(F32)
            square = jnp.sum(value * value, axis=0, keepdims=True)
            number = micro * local + image
            filled = extent(numbers, number, False, 0) * extent(numbers, number, False, 1) * width
            mean = jnp.sum(square, axis=1, keepdims=True) / filled.astype(F32)
            means[0, micro : micro + 1, image : image + 1] = jnp.sqrt(mean)


WHOLE = pl.BlockSpec(memory_space=pltpu.VMEM)
ANYWHERE = pl.BlockSpec(memory_space=pl.ANY)
COST = 30
BOTH = ("section", "dp")


def shape(dims, kind):
    return jax.ShapeDtypeStruct(dims, kind)


class Calls:
    def __init__(self, numbers):
        self.numbers = numbers
        self.last = None

    def __call__(self, kernel, name, ins, outs, scratch=(), plain=False, mb=8, us=0):
        count = len(ins)
        after = () if self.last is None else (self.last,)

        def body(numbers, *refs):
            refs = refs[:count] + refs[count + len(after) :]
            return kernel(*refs) if plain else kernel(numbers, *refs)

        result = pl.pallas_call(
            body,
            out_shape=outs,
            in_specs=[pl.BlockSpec(memory_space=pltpu.SMEM)]
            + [WHOLE] * count
            + [ANYWHERE] * len(after),
            out_specs=[WHOLE] * len(outs),
            scratch_shapes=list(scratch),
            cost_estimate=pl.CostEstimate(flops=1 + int(us * 1e9), bytes_accessed=1, transcendentals=0),
            compiler_params=pltpu.CompilerParams(vmem_limit_bytes=mb * 1024 * 1024),
            name=name,
        )(self.numbers, *ins, *after)
        self.last = result[0]
        return result


def swapped(value, digit, step=1):
    sections, members = (lax.axis_size(axis) for axis in BOTH)
    pairs = []
    for section in range(sections):
        for member in range(members):
            if digit == "first" or digit == "second":
                along = (digit == "first") == (member % 2 == 0)
                other = (section ^ along) * members + (member ^ (0 if along else 2))
            elif digit == "near":
                other = section * members + (member ^ 4)
            else:
                other = section * members + (member ^ (step * digit))
            pairs.append((section * members + member, other))
    return lax.ppermute(value, BOTH, pairs)


class Group:
    def __init__(self, name, calls, keep, send, short=0):
        self.name, self.calls, self.keep, self.short = name, calls, keep, short
        self.rows = keep.shape[1]
        self.arrived = swapped(send, 1)

    def call(self, kernel, what, ins, outs):
        return self.calls(
            functools.partial(kernel, self.short), f"{self.name}_{what}", ins,
            [shape(dims + (self.rows, LANES), BF16) for dims in outs], plain=True, us=COST,
        )

    def halve(self, digit):
        half = (self.keep.shape[0] // 2,)
        self.keep, send = self.call(halve_kernel, digit, (self.keep, self.arrived), [half] * 2)
        self.arrived = swapped(send, digit)

    def first(self):
        self.halve("first")

    def second(self):
        self.halve("second")

    def near(self):
        self.halve("near")

    def add(self, what, digit, step):
        (self.keep,) = self.call(sum_kernel, what, (self.keep, self.arrived), [self.keep.shape[:1]])
        self.arrived = swapped(self.keep, digit, step)

    def far(self):
        self.add("far", 4, 2)
        stride = 4 * ROW
        while stride < lax.axis_size("dp"):
            self.add(f"over_{stride}", stride, 1)
            stride *= 2

    def total(self):
        self.add("total", 4, 1)

    def join(self, what, digit):
        dims = (2 * self.keep.shape[0],)
        (self.keep,) = self.call(join_kernel, what, (self.keep, self.arrived), [dims])
        self.arrived = swapped(self.keep, digit)

    def join_row(self):
        self.join("join_row", "second")

    def join_square(self):
        self.join("join", "first")
        self.near_half = swapped(self.keep, 1)

    def join_cores(self):
        self.blocks = [self.keep, self.arrived, self.near_half, swapped(self.arrived, 1)]


def shards(
    entering_tokens,
    output_sensitivity,
    picture_tile_extents,
    pointwise_enlarge,
    enlarge_bias,
    channelwise_kernel,
    channelwise_conv_bias,
    pointwise_contract,
    convblock_scale,
    convblock_offset,
    attend_scale,
    attend_offset,
    query_key_proj,
    heads_output_proj,
    heads_output_bias,
    feedforward_scale,
    feedforward_offset,
    feedforward_enlarge,
    feedforward_enlarge_bias,
    feedforward_contract,
    contract_bias,
):
    micro_count, local_images, slots, width = entering_tokens.shape
    channels = pointwise_enlarge.shape[1]
    section, member = lax.axis_index("section"), lax.axis_index("dp")
    share = micro_count // 2
    images = share * local_images
    rows = images * slots
    fixed = jnp.stack(
        [section, member % 2, section * 2 + member // 2 % 2, member // 4 % ROW]
    ).astype(jnp.int32)
    extents = jnp.transpose(picture_tile_extents, (1, 2, 0)).reshape(-1, micro_count)
    numbers = jnp.concatenate(
        [jnp.broadcast_to(fixed, (2 * local_images, FIXED)), extents], axis=1
    )

    call = Calls(numbers)
    sent, expanded, slope, active, projected = call(
        conv_ahead_kernel, "conv_ahead",
        (entering_tokens, pointwise_enlarge, enlarge_bias, channelwise_kernel,
         channelwise_conv_bias, pointwise_contract, convblock_scale, convblock_offset),
        (shape((rows, width), BF16), shape((rows, channels), BF16), shape((rows, channels), BF16),
         shape((rows, channels), BF16), shape((rows, width), F32)),
        [pltpu.VMEM((rows, BLOCK), F32)], mb=20,
    )
    qkv, weights, context, middle = call(
        attend_ahead_kernel, "attend_ahead",
        (sent, attend_scale, attend_offset, query_key_proj, heads_output_proj, heads_output_bias),
        (shape((rows, 3 * width), BF16), shape((images * HEADS, slots, slots), BF16),
         shape((rows, width), BF16), shape((rows, width), F32)), mb=16,
    )
    halves = [shape((SQUARE * ROW, 2 * PIECE, LANES), BF16)] * 2
    whole = [pltpu.VMEM((2, SQUARE, ROW, 2 * PIECE, LANES), BF16)]
    output, grad_middle, keep, send, mlp_small, mlp_wide = call(
        mlp_kernel, "mlp",
        (middle, output_sensitivity, feedforward_scale, feedforward_offset, feedforward_enlarge,
         feedforward_enlarge_bias, feedforward_contract, contract_bias),
        [shape((rows, width), BF16), shape((rows, width), F32)] + halves
        + [shape((8, width), F32), shape((1, channels), F32)],
        whole, mb=24,
    )
    mlp = Group("mlp", call, keep, send)
    (grad_qkv,) = call(
        heads_back_kernel, "heads_back", (grad_middle, qkv, weights, heads_output_proj),
        [shape((rows, 3 * width), BF16)], plain=True, mb=16,
    )
    mlp.first()
    grad_sent, proj_low, keep, send, sent_small = call(
        sent_back_kernel, "sent_back",
        (sent, grad_middle, grad_qkv, context, projected, active, attend_scale, attend_offset,
         query_key_proj, convblock_scale),
        [shape((rows, width), BF16), shape((rows, width), BF16)] + halves
        + [shape((8, width), F32)],
        whole, mb=24,
    )
    inner = Group("inner", call, keep, send)
    early_pieces = shape((2, SQUARE, ROW // 2, PIECE, LANES), BF16)
    total, early, early_wide = call(
        conv_back_kernel, "conv_back",
        (entering_tokens, grad_sent, proj_low, expanded, slope, pointwise_enlarge,
         channelwise_kernel, pointwise_contract),
        [shape((rows, width), F32), early_pieces, shape((16, channels), F32)],
        [pltpu.VMEM((rows, BLOCK), F32)], mb=20,
    )
    mlp.second()
    inner.first()
    halves = [shape((SQUARE * ROW, PIECE + 16, LANES), BF16)] * 2
    own, give, keep, send = call(
        conv_end_kernel, "conv_end",
        (entering_tokens, total, proj_low, expanded, slope, pointwise_enlarge, channelwise_kernel,
         pointwise_contract, early, early_wide, mlp_small, sent_small, mlp_wide, output),
        [shape((rows, width), BF16)] * 2 + halves,
        [pltpu.VMEM((2, SQUARE, ROW, PIECE + 16, LANES), BF16), pltpu.VMEM((16, channels), F32),
         pltpu.VMEM((rows, BLOCK), F32), pltpu.VMEM((2 * SQUARE * ROW, 8, LANES), F32)],
        mb=20,
    )
    conv = Group("conv", call, keep, send, 16)
    mlp.near()
    inner.second()
    conv.first()
    mlp.far()
    inner.near()
    conv.second()
    mlp.total()
    inner.far()
    conv.near()
    arrived = lax.ppermute(give, "section", [(0, 1), (1, 0)])
    mlp.join_row()
    conv.far()
    inner.total()
    mlp.join_square()
    ends, means = call(
        ends_kernel, "ends", (own, arrived),
        [shape(entering_tokens.shape, BF16), shape((1, micro_count, local_images), F32)],
    )
    conv.total()
    inner.join_row()
    conv.join_row()
    mlp.join_cores()
    inner.join_square()

    line, wide_line = shape((width,), F32), shape((channels,), F32)
    tall, wide = shape((channels, width), F32), shape((width, channels), F32)
    narrower, widener = call(mlp_end_kernel, "mlp_end", mlp.blocks, [tall, wide], mb=12)
    conv.join_square()
    inner.join_cores()
    attention, mixing, projector = call(
        sent_end_kernel, "sent_end", inner.blocks,
        [shape((width, 3 * width), F32), shape((width, width), F32), tall],
        [pltpu.VMEM((width, 4 * width), F32)], mb=12,
    )
    conv.join_cores()
    (expander, upshift, depthwise, depthshift, postgain, postshift, pregain, preshift, mixshift,
     midgain, midshift, wideshift, narrowshift) = call(
        conv_all_kernel, "conv_all", conv.blocks,
        [wide, wide_line, shape((9, channels), F32), wide_line] + [line] * 7 + [wide_line, line],
        [pltpu.VMEM((2 * SQUARE * ROW * 8, LANES), F32)],
    )
    return (
        ends[None], means, expander, upshift, depthwise, depthshift, projector, postgain,
        postshift, pregain, preshift, attention, mixing, mixshift, midgain, midshift, widener,
        wideshift, narrower, narrowshift,
    )


def solution(mesh):
    tokens = P(None, "dp", None, None)
    placed = (tokens, tokens, P(None, "dp", None)) + (P(),) * 18
    return jax.shard_map(
        shards,
        mesh=mesh,
        in_specs=placed,
        out_specs=(P("section", None, "dp", None, None), P("section", None, "dp")) + (P(),) * 18,
        check_vma=False,
    )
```

```python
import functools
import math

import jax
import jax.numpy as jnp
from jax import lax
from jax.experimental import pallas as pl
from jax.experimental.pallas import tpu as pltpu
from jax.sharding import PartitionSpec as P

HEADS = 6
SIDE = 16
SLOTS = SIDE * SIDE
EPSILON = 1e-05
BLOCKED = -1000000000.0
LANES = 128
BLOCK = 256
SQUARE = 4
ROW = 4
PIECE = 144
HEIGHT = 48
ACROSS = PIECE // HEIGHT
SWAPPED = (0, 2, 1, 3)
BF16 = jnp.bfloat16
F32 = jnp.float32


def dot_nn(left, right):
    return jnp.dot(left, right, preferred_element_type=F32)


def dot_nt(left, right):
    return lax.dot_general(left, right, (((1,), (1,)), ((), ())), preferred_element_type=F32)


def dot_tn(left, right):
    return lax.dot_general(left, right, (((0,), (0,)), ((), ())), preferred_element_type=F32)


def norm_parts(values):
    centered = values - jnp.mean(values, axis=-1, keepdims=True)
    inverse = lax.rsqrt(jnp.mean(centered * centered, axis=-1, keepdims=True) + EPSILON)
    return centered * inverse, inverse


def norm_reverse(upstream, scaled, inverse, gain):
    lifted = upstream * gain
    return inverse * (
        lifted
        - jnp.mean(lifted, axis=-1, keepdims=True)
        - scaled * jnp.mean(lifted * scaled, axis=-1, keepdims=True)
    )


def across(vector):
    return vector[...].reshape(1, -1)


def own_share(tokens, rows):
    share = rows // (tokens.shape[1] * tokens.shape[2])
    return tokens[pl.ds(Here().section * share, share)].reshape(rows, tokens.shape[3])


def total_rows(values):
    return jnp.sum(values, axis=0, keepdims=True)


class Here:
    def __init__(self):
        member = lax.axis_index("dp")
        self.section = lax.axis_index("section")
        self.core = member % 2
        self.square = self.section * 2 + member // 2 % 2
        self.row = member // 4 % ROW


def own_share(tokens, rows):
    share = rows // (tokens.shape[1] * tokens.shape[2])
    return tokens[pl.ds(Here().section * share, share)].reshape(rows, tokens.shape[3])


def total_rows(values):
    return jnp.sum(values, axis=0, keepdims=True)


def own_share(tokens, rows):
    share = rows // (tokens.shape[1] * tokens.shape[2])
    return tokens[pl.ds(Here().section * share, share)].reshape(rows, tokens.shape[3])


def total_rows(values):
    return jnp.sum(values, axis=0, keepdims=True)


class Here:
    def __init__(self):
        member = lax.axis_index("dp")
        self.section = lax.axis_index("section")
        self.core = member % 2
        self.square = self.section * 2 + member // 2 % 2
        self.row = member // 4 % ROW


def own_share(tokens, rows):
    share = rows // (tokens.shape[1] * tokens.shape[2])
    return tokens[pl.ds(Here().section * share, share)].reshape(rows, tokens.shape[3])


def total_rows(values):
    return jnp.sum(values, axis=0, keepdims=True)


def extent(numbers, image, local, side):
    micros, images = numbers.shape[1] - FIXED, numbers.shape[0] // 2
    first = numbers[0, 0] * (micros // 2) if local else 0
    return numbers[image % images * 2 + side, FIXED + first + image // images]


def valid_column(numbers, image):
    slot = lax.broadcasted_iota(jnp.int32, (SLOTS, 1), 0)
    height, width = (extent(numbers, image, True, side) for side in range(2))
    inside = (slot // SIDE < height) & (slot % SIDE < width)
    return inside.astype(F32)


def valid_rows(numbers, images):
    return jnp.concatenate([valid_column(numbers, image) for image in range(images)], axis=0)


def column_shifts(row, first_column, last_column):
    before = jnp.where(first_column, 0.0, pltpu.roll(row, 1, 0))
    after = jnp.where(last_column, 0.0, pltpu.roll(row, SIDE - 1, 0))
    return before, after


def conv_ahead_kernel(
    extents, tokens, enlarge_from, enlarge_bias_from, taps_from, taps_bias_from, contract_from,
    gain_from, shift_from, sent, expanded, slope, active, projected, inside, filled,
    grid_cells, entering, enlarge, enlarge_bias, taps, taps_bias, contract, gain, shift, arrivals,
):
    rows, width = sent.shape
    images = rows // SLOTS
    channels = enlarge.shape[1]
    share = entering.shape[0]
    starts = range(0, channels, BLOCK)
    section = Here().section
    copies = [(tokens.at[pl.ds(section * share, share)], entering)]
    copies += [(enlarge_from.at[:, pl.ds(0, BLOCK)], enlarge.at[:, pl.ds(0, BLOCK)])]
    copies += [
        (enlarge_bias_from, enlarge_bias), (taps_from, taps), (taps_bias_from, taps_bias),
        (gain_from, gain), (shift_from, shift),
    ]
    early = len(copies)
    for start in starts:
        part = pl.ds(start, BLOCK)
        if start:
            copies.append((enlarge_from.at[:, part], enlarge.at[:, part]))
        copies.append((contract_from.at[part], contract.at[part]))
    copies = [
        pltpu.make_async_copy(source, target, arrivals.at[number])
        for number, (source, target) in enumerate(copies)
    ]
    for copy in copies:
        copy.start()
    micros, local = extents.shape[2], extents.shape[0]
    for image in range(micros * local):
        count = extents[image % local, 0, image // local] * extents[image % local, 1, image // local]
        filled[image : image + 1, :] = jnp.full((1, LANES), (count * width).astype(F32))
    slot = lax.broadcasted_iota(jnp.int32, (SLOTS, 1), 0)
    for image in range(images):
        height, across_it = (
            extents[image % local, side, section * share + image // local] for side in range(2)
        )
        held = (slot // SIDE < height) & (slot % SIDE < across_it)
        inside[image * SLOTS : (image + 1) * SLOTS, :] = held.astype(F32)
    for copy in copies[:early]:
        copy.wait()
    later = copies[early:]
    local_in = entering[...].reshape(rows, width)
    valid = inside[...]
    column = lax.broadcasted_iota(jnp.int32, (SIDE, BLOCK), 0)
    first_column, last_column = column == 0, column == SIDE - 1
    total = jnp.zeros((rows, width), F32)

    def cells_of(start):
        part = slice(start, start + BLOCK)
        if start:
            later[2 * (start // BLOCK) - 1].wait()
        cells = (dot_nn(local_in, enlarge[:, part]) + enlarge_bias[part].reshape(1, -1)) * valid
        grid_cells[start // BLOCK % 2] = cells
        expanded[:, part] = cells.astype(BF16)

    cells_of(0)
    for start in starts:
        part = slice(start, start + BLOCK)
        number = start // BLOCK
        if start + BLOCK < channels:
            cells_of(start + BLOCK)
        kernel = [taps[tap : tap + 1, part] for tap in range(9)]
        bias = taps_bias[part].reshape(1, -1)
        for image in range(images):
            base = image * SLOTS
            above = here = None
            for line in range(SIDE + 1):
                if line < SIDE:
                    row = grid_cells[number % 2, base + line * SIDE : base + (line + 1) * SIDE, :]
                    before, after = column_shifts(row, first_column, last_column)
                    sums = [
                        before * kernel[3 * a] + row * kernel[3 * a + 1] + after * kernel[3 * a + 2]
                        for a in range(3)
                    ]
                if line > 0:
                    convolved = above + sums[2] if line < SIDE else above
                    gate = jax.nn.sigmoid(convolved)
                    lit = convolved * gate
                    place = slice(base + (line - 1) * SIDE, base + line * SIDE)
                    active[place, part] = lit.astype(BF16)
                    slope[place, part] = (gate + lit * (1.0 - gate)).astype(BF16)
                if line < SIDE:
                    above = (here if line > 0 else bias) + sums[1]
                    here = bias + sums[0]
        later[2 * number].wait()
        total = total + dot_nn(active[:, part], contract[part, :])
    projected[...] = total
    scaled, _ = norm_parts(total)
    sent[...] = (local_in.astype(F32) + scaled * across(gain) + across(shift)).astype(BF16)


def head_lanes(width):
    return lax.broadcasted_iota(jnp.int32, (1, width), 1)


def attend_ahead_kernel(
    inside, sent, gain, shift, mixing_in, mixing_out, mixing_bias,
    qkv, weights, context, middle,
):
    rows, width = sent.shape
    images = rows // SLOTS
    head = width // HEADS
    factor = 1.0 / math.sqrt(head)
    entering = sent[...].astype(F32)
    scaled, _ = norm_parts(entering)
    normed = (scaled * across(gain) + across(shift)).astype(BF16)
    for start in range(0, 3 * width, width):
        part = slice(start, start + width)
        qkv[:, part] = dot_nn(normed, mixing_in[:, part]).astype(BF16)
    pair = 2 * head
    lane = head_lanes(pair)
    valid = [inside[image * SLOTS : (image + 1) * SLOTS, :] > 0.5 for image in range(images)]
    order = [(image, number) for image in range(images) for number in range(HEADS)]

    def where_of(image, number):
        at = number // 2 * pair
        return slice(image * SLOTS, (image + 1) * SLOTS), at

    def scores_of(image, number):
        place, at = where_of(image, number)
        low, high = number % 2 * head, (number % 2 + 1) * head
        keys = qkv[place, width + at : width + at + pair]
        own = jnp.where((lane >= low) & (lane < high), keys, jnp.zeros_like(keys))
        return dot_nt(own, qkv[place, at : at + pair])

    ahead = scores_of(*order[0])
    gathered = []
    for turn, (image, number) in enumerate(order):
        scores = ahead
        if turn + 1 < len(order):
            ahead = scores_of(*order[turn + 1])
        scores = jnp.where(valid[image], scores * factor, BLOCKED)
        powers = jnp.exp(scores - jnp.max(scores, axis=0, keepdims=True))
        low = (powers * (1.0 / jnp.sum(powers, axis=0, keepdims=True))).astype(BF16)
        weights[image * HEADS + number] = low
        place, at = where_of(image, number)
        gathered.append(dot_tn(low, qkv[place, 2 * width + at : 2 * width + at + pair]))
        if number % 2:
            context[place, at : at + pair] = jnp.where(lane < head, *gathered).astype(BF16)
            gathered = []
    middle[...] = entering + dot_nn(context[...], mixing_out[...]) + across(mixing_bias)


def place_tall(pieces, grad, first_row, offset):
    for low in range(first_row, first_row + grad.shape[0], 16):
        piece, inside = low // HEIGHT, low % HEIGHT
        core, square, row = piece // (SQUARE * ROW), piece // ROW % SQUARE, piece % ROW
        for lane in range(ACROSS):
            at = offset + lane * HEIGHT + inside
            pieces[core, square, row, at : at + 16, :] = grad[
                low - first_row : low - first_row + 16, lane * LANES : (lane + 1) * LANES
            ]


def place_wide(pieces, grad, first_lane, offset, first_row=0):
    for block in range(grad.shape[0] // HEIGHT):
        for lane in range(grad.shape[1] // LANES):
            row, inside = (first_lane + lane) // ACROSS, (first_lane + lane) % ACROSS
            at = offset + inside * HEIGHT
            pieces[block // SQUARE, block % SQUARE, row - first_row, at : at + HEIGHT, :] = grad[
                block * HEIGHT : (block + 1) * HEIGHT, lane * LANES : (lane + 1) * LANES
            ]


def square_at(here, core, step):
    return here.square ^ jnp.where(core == 0, step, SWAPPED[step])


def row_at(here, step):
    return step % 2 * 2 + (here.row % 2 ^ step // 2)


def hand_out(pieces, keep, send):
    here = Here()
    for target, core in ((keep, here.core), (send, 1 - here.core)):
        for step in range(SQUARE):
            square = square_at(here, core, step)
            for along in range(ROW):
                target[step * ROW + along] = pieces[core, square, row_at(here, along)]


def mlp_kernel(
    inside, middle, sensitivity, gain, shift, enlarge, enlarge_bias, contract, contract_bias,
    output, grad_middle, keep, send, small, wide_small, blocks,
):
    rows, width = middle.shape
    images = rows // SLOTS
    hidden_width = enlarge.shape[1]
    valid = inside[...]
    center = middle[...]
    scaled, inverse = norm_parts(center)
    hidden = (scaled * across(gain) + across(shift)).astype(BF16)
    grad_out = own_share(sensitivity, rows).astype(F32) * valid
    out_low = grad_out.astype(BF16)
    total = jnp.zeros((rows, width), F32)
    grad_hidden = jnp.zeros((rows, width), F32)

    def products(start):
        part = slice(start, start + BLOCK)
        return dot_nn(hidden, enlarge[:, part]), dot_nt(out_low, contract[part, :])

    ahead = products(0)
    for start in range(0, hidden_width, BLOCK):
        part = slice(start, start + BLOCK)
        widened, grad_wide = ahead
        if start + BLOCK < hidden_width:
            ahead = products(start + BLOCK)
        widened = widened + enlarge_bias[part].reshape(1, -1)
        normal_cdf = 0.5 * (1.0 + lax.erf(widened * (1.0 / math.sqrt(2.0))))
        normal_pdf = jnp.exp(-0.5 * widened * widened) * (1.0 / math.sqrt(2.0 * math.pi))
        activated = (widened * normal_cdf).astype(BF16)
        grad_wide = grad_wide * (normal_cdf + widened * normal_pdf)
        wide_small[:, part] = total_rows(grad_wide)
        wide_low = grad_wide.astype(BF16)
        total = total + dot_nn(activated, contract[part, :])
        place_tall(blocks, dot_tn(activated, out_low).astype(BF16), start, 0)
        place_wide(blocks, dot_tn(hidden, wide_low).astype(BF16), start // LANES, PIECE)
        grad_hidden = grad_hidden + dot_nt(wide_low, enlarge[:, part])
    output[...] = ((center + total + across(contract_bias)) * valid).astype(BF16)
    gradient = grad_out + norm_reverse(grad_hidden, scaled, inverse, across(gain))
    grad_middle[...] = gradient
    small[0:1, :] = total_rows(grad_out)
    small[1:2, :] = total_rows(grad_hidden * scaled)
    small[2:3, :] = total_rows(grad_hidden)
    small[3:4, :] = total_rows(gradient)
    hand_out(blocks, keep, send)


def heads_back_kernel(
    grad_middle, qkv, weights, mixing_out, grad_qkv,
):
    rows, width = grad_middle.shape
    images = rows // SLOTS
    head = width // HEADS
    factor = 1.0 / math.sqrt(head)
    grad_context = dot_nt(grad_middle[...].astype(BF16), mixing_out[...]).astype(BF16)
    pair = 2 * head
    lane = head_lanes(pair)
    order = [(image, number) for image in range(images) for number in range(HEADS)]

    def where_of(image, number):
        at = number // 2 * pair
        return slice(image * SLOTS, (image + 1) * SLOTS), at

    def weights_of(image, number):
        place, at = where_of(image, number)
        low, high = number % 2 * head, (number % 2 + 1) * head
        values = qkv[place, 2 * width + at : 2 * width + at + pair]
        own = jnp.where((lane >= low) & (lane < high), values, jnp.zeros_like(values))
        return dot_nt(own, grad_context[place, at : at + pair])

    ahead = weights_of(*order[0])
    parts = []
    for turn, (image, number) in enumerate(order):
        grad_weights = ahead
        if turn + 1 < len(order):
            ahead = weights_of(*order[turn + 1])
        place, at = where_of(image, number)
        low = weights[image * HEADS + number]
        grad_values = dot_nn(low, grad_context[place, at : at + pair])
        soft = low.astype(F32)
        lifted = soft * grad_weights
        scores_low = (lifted - soft * jnp.sum(lifted, axis=0, keepdims=True)).astype(BF16)
        queries = qkv[place, at : at + pair]
        keys = qkv[place, width + at : width + at + pair]
        parts.append(
            (dot_tn(scores_low, keys) * factor, dot_nn(scores_low, queries) * factor, grad_values)
        )
        if number % 2:
            for which in range(3):
                merged = jnp.where(lane < head, parts[0][which], parts[1][which])
                grad_qkv[place, which * width + at : which * width + at + pair] = merged.astype(
                    BF16
                )
            parts = []


def sent_back_kernel(
    sent, grad_middle, grad_qkv, context, projected, active, gain, shift, mixing_in,
    conv_gain, grad_sent, proj_low, keep, send, small, blocks,
):
    rows, width = sent.shape
    gradient = grad_middle[...]
    entering = sent[...].astype(F32)
    scaled, inverse = norm_parts(entering)
    normed = (scaled * across(gain) + across(shift)).astype(BF16)
    lifted = jnp.zeros((rows, width), F32)
    for which in range(3):
        part = slice(which * width, (which + 1) * width)
        piece = grad_qkv[:, part]
        place_wide(blocks, dot_tn(normed, piece).astype(BF16), which * width // LANES, 0)
        lifted = lifted + dot_nt(piece, mixing_in[:, part])
    mixing = dot_tn(context[...], gradient.astype(BF16)).astype(BF16)
    place_wide(blocks, mixing, 3 * width // LANES, 0)
    grad_low = (gradient + norm_reverse(lifted, scaled, inverse, across(gain))).astype(BF16)
    grad_sent[...] = grad_low
    small[0:1, :] = total_rows(lifted * scaled)
    small[1:2, :] = total_rows(lifted)
    incoming = grad_low.astype(F32)
    scaled, inverse = norm_parts(projected[...])
    low = norm_reverse(incoming, scaled, inverse, across(conv_gain)).astype(BF16)
    proj_low[...] = low
    small[2:3, :] = total_rows(incoming * scaled)
    small[3:4, :] = total_rows(incoming)
    for start in range(0, active.shape[1], BLOCK):
        part = slice(start, start + BLOCK)
        place_tall(blocks, dot_tn(active[:, part], low).astype(BF16), start, PIECE)
    hand_out(blocks, keep, send)


def conv_part(
    inside, local_in, proj_low, expanded, slope, enlarge, taps, contract, wide_small, grad_cells,
    blocks, total, first, last, first_row=0,
):
    rows = local_in.shape[0]
    images = rows // SLOTS
    valid = inside[...]
    column = lax.broadcasted_iota(jnp.int32, (SIDE, LANES), 0)
    first_column, last_column = column == 0, column == SIDE - 1

    def cells_of(start):
        part = slice(start, start + BLOCK)
        grad_conv = dot_nt(proj_low, contract[part, :]) * slope[:, part].astype(F32)
        wide_small[9:10, part] = total_rows(grad_conv)
        grad_cells[start // BLOCK % 2] = grad_conv

    cells_of(first)
    for start in range(first, last, BLOCK):
        part = slice(start, start + BLOCK)
        number = start // BLOCK
        if start + BLOCK < last:
            cells_of(start + BLOCK)
        pieces = []
        for lanes in range(0, BLOCK, LANES):
            chans = slice(start + lanes, start + lanes + LANES)
            kernel = [taps[tap : tap + 1, chans] for tap in range(9)]
            sums = [jnp.zeros((SIDE, LANES), F32) for _ in range(9)]
            outcome = []
            for image in range(images):
                base = image * SLOTS
                shifted = {}
                for line in range(SIDE):
                    for ahead in (line, line + 1):
                        if ahead < SIDE and ahead not in shifted:
                            row = grad_cells[
                                number % 2,
                                base + ahead * SIDE : base + (ahead + 1) * SIDE,
                                lanes : lanes + LANES,
                            ]
                            before, after = column_shifts(row, first_column, last_column)
                            shifted[ahead] = (after, row, before)
                    place = slice(base + line * SIDE, base + (line + 1) * SIDE)
                    cells = expanded[place, chans].astype(F32)
                    grid = jnp.zeros((SIDE, LANES), F32)
                    for a in range(3):
                        if 0 <= line + 1 - a < SIDE:
                            for b in range(3):
                                moved = shifted[line + 1 - a][b]
                                sums[3 * a + b] = sums[3 * a + b] + cells * moved
                                grid = grid + moved * kernel[3 * a + b]
                    outcome.append(grid)
            for tap in range(9):
                wide_small[tap : tap + 1, chans] = total_rows(sums[tap])
            pieces.append(jnp.concatenate(outcome, axis=0) * valid)
        grad_expanded = jnp.concatenate(pieces, axis=1)
        wide_small[10:11, part] = total_rows(grad_expanded)
        expanded_low = grad_expanded.astype(BF16)
        place_wide(
            blocks, dot_tn(local_in, expanded_low).astype(BF16), start // LANES, 0, first_row
        )
        total = total + dot_nt(expanded_low, enlarge[:, part])
    return total


def conv_back_kernel(
    inside, tokens, grad_sent, proj_low, expanded, slope, enlarge, taps, contract,
    total, early, early_wide, grad_cells,
):
    rows, width = grad_sent.shape
    total[...] = conv_part(
        inside, own_share(tokens, rows), proj_low[...], expanded, slope, enlarge, taps,
        contract, early_wide, grad_cells, early, grad_sent[...].astype(F32), 0,
        enlarge.shape[1] // 2,
    )


def small_rows(small, wide):
    mlp, sent = small
    mlp_wide, conv_wide = wide
    found = []
    for source, rows in ((mlp, 4), (sent, 4), (mlp_wide, 1), (conv_wide, 11)):
        for row in range(rows):
            for at in range(0, source.shape[1], LANES):
                found.append((source, row, at))
    return found


def conv_end_kernel(
    inside, tokens, total, proj_low, expanded, slope, enlarge, taps, contract, early, early_wide,
    mlp_small, sent_small, mlp_wide, grad_in, keep, send, pieces, conv_wide, grad_cells, short,
):
    rows, width = total.shape
    channels = enlarge.shape[1]
    half = channels // 2
    conv_wide[:, 0:half] = early_wide[:, 0:half]
    pieces[:, :, 0 : ROW // 2, 0:PIECE, :] = early[...]
    grad_in[...] = conv_part(
        inside, own_share(tokens, rows), proj_low[...], expanded, slope, enlarge, taps,
        contract, conv_wide, grad_cells, pieces, total[...], half, channels,
    ).astype(BF16)
    short[...] = jnp.zeros_like(short)
    places = small_rows((mlp_small, sent_small), (mlp_wide, conv_wide))
    for number, (source, row, at) in enumerate(places):
        piece, inside = number // 8, number % 8
        short[piece, inside : inside + 1, :] = source[row : row + 1, at : at + LANES]
    for piece in range(2 * SQUARE * ROW):
        value = short[piece]
        high = value.astype(BF16).astype(F32)
        pair = jnp.concatenate([high, value - high], axis=0).astype(BF16)
        core, square, row = piece // (SQUARE * ROW), piece // ROW % SQUARE, piece % ROW
        pieces[core, square, row, PIECE : PIECE + 16, :] = pair
    hand_out(pieces, keep, send)


def summed(parts, short):
    total = parts[0].astype(F32)
    for part in parts[1:]:
        total = total + part.astype(F32)
    if not short:
        return total.astype(BF16)
    main = total.shape[0] - short
    value = total[main : main + 8] + total[main + 8 : main + 16]
    high = value.astype(BF16).astype(F32)
    return jnp.concatenate([total[:main], high, value - high], axis=0).astype(BF16)


def add_kernel(short, count, *refs):
    parts, outs = refs[:count], refs[count:]
    at = 0
    for out in outs:
        for step in range(out.shape[0]):
            out[step] = summed([part[at + step] for part in parts], short)
        at += out.shape[0]


def join_kernel(short, own, arrived, out):
    half = own.shape[0]
    out[0:half] = own[...]
    out[half:] = arrived[...]


def pieces_of(parts):
    half = len(parts) // 2
    here = Here()
    for side in range(2):
        core = here.core if side == 0 else 1 - here.core
        step = 0
        for part in parts[side * half : (side + 1) * half]:
            for inside in range(part.shape[0]):
                square = square_at(here, core, step // ROW)
                yield core * SQUARE + square, row_at(here, step % ROW), part, inside
                step += 1


class Leaving:
    def __init__(self, stage, semaphores):
        self.stage, self.semaphores, self.copies = stage, semaphores, []

    def put(self, part, step, offset):
        slot = len(self.copies)
        for lane in range(ACROSS):
            low = offset + lane * HEIGHT
            self.stage[slot, :, lane * LANES : (lane + 1) * LANES] = part[
                step, low : low + HEIGHT, :
            ].astype(F32)
        return self.stage.at[slot], self.semaphores.at[slot]

    def tall(self, target, block, row, part, step, offset):
        source, semaphore = self.put(part, step, offset)
        at = pl.multiple_of((block * ROW + row) * HEIGHT, 16)
        self.copies.append(
            pltpu.make_async_copy(source, target.at[pl.ds(at, HEIGHT)], semaphore)
        )
        self.copies[-1].start()

    def wide(self, targets, block, row, part, step, offset):
        source, semaphore = self.put(part, step, offset)
        at = pl.multiple_of(block * HEIGHT, 16)
        span = ACROSS * LANES
        if len(targets) == 1:
            lanes = pl.ds(pl.multiple_of(row * span, LANES), span)
            self.copies.append(
                pltpu.make_async_copy(source, targets[0].at[pl.ds(at, HEIGHT), lanes], semaphore)
            )
            self.copies[-1].start()
            return
        last = pltpu.make_async_copy(source, targets[1].at[pl.ds(at, HEIGHT)], semaphore)
        self.copies.append(last)
        lanes = pl.ds(pl.multiple_of(jnp.minimum(row, ROW - 2) * span, LANES), span)
        others = pltpu.make_async_copy(source, targets[0].at[pl.ds(at, HEIGHT), lanes], semaphore)
        pl.when(row == ROW - 1)(last.start)
        pl.when(row < ROW - 1)(others.start)

    def wait(self):
        for copy in self.copies:
            copy.wait()


def mlp_end_kernel(*refs):
    (narrower, widener, stage, semaphores), parts = refs[-4:], refs[:-4]
    leaving = Leaving(stage, semaphores)
    for block, row, part, step in pieces_of(parts):
        leaving.tall(narrower, block, row, part, step, 0)
        leaving.wide((widener,), block, row, part, step, PIECE)
    leaving.wait()


def sent_end_kernel(*refs):
    (attention, mixing, projector, stage, semaphores), parts = refs[-5:], refs[:-5]
    leaving = Leaving(stage, semaphores)
    for block, row, part, step in pieces_of(parts):
        leaving.wide((attention, mixing), block, row, part, step, 0)
        leaving.tall(projector, block, row, part, step, PIECE)
    leaving.wait()


def conv_all_kernel(*refs):
    (*shorts, short, stage, semaphores), (expander, *parts) = refs[-15:], refs[-16:-15] + refs[:-16]
    leaving = Leaving(stage, semaphores)
    for block, row, part, step in pieces_of(parts):
        leaving.wide((expander,), block, row, part, step, 0)
        pair = part[step, PIECE : PIECE + 16, :].astype(F32)
        short[pl.ds(pl.multiple_of((block * ROW + row) * 8, 8), 8), :] = pair[0:8] + pair[8:16]
    (upshift, depthwise, depthshift, postgain, postshift, pregain, preshift, mixshift, midgain,
     midshift, wideshift, narrowshift) = shorts
    lanes = narrowshift.shape[0] // LANES
    wide_lanes = upshift.shape[0] // LANES
    number = 0
    for target in (narrowshift, midgain, midshift, mixshift, pregain, preshift, postgain, postshift):
        for lane in range(lanes):
            target[lane * LANES : (lane + 1) * LANES] = short[number, :]
            number += 1
    for target in (wideshift,) + (depthwise,) * 9 + (depthshift, upshift):
        for lane in range(wide_lanes):
            value = short[number : number + 1, :]
            if target is depthwise:
                tap = number // wide_lanes - 3
                target[tap : tap + 1, lane * LANES : (lane + 1) * LANES] = value
            else:
                target[lane * LANES : (lane + 1) * LANES] = value.reshape(LANES)
            number += 1
    leaving.wait()


def give_kernel(output, grad_in, own, give):
    first = Here().section == 0
    own[...] = jnp.where(first, grad_in[...], output[...])
    give[...] = jnp.where(first, output[...], grad_in[...])


def ends_kernel(filled, own, arrived, ends, means, semaphores):
    share = ends.shape[0] // 2
    local, slots, width = ends.shape[1:]
    first = Here().section
    copies = []
    for source, section in ((own, first), (arrived, 1 - first)):
        for number in range(share * local):
            copies.append(
                pltpu.make_async_copy(
                    source.at[pl.ds(number * slots, slots)],
                    ends.at[section * share + number // local, number % local],
                    semaphores.at[len(copies)],
                )
            )
            copies[-1].start()
    for source, section in ((own, first), (arrived, 1 - first)):
        for number in range(share * local):
            value = source[number * slots : (number + 1) * slots, :].astype(F32)
            square = jnp.sum(value * value, axis=0, keepdims=True)
            image = (section * share + number // local) * local + number % local
            mean = jnp.sum(square, axis=1, keepdims=True) / filled[pl.ds(image, 1), 0:1]
            means[image, :, :] = jnp.broadcast_to(jnp.sqrt(mean), (1, LANES))
    for copy in copies:
        copy.wait()


WHOLE = pl.BlockSpec(memory_space=pltpu.VMEM)
ANYWHERE = pl.BlockSpec(memory_space=pl.ANY)
REMOTE = pl.BlockSpec(memory_space=pltpu.HBM)
SCALARS = pl.BlockSpec(memory_space=pltpu.SMEM)
COST = 30
COSTS = {'conv_first': 0, 'conv_second': 30, 'conv_far': 0, 'conv_join_square': 0, 'give': 0, 'mlp_cores': 30, 'conv_cores': 30, 'conv_all': 0, 'inner_cores': 30, 'conv_total': 0, 'inner_join_square': 30, 'mlp_end': 0, 'mlp_far': 0}
BOTH = ("section", "dp")


def shape(dims, kind):
    return jax.ShapeDtypeStruct(dims, kind)


class Calls:
    def __init__(self):
        self.last = None

    def __call__(self, kernel, name, ins, outs, scratch=(), mb=8, us=0, smem=(), hbm=(), hbm_outs=()):
        count = len(ins)
        after = () if self.last is None else (self.last,)


        def body(*refs):
            token = refs[count + len(after)]
            token[...] = jnp.zeros_like(token)
            kernel(*refs[:count], *refs[count + len(after) + 1 :])

        ins = [
            pltpu.with_memory_space_constraint(value, pltpu.HBM) if place in hbm else value
            for place, value in enumerate(ins)
        ]
        outs = [
            pltpu.HBM(out.shape, out.dtype) if place in hbm_outs else out
            for place, out in enumerate(outs)
        ]
        self.last, *result = pl.pallas_call(
            body,
            out_shape=[shape((8, LANES), F32)] + outs,
            in_specs=[
                SCALARS if place in smem else REMOTE if place in hbm else WHOLE
                for place in range(count)
            ]
            + [ANYWHERE] * len(after),
            out_specs=[WHOLE]
            + [REMOTE if place in hbm_outs else WHOLE for place in range(len(outs))],
            scratch_shapes=list(scratch),
            cost_estimate=pl.CostEstimate(
                flops=1 + int(COSTS.get(name, us) * 1e9), bytes_accessed=1, transcendentals=0
            ),
            compiler_params=pltpu.CompilerParams(vmem_limit_bytes=mb * 1024 * 1024),
            name=name,
        )(*ins, *after)
        return result


    def fence(self, value, name):
        def body(after, value, token, out):
            token[...] = jnp.zeros_like(token)

        self.last, value = pl.pallas_call(
            body,
            out_shape=[shape((8, LANES), F32), shape(value.shape, value.dtype)],
            in_specs=[ANYWHERE] * 2,
            out_specs=[WHOLE, ANYWHERE],
            input_output_aliases={1: 1},
            cost_estimate=pl.CostEstimate(
                flops=1 + int(COSTS.get(name, 0) * 1e9), bytes_accessed=1, transcendentals=0
            ),
            compiler_params=pltpu.CompilerParams(vmem_limit_bytes=1024 * 1024),
            name=name,
        )(self.last, value)
        return value


def swapped(value, digit, step=0):
    sections, members = (lax.axis_size(axis) for axis in BOTH)
    pairs = []
    for section in range(sections):
        for member in range(members):
            if digit == "first" or digit == "second":
                across = 2 if digit == "first" else 1
            else:
                across = step if digit == "square" else 0
            if member % 2:
                across = SWAPPED[across]
            along = {"near": 4}.get(digit, digit if isinstance(digit, int) else 0)
            other = (section ^ across // 2) * members + (member ^ (across % 2 * 2 + along))
            pairs.append((section * members + member, other))
    return lax.ppermute(value, BOTH, pairs)


class Group:
    def __init__(self, name, calls, keep, send, short=0, cost=COST):
        self.name, self.calls, self.short, self.cost = name, calls, short, cost
        self.rows = keep.shape[1]
        self.parts = [keep, swapped(send, 1)]

    def call(self, kernel, what, ins, outs):
        return self.calls(
            functools.partial(kernel, self.short), f"{self.name}_{what}", ins,
            [shape((count, self.rows, LANES), BF16) for count in outs], us=self.cost,
        )

    def add(self, what, outs=1):
        pieces = [self.parts[0].shape[0] // outs] * outs
        kernel = lambda short, *refs: add_kernel(short, len(self.parts), *refs)
        return self.call(kernel, what, self.parts, pieces)

    def halve(self, what):
        keep, send = self.add(what, 2)
        self.parts = [keep, swapped(send, what)]

    def first(self):
        self.halve("first")

    def second(self):
        self.halve("second")

    def square(self):
        keep, *send = self.add("square", SQUARE)
        self.parts = [keep] + [swapped(part, "square", 1 + at) for at, part in enumerate(send)]

    def near(self):
        self.halve("near")

    def far(self):
        stride, what = 4, "far"
        while stride < lax.axis_size("dp") // 2:
            stride *= 2
            (own,) = self.add(what)
            self.parts, what = [own, swapped(own, stride)], f"over_{stride}"

    def total(self):
        (own,) = self.add("total")
        self.parts = [own, swapped(own, "near")]

    def join(self, what):
        (own,) = self.call(join_kernel, what, self.parts, [2 * self.parts[0].shape[0]])
        return own

    def join_row(self):
        own = self.join("join_row")
        self.parts = [own, swapped(own, "second")]

    def join_square(self):
        own = self.join("join_square")
        self.parts = [own, swapped(own, "first")]
        self.near_half = swapped(own, 1)

    def join_cores(self):
        far_half = self.calls.fence(self.parts[1], f"{self.name}_cores")
        self.blocks = [self.parts[0], far_half, self.near_half, swapped(far_half, 1)]

    def join_all(self):
        own = self.join("join_row")
        self.parts = [own] + [swapped(own, "square", step) for step in range(1, SQUARE)]
        self.blocks = self.parts + [swapped(part, 1) for part in self.parts]


def shards(
    entering_tokens,
    output_sensitivity,
    picture_tile_extents,
    pointwise_enlarge,
    enlarge_bias,
    channelwise_kernel,
    channelwise_conv_bias,
    pointwise_contract,
    convblock_scale,
    convblock_offset,
    attend_scale,
    attend_offset,
    query_key_proj,
    heads_output_proj,
    heads_output_bias,
    feedforward_scale,
    feedforward_offset,
    feedforward_enlarge,
    feedforward_enlarge_bias,
    feedforward_contract,
    contract_bias,
):
    micro_count, local_images, slots, width = entering_tokens.shape
    channels = pointwise_enlarge.shape[1]
    share = micro_count // 2
    images = share * local_images
    rows = images * slots
    call = Calls()
    extents = jnp.transpose(picture_tile_extents, (1, 2, 0))
    sent, expanded, slope, active, projected, inside, filled = call(
        conv_ahead_kernel, "conv_ahead",
        (extents, entering_tokens, pointwise_enlarge, enlarge_bias, channelwise_kernel,
         channelwise_conv_bias, pointwise_contract, convblock_scale, convblock_offset),
        [shape((rows, width), BF16), shape((rows, channels), BF16), shape((rows, channels), BF16),
         shape((rows, channels), BF16), shape((rows, width), F32), shape((rows, 1), F32),
         shape((micro_count * local_images, LANES), F32)],
        [pltpu.VMEM((2, rows, BLOCK), F32), pltpu.VMEM((share, local_images, slots, width), BF16)]
        + [pltpu.VMEM(value.shape, value.dtype) for value in
           (pointwise_enlarge, enlarge_bias, channelwise_kernel, channelwise_conv_bias,
            pointwise_contract, convblock_scale, convblock_offset)]
        + [pltpu.SemaphoreType.DMA((6 + 2 * channels // BLOCK,))],
        mb=20, smem=(0,), hbm=range(1, 9),
    )
    qkv, weights, context, middle = call(
        attend_ahead_kernel, "attend_ahead",
        (inside, sent, attend_scale, attend_offset, query_key_proj, heads_output_proj,
         heads_output_bias),
        [shape((rows, 3 * width), BF16), shape((images * HEADS, slots, slots), BF16),
         shape((rows, width), BF16), shape((rows, width), F32)], mb=16,
    )
    halves = [shape((SQUARE * ROW, 2 * PIECE, LANES), BF16)] * 2
    whole = [pltpu.VMEM((2, SQUARE, ROW, 2 * PIECE, LANES), BF16)]
    output, grad_middle, keep, send, mlp_small, mlp_wide = call(
        mlp_kernel, "mlp",
        (inside, middle, output_sensitivity, feedforward_scale, feedforward_offset, feedforward_enlarge,
         feedforward_enlarge_bias, feedforward_contract, contract_bias),
        [shape((rows, width), BF16), shape((rows, width), F32)] + halves
        + [shape((8, width), F32), shape((1, channels), F32)],
        whole, mb=24,
    )
    mlp = Group("mlp", call, keep, send)
    (grad_qkv,) = call(
        heads_back_kernel, "heads_back", (grad_middle, qkv, weights, heads_output_proj),
        [shape((rows, 3 * width), BF16)], mb=16,
    )
    mlp.first()
    grad_sent, proj_low, keep, send, sent_small = call(
        sent_back_kernel, "sent_back",
        (sent, grad_middle, grad_qkv, context, projected, active, attend_scale, attend_offset,
         query_key_proj, convblock_scale),
        [shape((rows, width), BF16), shape((rows, width), BF16)] + halves
        + [shape((8, width), F32)],
        whole, mb=24,
    )
    inner = Group("inner", call, keep, send)
    early_pieces = shape((2, SQUARE, ROW // 2, PIECE, LANES), BF16)
    total, early, early_wide = call(
        conv_back_kernel, "conv_back",
        (inside, entering_tokens, grad_sent, proj_low, expanded, slope, pointwise_enlarge,
         channelwise_kernel, pointwise_contract),
        [shape((rows, width), F32), early_pieces, shape((16, channels), F32)],
        [pltpu.VMEM((2, rows, BLOCK), F32)], mb=20,
    )
    mlp.second()
    inner.first()
    halves = [shape((SQUARE * ROW, PIECE + 16, LANES), BF16)] * 2
    grad_in, keep, send = call(
        conv_end_kernel, "conv_end",
        (inside, entering_tokens, total, proj_low, expanded, slope, pointwise_enlarge, channelwise_kernel,
         pointwise_contract, early, early_wide, mlp_small, sent_small, mlp_wide),
        [shape((rows, width), BF16)] + halves,
        [pltpu.VMEM((2, SQUARE, ROW, PIECE + 16, LANES), BF16), pltpu.VMEM((16, channels), F32),
         pltpu.VMEM((2, rows, BLOCK), F32), pltpu.VMEM((2 * SQUARE * ROW, 8, LANES), F32)],
        mb=20,
    )
    conv = Group("conv", call, keep, send, 16)
    line, wide_line = shape((width,), F32), shape((channels,), F32)
    tall, wide = shape((channels, width), F32), shape((width, channels), F32)
    pieces = 2 * SQUARE * ROW

    def leaving(count):
        return [pltpu.VMEM((count, HEIGHT, ACROSS * LANES), F32), pltpu.SemaphoreType.DMA((count,))]

    mlp.near()
    conv.first()
    inner.second()
    mlp.far()
    conv.second()
    own, give = call(
        give_kernel, "give", (output, grad_in), [shape((rows, width), BF16)] * 2, us=COST
    )
    arrived = lax.ppermute(give, "section", [(0, 1), (1, 0)])
    inner.near()
    conv.near()
    mlp.total()
    inner.far()
    conv.far()
    mlp.join_row()
    ends, means = call(
        ends_kernel, "ends", (filled, own, arrived),
        [shape(entering_tokens.shape, BF16), shape((micro_count * local_images, 1, LANES), F32)],
        [pltpu.SemaphoreType.DMA((micro_count * local_images,))], hbm_outs=(0,), us=COST,
    )
    inner.total()
    mlp.join_square()
    conv.total()
    inner.join_row()
    conv.join_row()
    mlp.join_cores()
    conv.join_square()
    inner.join_square()
    narrower, widener = call(
        mlp_end_kernel, "mlp_end", mlp.blocks, [tall, wide], leaving(2 * pieces), mb=12,
        hbm_outs=(0, 1), us=COST,
    )
    inner.join_cores()
    conv.join_cores()
    attention, mixing, projector = call(
        sent_end_kernel, "sent_end", inner.blocks,
        [shape((width, 3 * width), F32), shape((width, width), F32), tall],
        leaving(2 * pieces), mb=12, hbm_outs=(0, 1, 2), us=COST,
    )
    (expander, upshift, depthwise, depthshift, postgain, postshift, pregain, preshift, mixshift,
     midgain, midshift, wideshift, narrowshift) = call(
        conv_all_kernel, "conv_all", conv.blocks,
        [wide, wide_line, shape((9, channels), F32), wide_line] + [line] * 7 + [wide_line, line],
        [pltpu.VMEM((pieces * 8, LANES), F32)] + leaving(pieces), hbm_outs=(0,), us=COST,
    )
    means = means[:, 0, 0].reshape(1, micro_count, local_images)
    return (
        ends[None], means, expander, upshift, depthwise, depthshift, projector, postgain,
        postshift, pregain, preshift, attention, mixing, mixshift, midgain, midshift, widener,
        wideshift, narrower, narrowshift,
    )


def solution(mesh):
    tokens = P(None, "dp", None, None)
    placed = (tokens, tokens, P(None, "dp", None)) + (P(),) * 18
    return jax.shard_map(
        shards,
        mesh=mesh,
        in_specs=placed,
        out_specs=(P("section", None, "dp", None, None), P("section", None, "dp")) + (P(),) * 18,
        check_vma=False,
    )
```

```python
import functools
import math

import jax
import jax.numpy as jnp
from jax import lax
from jax.experimental import pallas as pl
from jax.experimental.pallas import tpu as pltpu
from jax.sharding import PartitionSpec as P

HEADS = 6
SIDE = 16
SLOTS = SIDE * SIDE
EPSILON = 1e-05
BLOCKED = -1000000000.0
LANES = 128
BLOCK = 512
WIDE = 768
SQUARE = 4
ROW = 4
PIECE = 144
HEIGHT = 48
ACROSS = PIECE // HEIGHT
SWAPPED = (0, 2, 1, 3)
BF16 = jnp.bfloat16
F32 = jnp.float32


def dot_nn(left, right):
    return jnp.dot(left, right, preferred_element_type=F32)


def dot_nt(left, right):
    return lax.dot_general(left, right, (((1,), (1,)), ((), ())), preferred_element_type=F32)


def dot_tn(left, right):
    return lax.dot_general(left, right, (((0,), (0,)), ((), ())), preferred_element_type=F32)


def norm_parts(values):
    centered = values - jnp.mean(values, axis=-1, keepdims=True)
    inverse = lax.rsqrt(jnp.mean(centered * centered, axis=-1, keepdims=True) + EPSILON)
    return centered * inverse, inverse


def norm_reverse(upstream, scaled, inverse, gain):
    lifted = upstream * gain
    return inverse * (
        lifted
        - jnp.mean(lifted, axis=-1, keepdims=True)
        - scaled * jnp.mean(lifted * scaled, axis=-1, keepdims=True)
    )


def across(vector):
    return vector[...].reshape(1, -1)


def own_share(tokens, rows):
    share = rows // (tokens.shape[1] * tokens.shape[2])
    return tokens[pl.ds(Here().section * share, share)].reshape(rows, tokens.shape[3])


def total_rows(values):
    return jnp.sum(values, axis=0, keepdims=True)


class Here:
    def __init__(self):
        member = lax.axis_index("dp")
        self.section = lax.axis_index("section")
        self.core = member % 2
        self.square = self.section * 2 + member // 2 % 2
        self.row = member // 4 % ROW


def own_share(tokens, rows):
    share = rows // (tokens.shape[1] * tokens.shape[2])
    return tokens[pl.ds(Here().section * share, share)].reshape(rows, tokens.shape[3])


def total_rows(values):
    return jnp.sum(values, axis=0, keepdims=True)


def own_share(tokens, rows):
    share = rows // (tokens.shape[1] * tokens.shape[2])
    return tokens[pl.ds(Here().section * share, share)].reshape(rows, tokens.shape[3])


def total_rows(values):
    return jnp.sum(values, axis=0, keepdims=True)


class Here:
    def __init__(self):
        member = lax.axis_index("dp")
        self.section = lax.axis_index("section")
        self.core = member % 2
        self.square = self.section * 2 + member // 2 % 2
        self.row = member // 4 % ROW


def own_share(tokens, rows):
    share = rows // (tokens.shape[1] * tokens.shape[2])
    return tokens[pl.ds(Here().section * share, share)].reshape(rows, tokens.shape[3])


def total_rows(values):
    return jnp.sum(values, axis=0, keepdims=True)


def column_shifts(row, first_column, last_column):
    before = jnp.where(first_column, 0.0, pltpu.roll(row, 1, 0))
    after = jnp.where(last_column, 0.0, pltpu.roll(row, SIDE - 1, 0))
    return before, after


def conv_ahead_kernel(
    extents_from, tokens, enlarge_from, enlarge_bias_from, taps_from, taps_bias_from, contract_from,
    gain_from, shift_from, sent, expanded, slope, active, projected, inside, filled,
    grid_cells, entering, enlarge, enlarge_bias, taps, taps_bias, contract, gain, shift, extents, arrivals,
):
    rows, width = sent.shape
    images = rows // SLOTS
    channels = enlarge.shape[1]
    share = entering.shape[0]
    starts = range(0, channels, BLOCK)
    section = Here().section
    copies = [(extents_from, extents)]
    copies += [
        (tokens.at[section * share + number // 2, :, half], entering.at[number // 2, :, half])
        for number in range(2 * share)
        for half in (pl.ds(number % 2 * (SLOTS // 2), SLOTS // 2),)
    ]
    copies += [(enlarge_from.at[:, pl.ds(0, BLOCK)], enlarge.at[:, pl.ds(0, BLOCK)])]
    copies += [
        (enlarge_bias_from, enlarge_bias), (taps_from, taps), (taps_bias_from, taps_bias),
        (gain_from, gain), (shift_from, shift),
    ]
    early = len(copies)
    for start in starts:
        part = pl.ds(start, BLOCK)
        if start:
            copies.append((enlarge_from.at[:, part], enlarge.at[:, part]))
        copies.append((contract_from.at[part], contract.at[part]))
    copies = [
        pltpu.make_async_copy(source, target, arrivals.at[number])
        for number, (source, target) in enumerate(copies)
    ]
    for copy in copies:
        copy.start()
    copies[0].wait()
    micros, local = extents.shape[2], extents.shape[0]
    for image in range(micros * local):
        count = extents[image % local, 0, image // local] * extents[image % local, 1, image // local]
        filled[image : image + 1, :] = jnp.full((1, LANES), (count * width).astype(F32))
    slot = lax.broadcasted_iota(jnp.int32, (SLOTS, 1), 0)
    for image in range(images):
        height, across_it = (
            extents[image % local, side, section * share + image // local] for side in range(2)
        )
        held = (slot // SIDE < height) & (slot % SIDE < across_it)
        inside[image * SLOTS : (image + 1) * SLOTS, :] = held.astype(F32)
    for copy in copies[1:early]:
        copy.wait()
    later = copies[early:]
    local_in = entering[...].reshape(rows, width)
    valid = inside[...]
    column = lax.broadcasted_iota(jnp.int32, (SIDE, LANES), 0)
    first_column, last_column = column == 0, column == SIDE - 1
    total = jnp.zeros((rows, width), F32)

    def cells_of(start):
        part = slice(start, start + BLOCK)
        if start:
            later[2 * (start // BLOCK) - 1].wait()
        cells = (dot_nn(local_in, enlarge[:, part]) + enlarge_bias[part].reshape(1, -1)) * valid
        grid_cells[start // BLOCK % 2] = cells
        expanded[:, part] = cells.astype(BF16)

    cells_of(0)
    for start in starts:
        part = slice(start, start + BLOCK)
        number = start // BLOCK
        if start + BLOCK < channels:
            cells_of(start + BLOCK)
        for left in range(0, BLOCK, LANES):
            inner = slice(start + left, start + left + LANES)
            kernel = [taps[tap : tap + 1, inner] for tap in range(9)]
            bias = taps_bias[inner].reshape(1, -1)
            for image in range(images):
                base = image * SLOTS
                above = here = None
                for line in range(SIDE + 1):
                    if line < SIDE:
                        row = grid_cells[
                            number % 2,
                            base + line * SIDE : base + (line + 1) * SIDE,
                            left : left + LANES,
                        ]
                        before, after = column_shifts(row, first_column, last_column)
                        sums = [
                            before * kernel[3 * a]
                            + row * kernel[3 * a + 1]
                            + after * kernel[3 * a + 2]
                            for a in range(3)
                        ]
                    if line > 0:
                        convolved = above + sums[2] if line < SIDE else above
                        gate = jax.nn.sigmoid(convolved)
                        lit = convolved * gate
                        place = slice(base + (line - 1) * SIDE, base + line * SIDE)
                        active[place, inner] = lit.astype(BF16)
                        slope[place, inner] = (gate + lit * (1.0 - gate)).astype(BF16)
                    if line < SIDE:
                        above = (here if line > 0 else bias) + sums[1]
                        here = bias + sums[0]
        later[2 * number].wait()
        total = total + dot_nn(active[:, part], contract[part, :])
    projected[...] = total
    scaled, _ = norm_parts(total)
    sent[...] = (local_in.astype(F32) + scaled * across(gain) + across(shift)).astype(BF16)


def head_lanes(width):
    return lax.broadcasted_iota(jnp.int32, (1, width), 1)


def attend_ahead_kernel(
    inside, sent, gain, shift, mixing_in, mixing_out, mixing_bias,
    qkv, weights, context, middle,
):
    rows, width = sent.shape
    images = rows // SLOTS
    head = width // HEADS
    factor = 1.0 / math.sqrt(head)
    entering = sent[...].astype(F32)
    scaled, _ = norm_parts(entering)
    normed = (scaled * across(gain) + across(shift)).astype(BF16)
    for start in range(0, 3 * width, width):
        part = slice(start, start + width)
        qkv[:, part] = dot_nn(normed, mixing_in[:, part]).astype(BF16)
    pair = 2 * head
    lane = head_lanes(pair)
    valid = [inside[image * SLOTS : (image + 1) * SLOTS, :] > 0.5 for image in range(images)]
    order = [(image, number) for image in range(images) for number in range(HEADS)]

    def where_of(image, number):
        at = number // 2 * pair
        return slice(image * SLOTS, (image + 1) * SLOTS), at

    def scores_of(image, number):
        place, at = where_of(image, number)
        low, high = number % 2 * head, (number % 2 + 1) * head
        keys = qkv[place, width + at : width + at + pair]
        own = jnp.where((lane >= low) & (lane < high), keys, jnp.zeros_like(keys))
        return dot_nt(own, qkv[place, at : at + pair])

    ahead = scores_of(*order[0])
    gathered = []
    for turn, (image, number) in enumerate(order):
        scores = ahead
        if turn + 1 < len(order):
            ahead = scores_of(*order[turn + 1])
        scores = jnp.where(valid[image], scores * factor, BLOCKED)
        powers = jnp.exp(scores - jnp.max(scores, axis=0, keepdims=True))
        low = (powers * (1.0 / jnp.sum(powers, axis=0, keepdims=True))).astype(BF16)
        weights[image * HEADS + number] = low
        place, at = where_of(image, number)
        gathered.append(dot_tn(low, qkv[place, 2 * width + at : 2 * width + at + pair]))
        if number % 2:
            context[place, at : at + pair] = jnp.where(lane < head, *gathered).astype(BF16)
            gathered = []
    middle[...] = entering + dot_nn(context[...], mixing_out[...]) + across(mixing_bias)


def place_tall(pieces, grad, first_row, offset):
    for low in range(first_row, first_row + grad.shape[0], 16):
        piece, inside = low // HEIGHT, low % HEIGHT
        core, square, row = piece // (SQUARE * ROW), piece // ROW % SQUARE, piece % ROW
        for lane in range(ACROSS):
            at = offset + lane * HEIGHT + inside
            pieces[core, square, row, at : at + 16, :] = grad[
                low - first_row : low - first_row + 16, lane * LANES : (lane + 1) * LANES
            ]


def place_wide(pieces, grad, first_lane, offset, first_row=0):
    for block in range(grad.shape[0] // HEIGHT):
        for lane in range(grad.shape[1] // LANES):
            row, inside = (first_lane + lane) // ACROSS, (first_lane + lane) % ACROSS
            at = offset + inside * HEIGHT
            pieces[block // SQUARE, block % SQUARE, row - first_row, at : at + HEIGHT, :] = grad[
                block * HEIGHT : (block + 1) * HEIGHT, lane * LANES : (lane + 1) * LANES
            ]


def square_at(here, core, step):
    return here.square ^ jnp.where(core == 0, step, SWAPPED[step])


def row_at(here, step):
    return step % 2 * 2 + (here.row % 2 ^ step // 2)


def mlp_kernel(
    inside, middle, sensitivity, gain, shift, enlarge, enlarge_bias, contract,
    lit, grad_middle, blocks, send, small, wide_small,
):
    rows, width = middle.shape
    images = rows // SLOTS
    hidden_width = enlarge.shape[1]
    valid = inside[...]
    center = middle[...]
    scaled, inverse = norm_parts(center)
    hidden = (scaled * across(gain) + across(shift)).astype(BF16)
    grad_out = own_share(sensitivity, rows).astype(F32) * valid
    out_low = grad_out.astype(BF16)
    grad_hidden = jnp.zeros((rows, width), F32)
    out_turned, hidden_turned = out_low.T, hidden.T

    def products(start):
        part = slice(start, start + WIDE)
        return dot_nn(hidden, enlarge[:, part]), dot_nt(out_low, contract[part, :])

    ahead = products(0)
    for start in range(0, hidden_width, WIDE):
        part = slice(start, start + WIDE)
        widened, grad_wide = ahead
        if start + WIDE < hidden_width:
            ahead = products(start + WIDE)
        widened = widened + enlarge_bias[part].reshape(1, -1)
        normal_cdf = 0.5 * (1.0 + lax.erf(widened * (1.0 / math.sqrt(2.0))))
        normal_pdf = jnp.exp(-0.5 * widened * widened) * (1.0 / math.sqrt(2.0 * math.pi))
        activated = (widened * normal_cdf).astype(BF16)
        lit[:, part] = activated
        grad_wide = grad_wide * (normal_cdf + widened * normal_pdf)
        wide_small[:, part] = total_rows(grad_wide)
        wide_low = grad_wide.astype(BF16)
        place_tall(blocks, dot_nn(out_turned, activated).astype(BF16).T, start, 0)
        place_wide(blocks, dot_nn(hidden_turned, wide_low).astype(BF16), start // LANES, PIECE)
        grad_hidden = grad_hidden + dot_nt(wide_low, enlarge[:, part])
    gradient = grad_out + norm_reverse(grad_hidden, scaled, inverse, across(gain))
    grad_middle[...] = gradient
    small[0:1, :] = total_rows(grad_out)
    small[1:2, :] = total_rows(grad_hidden * scaled)
    small[2:3, :] = total_rows(grad_hidden)
    small[3:4, :] = total_rows(gradient)
    send[...] = blocks[1 - Here().core]


def heads_back_kernel(
    grad_middle, qkv, weights, mixing_out, grad_qkv,
):
    rows, width = grad_middle.shape
    images = rows // SLOTS
    head = width // HEADS
    factor = 1.0 / math.sqrt(head)
    grad_context = dot_nt(grad_middle[...].astype(BF16), mixing_out[...]).astype(BF16)
    pair = 2 * head
    lane = head_lanes(pair)
    order = [(image, number) for image in range(images) for number in range(HEADS)]

    def where_of(image, number):
        at = number // 2 * pair
        return slice(image * SLOTS, (image + 1) * SLOTS), at

    def weights_of(image, number):
        place, at = where_of(image, number)
        low, high = number % 2 * head, (number % 2 + 1) * head
        values = qkv[place, 2 * width + at : 2 * width + at + pair]
        own = jnp.where((lane >= low) & (lane < high), values, jnp.zeros_like(values))
        return dot_nt(own, grad_context[place, at : at + pair])

    ahead = weights_of(*order[0])
    parts = []
    for turn, (image, number) in enumerate(order):
        grad_weights = ahead
        if turn + 1 < len(order):
            ahead = weights_of(*order[turn + 1])
        place, at = where_of(image, number)
        low = weights[image * HEADS + number]
        grad_values = dot_nn(low, grad_context[place, at : at + pair])
        soft = low.astype(F32)
        lifted = soft * grad_weights
        scores_low = (lifted - soft * jnp.sum(lifted, axis=0, keepdims=True)).astype(BF16)
        queries = qkv[place, at : at + pair]
        keys = qkv[place, width + at : width + at + pair]
        if number % 2 == 0:
            keys_turned = keys.T
        mine = slice(number % 2 * head, (number % 2 + 1) * head)
        parts.append(
            (
                dot_nn(keys_turned[mine], scores_low) * factor,
                dot_nn(scores_low, queries) * factor,
                grad_values,
            )
        )
        if number % 2:
            for which in range(3):
                if which:
                    merged = jnp.where(lane < head, parts[0][which], parts[1][which])
                else:
                    merged = jnp.concatenate([parts[0][0], parts[1][0]], axis=0).T
                grad_qkv[place, which * width + at : which * width + at + pair] = merged.astype(
                    BF16
                )
            parts = []


def sent_back_kernel(
    sent, grad_middle, grad_qkv, context, projected, active, gain, shift, mixing_in,
    conv_gain, grad_sent, proj_low, blocks, send, small,
):
    rows, width = sent.shape
    gradient = grad_middle[...]
    entering = sent[...].astype(F32)
    scaled, inverse = norm_parts(entering)
    normed = (scaled * across(gain) + across(shift)).astype(BF16)
    place_wide(blocks, dot_tn(normed, grad_qkv[...]).astype(BF16), 0, 0)
    lifted = dot_nt(grad_qkv[...], mixing_in[...])
    mixing = dot_tn(context[...], gradient.astype(BF16)).astype(BF16)
    place_wide(blocks, mixing, 3 * width // LANES, 0)
    grad_low = (gradient + norm_reverse(lifted, scaled, inverse, across(gain))).astype(BF16)
    grad_sent[...] = grad_low
    small[0:1, :] = total_rows(lifted * scaled)
    small[1:2, :] = total_rows(lifted)
    incoming = grad_low.astype(F32)
    scaled, inverse = norm_parts(projected[...])
    low = norm_reverse(incoming, scaled, inverse, across(conv_gain)).astype(BF16)
    proj_low[...] = low
    small[2:3, :] = total_rows(incoming * scaled)
    small[3:4, :] = total_rows(incoming)
    turned = low.T
    for start in range(0, active.shape[1], WIDE):
        grad = dot_nn(turned, active[:, start : start + WIDE]).astype(BF16).T
        place_tall(blocks, grad, start, PIECE)
    send[...] = blocks[1 - Here().core]


def conv_part(
    inside, local_in, proj_low, expanded, slope, taps, contract, wide_small, grad_cells, blocks,
    grad_low, first, last, first_row=0,
):
    rows = local_in.shape[0]
    images = rows // SLOTS
    valid = inside[...]
    column = lax.broadcasted_iota(jnp.int32, (SIDE, LANES), 0)
    first_column, last_column = column == 0, column == SIDE - 1
    for start in range(first, last, WIDE):
        part = slice(start, start + WIDE)
        grad_conv = dot_nt(proj_low, contract[part, :]) * slope[:, part].astype(F32)
        wide_small[9:10, part] = total_rows(grad_conv)
        grad_cells[0] = grad_conv
        pieces = []
        for lanes in range(0, WIDE, LANES):
            chans = slice(start + lanes, start + lanes + LANES)
            kernel = [taps[tap : tap + 1, chans] for tap in range(9)]
            sums = [jnp.zeros((SIDE, LANES), F32) for _ in range(9)]
            outcome = []
            for image in range(images):
                base = image * SLOTS
                shifted = {}
                for line in range(SIDE):
                    for ahead in (line, line + 1):
                        if ahead < SIDE and ahead not in shifted:
                            row = grad_cells[
                                0,
                                base + ahead * SIDE : base + (ahead + 1) * SIDE,
                                lanes : lanes + LANES,
                            ]
                            before, after = column_shifts(row, first_column, last_column)
                            shifted[ahead] = (after, row, before)
                    place = slice(base + line * SIDE, base + (line + 1) * SIDE)
                    cells = expanded[place, chans].astype(F32)
                    grid = jnp.zeros((SIDE, LANES), F32)
                    for a in range(3):
                        if 0 <= line + 1 - a < SIDE:
                            for b in range(3):
                                moved = shifted[line + 1 - a][b]
                                sums[3 * a + b] = sums[3 * a + b] + cells * moved
                                grid = grid + moved * kernel[3 * a + b]
                    outcome.append(grid)
            for tap in range(9):
                wide_small[tap : tap + 1, chans] = total_rows(sums[tap])
            pieces.append(jnp.concatenate(outcome, axis=0) * valid)
        grad_expanded = jnp.concatenate(pieces, axis=1)
        wide_small[10:11, part] = total_rows(grad_expanded)
        expanded_low = grad_expanded.astype(BF16)
        place_wide(
            blocks, dot_tn(local_in, expanded_low).astype(BF16), start // LANES, 0, first_row
        )
        grad_low[:, start - first : start - first + WIDE] = expanded_low


def conv_back_kernel(
    inside, tokens, proj_low, expanded, slope, taps, contract,
    grad_low, early, early_wide, grad_cells,
):
    conv_part(
        inside, own_share(tokens, proj_low.shape[0]), proj_low[...], expanded, slope, taps,
        contract, early_wide, grad_cells, early, grad_low, 0, expanded.shape[1] // 2,
    )


def small_rows(small, wide):
    mlp, sent = small
    mlp_wide, conv_wide = wide
    found = []
    for source, rows in ((mlp, 4), (sent, 4), (mlp_wide, 1), (conv_wide, 11)):
        for row in range(rows):
            for at in range(0, source.shape[1], LANES):
                found.append((source, row, at))
    return found


def conv_end_kernel(
    inside, tokens, proj_low, expanded, slope, taps, contract, early, early_wide,
    mlp_small, sent_small, mlp_wide, grad_low, pieces, send, conv_wide, grad_cells, short,
):
    channels = expanded.shape[1]
    half = channels // 2
    conv_wide[:, 0:half] = early_wide[:, 0:half]
    pieces[:, :, 0 : ROW // 2, 0:PIECE, :] = early[...]
    conv_part(
        inside, own_share(tokens, proj_low.shape[0]), proj_low[...], expanded, slope, taps,
        contract, conv_wide, grad_cells, pieces, grad_low, half, channels,
    )
    short[...] = jnp.zeros_like(short)
    places = small_rows((mlp_small, sent_small), (mlp_wide, conv_wide))
    for number, (source, row, at) in enumerate(places):
        piece, inside = number // 8, number % 8
        short[piece, inside : inside + 1, :] = source[row : row + 1, at : at + LANES]
    for piece in range(2 * SQUARE * ROW):
        value = short[piece]
        high = value.astype(BF16).astype(F32)
        pair = jnp.concatenate([high, value - high], axis=0).astype(BF16)
        core, square, row = piece // (SQUARE * ROW), piece // ROW % SQUARE, piece % ROW
        pieces[core, square, row, PIECE : PIECE + 16, :] = pair
    send[...] = pieces[1 - Here().core]


def summed(parts, short):
    total = parts[0].astype(F32)
    for part in parts[1:]:
        total = total + part.astype(F32)
    if not short:
        return total.astype(BF16)
    main = total.shape[0] - short
    value = total[main : main + 8] + total[main + 8 : main + 16]
    high = value.astype(BF16).astype(F32)
    return jnp.concatenate([total[:main], high, value - high], axis=0).astype(BF16)


def add_kernel(short, count, *refs):
    parts, outs = refs[:count], refs[count:]
    at = 0
    for out in outs:
        for step in range(out.shape[0]):
            out[step] = summed([part[at + step] for part in parts], short)
        at += out.shape[0]


def first_kernel(short, pieces, arrived, kept, send):
    here = Here()
    half = kept.shape[0]
    for step in range(2 * half):
        square, row = square_at(here, here.core, step // ROW), row_at(here, step % ROW)
        parts = (pieces[here.core, square, row], arrived[square, row])
        (kept, send)[step // half][step % half] = summed(parts, short)


def join_kernel(short, own, arrived, out):
    half = own.shape[0]
    out[0:half] = own[...]
    out[half:] = arrived[...]


def pieces_of(parts, begin=0):
    half = len(parts) // 2
    here = Here()
    for side in range(2):
        core = here.core if side == 0 else 1 - here.core
        step = begin
        for part in parts[side * half : (side + 1) * half]:
            for inside in range(part.shape[0]):
                square = square_at(here, core, step // ROW)
                yield core * SQUARE + square, row_at(here, step % ROW), part, inside
                step += 1


class Leaving:
    def __init__(self, stage, semaphores):
        self.stage, self.semaphores, self.copies = stage, semaphores, []

    def put(self, part, step, offset):
        slot = len(self.copies)
        for lane in range(ACROSS):
            low = offset + lane * HEIGHT
            self.stage[slot, :, lane * LANES : (lane + 1) * LANES] = part[
                step, low : low + HEIGHT, :
            ].astype(F32)
        return self.stage.at[slot], self.semaphores.at[slot]

    def tall(self, target, block, row, part, step, offset):
        source, semaphore = self.put(part, step, offset)
        at = pl.multiple_of((block * ROW + row) * HEIGHT, 16)
        self.copies.append(
            pltpu.make_async_copy(source, target.at[pl.ds(at, HEIGHT)], semaphore)
        )
        self.copies[-1].start()

    def wide(self, targets, block, row, part, step, offset):
        source, semaphore = self.put(part, step, offset)
        at = pl.multiple_of(block * HEIGHT, 16)
        span = ACROSS * LANES
        if len(targets) == 1:
            lanes = pl.ds(pl.multiple_of(row * span, LANES), span)
            self.copies.append(
                pltpu.make_async_copy(source, targets[0].at[pl.ds(at, HEIGHT), lanes], semaphore)
            )
            self.copies[-1].start()
            return
        last = pltpu.make_async_copy(source, targets[1].at[pl.ds(at, HEIGHT)], semaphore)
        self.copies.append(last)
        lanes = pl.ds(pl.multiple_of(jnp.minimum(row, ROW - 2) * span, LANES), span)
        others = pltpu.make_async_copy(source, targets[0].at[pl.ds(at, HEIGHT), lanes], semaphore)
        pl.when(row == ROW - 1)(last.start)
        pl.when(row < ROW - 1)(others.start)

    def wait(self):
        for copy in self.copies:
            copy.wait()


def mlp_end_kernel(*refs):
    (narrower, widener, stage, semaphores), parts = refs[-4:], refs[:-4]
    leaving = Leaving(stage, semaphores)
    for block, row, part, step in pieces_of(parts):
        leaving.tall(narrower, block, row, part, step, 0)
        leaving.wide((widener,), block, row, part, step, PIECE)
    leaving.wait()


def sent_end_kernel(*refs):
    (attention, mixing, projector, stage, semaphores), parts = refs[-5:], refs[:-5]
    leaving = Leaving(stage, semaphores)
    for block, row, part, step in pieces_of(parts):
        leaving.wide((attention, mixing), block, row, part, step, 0)
        leaving.tall(projector, block, row, part, step, PIECE)
    leaving.wait()


def conv_all_kernel(*refs):
    (*shorts, short, stage, semaphores), (expander, *parts) = refs[-15:], refs[-16:-15] + refs[:-16]
    leaving = Leaving(stage, semaphores)
    for block, row, part, step in pieces_of(parts):
        leaving.wide((expander,), block, row, part, step, 0)
        pair = part[step, PIECE : PIECE + 16, :].astype(F32)
        short[pl.ds(pl.multiple_of((block * ROW + row) * 8, 8), 8), :] = pair[0:8] + pair[8:16]
    (upshift, depthwise, depthshift, postgain, postshift, pregain, preshift, mixshift, midgain,
     midshift, wideshift, narrowshift) = shorts
    lanes = narrowshift.shape[0] // LANES
    wide_lanes = upshift.shape[0] // LANES
    number = 0
    for target in (narrowshift, midgain, midshift, mixshift, pregain, preshift, postgain, postshift):
        for lane in range(lanes):
            target[lane * LANES : (lane + 1) * LANES] = short[number, :]
            number += 1
    for target in (wideshift,) + (depthwise,) * 9 + (depthshift, upshift):
        for lane in range(wide_lanes):
            value = short[number : number + 1, :]
            if target is depthwise:
                tap = number // wide_lanes - 3
                target[tap : tap + 1, lane * LANES : (lane + 1) * LANES] = value
            else:
                target[lane * LANES : (lane + 1) * LANES] = value.reshape(LANES)
            number += 1
    leaving.wait()


def give_kernel(
    inside, middle, lit, contract, contract_bias, grad_sent, early_low, late_low, enlarge,
    own, give,
):
    half = early_low.shape[1]
    total = middle[...] + dot_nn(lit[...], contract[...]) + across(contract_bias)
    output = (total * inside[...]).astype(BF16)
    gradient = grad_sent[...].astype(F32) + dot_nt(early_low[...], enlarge[:, 0:half])
    gradient = (gradient + dot_nt(late_low[...], enlarge[:, half:])).astype(BF16)
    first = Here().section == 0
    own[...] = jnp.where(first, gradient, output)
    give[...] = jnp.where(first, output, gradient)


def ends_kernel(filled, own, arrived, ends, means, semaphores):
    share = ends.shape[0] // 2
    local, slots, width = ends.shape[1:]
    first = Here().section
    copies = []
    for source, section in ((own, first), (arrived, 1 - first)):
        for number in range(share * local):
            copies.append(
                pltpu.make_async_copy(
                    source.at[pl.ds(number * slots, slots)],
                    ends.at[section * share + number // local, number % local],
                    semaphores.at[len(copies)],
                )
            )
            copies[-1].start()
    micro = lax.broadcasted_iota(jnp.int32, (1, ends.shape[0]), 1)
    rows = [jnp.zeros((1, ends.shape[0]), F32) for _ in range(local)]
    for source, section in ((own, first), (arrived, 1 - first)):
        for number in range(share * local):
            value = source[number * slots : (number + 1) * slots, :].astype(F32)
            square = jnp.sum(value * value, axis=0, keepdims=True)
            image = (section * share + number // local) * local + number % local
            mean = jnp.sum(square, axis=1, keepdims=True) / filled[pl.ds(image, 1), 0:1]
            held = micro == section * share + number // local
            rows[number % local] = jnp.where(held, jnp.sqrt(mean), rows[number % local])
    for image in range(local):
        means[0, image : image + 1, :] = rows[image]
    for copy in copies:
        copy.wait()


WHOLE = pl.BlockSpec(memory_space=pltpu.VMEM)
ANYWHERE = pl.BlockSpec(memory_space=pl.ANY)
REMOTE = pl.BlockSpec(memory_space=pltpu.HBM)
SCALARS = pl.BlockSpec(memory_space=pltpu.SMEM)
COST = 30
ORDER = (
    "mlp.near", "conv.first", "inner.second", "mlp.far", "conv.second", "swap_ends", "inner.near",
    "conv.near", "mlp.total", "inner.far", "conv.far", "mlp.join_row", "put_ends", "inner.total",
    "conv.total", "inner.join_row", "mlp.join_square", "conv.join_row", "inner.join_square",
    "mlp.join_cores", "conv.join_square", "put_mlp", "inner.join_cores", "conv.join_cores",
    "put_inner", "put_conv",
)
COSTS = {
    "conv_first": 0, "conv_second": 30, "conv_far": 0, "conv_join_square": 30, "give": 30,
    "mlp_cores": 0, "conv_cores": 30, "conv_all": 0, "inner_cores": 30, "conv_total": 30,
    "inner_join_square": 0, "mlp_end": 0, "mlp_far": 0, "conv_near": 0,
}
BOTH = ("section", "dp")


def shape(dims, kind):
    return jax.ShapeDtypeStruct(dims, kind)


class Calls:
    def __init__(self):
        self.last = None

    def __call__(self, kernel, name, ins, outs, scratch=(), mb=8, us=0, smem=(), hbm=(), hbm_outs=(), aliases={}):
        count = len(ins)
        after = () if self.last is None else (self.last,)


        def body(*refs):
            token = refs[count + len(after)]
            token[...] = jnp.zeros_like(token)
            kernel(*refs[:count], *refs[count + len(after) + 1 :])

        ins = [
            pltpu.with_memory_space_constraint(value, pltpu.HBM) if place in hbm else value
            for place, value in enumerate(ins)
        ]
        outs = [
            pltpu.HBM(out.shape, out.dtype) if place in hbm_outs else out
            for place, out in enumerate(outs)
        ]
        self.last, *result = pl.pallas_call(
            body,
            out_shape=[shape((8, LANES), F32)] + outs,
            in_specs=[
                SCALARS if place in smem else REMOTE if place in hbm else WHOLE
                for place in range(count)
            ]
            + [ANYWHERE] * len(after),
            out_specs=[WHOLE]
            + [REMOTE if place in hbm_outs else WHOLE for place in range(len(outs))],
            scratch_shapes=list(scratch),
            input_output_aliases={place: out + 1 for place, out in aliases.items()},
            cost_estimate=pl.CostEstimate(
                flops=1 + int(COSTS.get(name, us) * 1e9), bytes_accessed=1, transcendentals=0
            ),
            compiler_params=pltpu.CompilerParams(vmem_limit_bytes=mb * 1024 * 1024),
            name=name,
        )(*ins, *after)
        return result


    def fence(self, value, name):
        def body(after, value, token, out):
            token[...] = jnp.zeros_like(token)

        self.last, value = pl.pallas_call(
            body,
            out_shape=[shape((8, LANES), F32), shape(value.shape, value.dtype)],
            in_specs=[ANYWHERE] * 2,
            out_specs=[WHOLE, ANYWHERE],
            input_output_aliases={1: 1},
            cost_estimate=pl.CostEstimate(
                flops=1 + int(COSTS.get(name, 0) * 1e9), bytes_accessed=1, transcendentals=0
            ),
            compiler_params=pltpu.CompilerParams(vmem_limit_bytes=1024 * 1024),
            name=name,
        )(self.last, value)
        return value


def swapped(value, digit, step=0):
    sections, members = (lax.axis_size(axis) for axis in BOTH)
    pairs = []
    for section in range(sections):
        for member in range(members):
            if digit == "first" or digit == "second":
                across = 2 if digit == "first" else 1
            else:
                across = step if digit == "square" else 0
            if member % 2:
                across = SWAPPED[across]
            along = {"near": 4}.get(digit, digit if isinstance(digit, int) else 0)
            other = (section ^ across // 2) * members + (member ^ (across % 2 * 2 + along))
            pairs.append((section * members + member, other))
    return lax.ppermute(value, BOTH, pairs)


class Group:
    def __init__(self, name, calls, keep, send, short=0, cost=COST):
        self.name, self.calls, self.short, self.cost = name, calls, short, cost
        self.rows = keep.shape[3]
        self.parts = [keep, swapped(send, 1)]

    def call(self, kernel, what, ins, outs):
        return self.calls(
            functools.partial(kernel, self.short), f"{self.name}_{what}", ins,
            [shape((count, self.rows, LANES), BF16) for count in outs], us=self.cost,
        )

    def add(self, what, outs=1):
        pieces = [self.parts[0].shape[0] // outs] * outs
        kernel = lambda short, *refs: add_kernel(short, len(self.parts), *refs)
        return self.call(kernel, what, self.parts, pieces)

    def halve(self, what):
        keep, send = self.add(what, 2)
        self.parts = [keep, swapped(send, what)]

    def first(self):
        half = SQUARE * ROW // 2
        keep, send = self.call(first_kernel, "first", self.parts, [half] * 2)
        self.parts = [keep, swapped(send, "first")]

    def second(self):
        self.halve("second")

    def square(self):
        keep, *send = self.add("square", SQUARE)
        self.parts = [keep] + [swapped(part, "square", 1 + at) for at, part in enumerate(send)]

    def near(self):
        self.halve("near")

    def far(self):
        stride, what = 4, "far"
        while stride < lax.axis_size("dp") // 2:
            stride *= 2
            (own,) = self.add(what)
            self.parts, what = [own, swapped(own, stride)], f"over_{stride}"

    def total(self):
        (own,) = self.add("total")
        self.parts = [own, swapped(own, "near")]

    def join(self, what):
        (own,) = self.call(join_kernel, what, self.parts, [2 * self.parts[0].shape[0]])
        return own

    def join_row(self):
        own = self.join("join_row")
        self.parts = [own, swapped(own, "second")]

    def join_square(self):
        own = self.join("join_square")
        self.parts = [own, swapped(own, "first")]
        self.near_half = swapped(own, 1)

    def join_cores(self):
        far_half = self.calls.fence(self.parts[1], f"{self.name}_cores")
        self.blocks = [self.parts[0], far_half, self.near_half, swapped(far_half, 1)]

    def early(self):
        return [self.parts[0], self.near_half]

    def late(self):
        return self.blocks[1::2]

    def join_all(self):
        own = self.join("join_row")
        self.parts = [own] + [swapped(own, "square", step) for step in range(1, SQUARE)]
        self.blocks = self.parts + [swapped(part, 1) for part in self.parts]


def shards(
    entering_tokens,
    output_sensitivity,
    picture_tile_extents,
    pointwise_enlarge,
    enlarge_bias,
    channelwise_kernel,
    channelwise_conv_bias,
    pointwise_contract,
    convblock_scale,
    convblock_offset,
    attend_scale,
    attend_offset,
    query_key_proj,
    heads_output_proj,
    heads_output_bias,
    feedforward_scale,
    feedforward_offset,
    feedforward_enlarge,
    feedforward_enlarge_bias,
    feedforward_contract,
    contract_bias,
):
    micro_count, local_images, slots, width = entering_tokens.shape
    channels = pointwise_enlarge.shape[1]
    share = micro_count // 2
    images = share * local_images
    rows = images * slots
    call = Calls()
    extents = jnp.transpose(picture_tile_extents, (1, 2, 0))
    sent, expanded, slope, active, projected, inside, filled = call(
        conv_ahead_kernel, "conv_ahead",
        (extents, entering_tokens, pointwise_enlarge, enlarge_bias, channelwise_kernel,
         channelwise_conv_bias, pointwise_contract, convblock_scale, convblock_offset),
        [shape((rows, width), BF16), shape((rows, channels), BF16), shape((rows, channels), BF16),
         shape((rows, channels), BF16), shape((rows, width), F32), shape((rows, 1), F32),
         shape((micro_count * local_images, LANES), F32)],
        [pltpu.VMEM((2, rows, BLOCK), F32), pltpu.VMEM((share, local_images, slots, width), BF16)]
        + [pltpu.VMEM(value.shape, value.dtype) for value in
           (pointwise_enlarge, enlarge_bias, channelwise_kernel, channelwise_conv_bias,
            pointwise_contract, convblock_scale, convblock_offset)]
        + [pltpu.SMEM(extents.shape, jnp.int32), pltpu.SemaphoreType.DMA((6 + 2 * share + 2 * channels // BLOCK,))],
        mb=14, hbm=range(9),
    )
    qkv, weights, context, middle = call(
        attend_ahead_kernel, "attend_ahead",
        (inside, sent, attend_scale, attend_offset, query_key_proj, heads_output_proj,
         heads_output_bias),
        [shape((rows, 3 * width), BF16), shape((images * HEADS, slots, slots), BF16),
         shape((rows, width), BF16), shape((rows, width), F32)], mb=10,
    )
    halves = [shape((cores, SQUARE, ROW, 2 * PIECE, LANES), BF16) for cores in (2, 1)]
    halves[1] = shape(halves[1].shape[1:], BF16)
    lit, grad_middle, keep, send, mlp_small, mlp_wide = call(
        mlp_kernel, "mlp",
        (inside, middle, output_sensitivity, feedforward_scale, feedforward_offset, feedforward_enlarge,
         feedforward_enlarge_bias, feedforward_contract),
        [shape((rows, channels), BF16), shape((rows, width), F32)] + halves
        + [shape((8, width), F32), shape((1, channels), F32)],
        mb=18,
    )
    mlp = Group("mlp", call, keep, send)
    (grad_qkv,) = call(
        heads_back_kernel, "heads_back", (grad_middle, qkv, weights, heads_output_proj),
        [shape((rows, 3 * width), BF16)], mb=10,
    )
    mlp.first()
    grad_sent, proj_low, keep, send, sent_small = call(
        sent_back_kernel, "sent_back",
        (sent, grad_middle, grad_qkv, context, projected, active, attend_scale, attend_offset,
         query_key_proj, convblock_scale),
        [shape((rows, width), BF16), shape((rows, width), BF16)] + halves
        + [shape((8, width), F32)],
        mb=14,
    )
    inner = Group("inner", call, keep, send)
    early_pieces = shape((2, SQUARE, ROW // 2, PIECE, LANES), BF16)
    early_low, early, early_wide = call(
        conv_back_kernel, "conv_back",
        (inside, entering_tokens, proj_low, expanded, slope, channelwise_kernel,
         pointwise_contract),
        [shape((rows, channels // 2), BF16), early_pieces, shape((16, channels), F32)],
        [pltpu.VMEM((1, rows, WIDE), F32)], mb=12,
    )
    mlp.second()
    inner.first()
    halves = [shape((cores, SQUARE, ROW, PIECE + 16, LANES), BF16) for cores in (2, 1)]
    halves[1] = shape(halves[1].shape[1:], BF16)
    late_low, keep, send = call(
        conv_end_kernel, "conv_end",
        (inside, entering_tokens, proj_low, expanded, slope, channelwise_kernel,
         pointwise_contract, early, early_wide, mlp_small, sent_small, mlp_wide),
        [shape((rows, channels // 2), BF16)] + halves,
        [pltpu.VMEM((16, channels), F32), pltpu.VMEM((1, rows, WIDE), F32),
         pltpu.VMEM((2 * SQUARE * ROW, 8, LANES), F32)],
        mb=14,
    )
    conv = Group("conv", call, keep, send, 16)
    line, wide_line = shape((width,), F32), shape((channels,), F32)
    tall, wide = shape((channels, width), F32), shape((width, channels), F32)
    pieces = 2 * SQUARE * ROW

    def leaving(count):
        return [pltpu.VMEM((count, HEIGHT, ACROSS * LANES), F32), pltpu.SemaphoreType.DMA((count,))]

    def swap_ends():
        own, give = call(
            give_kernel, "give",
            (inside, middle, lit, feedforward_contract, contract_bias, grad_sent, early_low,
             late_low, pointwise_enlarge),
            [shape((rows, width), BF16)] * 2, mb=10, us=COST,
        )
        return own, lax.ppermute(give, "section", [(0, 1), (1, 0)])

    def put_ends(own, arrived):
        return call(
            ends_kernel, "ends", (filled, own, arrived),
            [shape(entering_tokens.shape, BF16), shape((1, local_images, micro_count), F32)],
            [pltpu.SemaphoreType.DMA((micro_count * local_images,))], hbm_outs=(0,), us=COST,
        )

    def put_mlp():
        return call(
            mlp_end_kernel, "mlp_end", mlp.blocks, [tall, wide], leaving(2 * pieces), mb=12,
            hbm_outs=(0, 1), us=COST,
        )

    def put_inner():
        return call(
            sent_end_kernel, "sent_end", inner.blocks,
            [shape((width, 3 * width), F32), shape((width, width), F32), tall],
            leaving(2 * pieces), mb=12, hbm_outs=(0, 1, 2), us=COST,
        )

    def put_conv():
        return call(
            conv_all_kernel, "conv_all", conv.blocks,
            [wide, wide_line, shape((9, channels), F32), wide_line] + [line] * 7
            + [wide_line, line],
            [pltpu.VMEM((pieces * 8, LANES), F32)] + leaving(pieces), hbm_outs=(0,), us=COST,
        )

    done = {}
    for step in ORDER:
        name, _, what = step.partition(".")
        if what:
            getattr({"mlp": mlp, "inner": inner, "conv": conv}[name], what)()
        elif name == "swap_ends":
            done[name] = swap_ends()
        elif name == "put_ends":
            done[name] = put_ends(*done["swap_ends"])
        else:
            done[name] = {"put_mlp": put_mlp, "put_inner": put_inner, "put_conv": put_conv}[name]()
    narrower, widener = done["put_mlp"]
    attention, mixing, projector = done["put_inner"]
    (expander, upshift, depthwise, depthshift, postgain, postshift, pregain, preshift, mixshift,
     midgain, midshift, wideshift, narrowshift) = done["put_conv"]
    ends, means = done["put_ends"]
    means = jnp.transpose(means, (0, 2, 1))
    return (
        ends[None], means, expander, upshift, depthwise, depthshift, projector, postgain,
        postshift, pregain, preshift, attention, mixing, mixshift, midgain, midshift, widener,
        wideshift, narrower, narrowshift,
    )


def solution(mesh):
    tokens = P(None, "dp", None, None)
    placed = (tokens, tokens, P(None, "dp", None)) + (P(),) * 18
    return jax.shard_map(
        shards,
        mesh=mesh,
        in_specs=placed,
        out_specs=(P("section", None, "dp", None, None), P("section", None, "dp")) + (P(),) * 18,
        check_vma=False,
    )
```

```python
import functools
import math

import jax
import jax.numpy as jnp
from jax import lax
from jax.experimental import pallas as pl
from jax.experimental.pallas import tpu as pltpu
from jax.sharding import PartitionSpec as P

HEADS = 6
SIDE = 16
SLOTS = SIDE * SIDE
EPSILON = 1e-05
BLOCKED = -1000000000.0
LANES = 128
BLOCK = 512
WIDE = 768
SQUARE = 4
ROW = 4
PIECE = 144
HEIGHT = 48
ACROSS = PIECE // HEIGHT
SWAPPED = (0, 2, 1, 3)
BF16 = jnp.bfloat16
F32 = jnp.float32


def dot_nn(left, right):
    return jnp.dot(left, right, preferred_element_type=F32)


def dot_nt(left, right):
    return lax.dot_general(left, right, (((1,), (1,)), ((), ())), preferred_element_type=F32)


def dot_tn(left, right):
    return lax.dot_general(left, right, (((0,), (0,)), ((), ())), preferred_element_type=F32)


def norm_parts(values):
    centered = values - jnp.mean(values, axis=-1, keepdims=True)
    inverse = lax.rsqrt(jnp.mean(centered * centered, axis=-1, keepdims=True) + EPSILON)
    return centered * inverse, inverse


def norm_reverse(upstream, scaled, inverse, gain):
    lifted = upstream * gain
    return inverse * (
        lifted
        - jnp.mean(lifted, axis=-1, keepdims=True)
        - scaled * jnp.mean(lifted * scaled, axis=-1, keepdims=True)
    )


def across(vector):
    return vector[...].reshape(1, -1)


def own_share(tokens, rows):
    share = rows // (tokens.shape[1] * tokens.shape[2])
    return tokens[pl.ds(Here().section * share, share)].reshape(rows, tokens.shape[3])


def total_rows(values):
    return jnp.sum(values, axis=0, keepdims=True)


class Here:
    def __init__(self):
        member = lax.axis_index("dp")
        self.section = lax.axis_index("section")
        self.core = member % 2
        self.square = self.section * 2 + member // 2 % 2
        self.row = member // 4 % ROW


def own_share(tokens, rows):
    share = rows // (tokens.shape[1] * tokens.shape[2])
    return tokens[pl.ds(Here().section * share, share)].reshape(rows, tokens.shape[3])


def total_rows(values):
    return jnp.sum(values, axis=0, keepdims=True)


def own_share(tokens, rows):
    share = rows // (tokens.shape[1] * tokens.shape[2])
    return tokens[pl.ds(Here().section * share, share)].reshape(rows, tokens.shape[3])


def total_rows(values):
    return jnp.sum(values, axis=0, keepdims=True)


class Here:
    def __init__(self):
        member = lax.axis_index("dp")
        self.section = lax.axis_index("section")
        self.core = member % 2
        self.square = self.section * 2 + member // 2 % 2
        self.row = member // 4 % ROW


def own_share(tokens, rows):
    share = rows // (tokens.shape[1] * tokens.shape[2])
    return tokens[pl.ds(Here().section * share, share)].reshape(rows, tokens.shape[3])


def total_rows(values):
    return jnp.sum(values, axis=0, keepdims=True)


def column_shifts(row, first_column, last_column):
    before = jnp.where(first_column, 0.0, pltpu.roll(row, 1, 0))
    after = jnp.where(last_column, 0.0, pltpu.roll(row, SIDE - 1, 0))
    return before, after


def conv_ahead_kernel(
    extents_from, tokens, enlarge_from, enlarge_bias_from, taps_from, taps_bias_from, contract_from,
    gain_from, shift_from, sent, expanded, slope, active, projected, inside, filled,
    grid_cells, entering, enlarge, enlarge_bias, taps, taps_bias, contract, gain, shift, extents, arrivals,
):
    rows, width = sent.shape
    images = rows // SLOTS
    channels = enlarge.shape[1]
    share = entering.shape[0]
    starts = range(0, channels, BLOCK)
    section = Here().section
    copies = [(extents_from, extents)]
    copies += [
        (tokens.at[section * share + number // 2, :, half], entering.at[number // 2, :, half])
        for number in range(2 * share)
        for half in (pl.ds(number % 2 * (SLOTS // 2), SLOTS // 2),)
    ]
    copies += [(enlarge_from.at[:, pl.ds(0, BLOCK)], enlarge.at[:, pl.ds(0, BLOCK)])]
    copies += [
        (enlarge_bias_from, enlarge_bias), (taps_from, taps), (taps_bias_from, taps_bias),
        (gain_from, gain), (shift_from, shift),
    ]
    early = len(copies)
    for start in starts:
        part = pl.ds(start, BLOCK)
        if start:
            copies.append((enlarge_from.at[:, part], enlarge.at[:, part]))
        copies.append((contract_from.at[part], contract.at[part]))
    copies = [
        pltpu.make_async_copy(source, target, arrivals.at[number])
        for number, (source, target) in enumerate(copies)
    ]
    for copy in copies:
        copy.start()
    copies[0].wait()
    micros, local = extents.shape[2], extents.shape[0]
    for image in range(micros * local):
        count = extents[image % local, 0, image // local] * extents[image % local, 1, image // local]
        filled[image : image + 1, :] = jnp.full((1, LANES), (count * width).astype(F32))
    slot = lax.broadcasted_iota(jnp.int32, (SLOTS, 1), 0)
    for image in range(images):
        height, across_it = (
            extents[image % local, side, section * share + image // local] for side in range(2)
        )
        held = (slot // SIDE < height) & (slot % SIDE < across_it)
        inside[image * SLOTS : (image + 1) * SLOTS, :] = held.astype(F32)
    for copy in copies[1:early]:
        copy.wait()
    later = copies[early:]
    local_in = entering[...].reshape(rows, width)
    valid = inside[...]
    column = lax.broadcasted_iota(jnp.int32, (SIDE, LANES), 0)
    first_column, last_column = column == 0, column == SIDE - 1
    total = jnp.zeros((rows, width), F32)

    def cells_of(start):
        part = slice(start, start + BLOCK)
        if start:
            later[2 * (start // BLOCK) - 1].wait()
        cells = (dot_nn(local_in, enlarge[:, part]) + enlarge_bias[part].reshape(1, -1)) * valid
        grid_cells[start // BLOCK % 2] = cells
        expanded[:, part] = cells.astype(BF16)

    cells_of(0)
    for start in starts:
        part = slice(start, start + BLOCK)
        number = start // BLOCK
        if start + BLOCK < channels:
            cells_of(start + BLOCK)
        for left in range(0, BLOCK, LANES):
            inner = slice(start + left, start + left + LANES)
            kernel = [taps[tap : tap + 1, inner] for tap in range(9)]
            bias = taps_bias[inner].reshape(1, -1)
            for image in range(images):
                base = image * SLOTS
                above = here = None
                for line in range(SIDE + 1):
                    if line < SIDE:
                        row = grid_cells[
                            number % 2,
                            base + line * SIDE : base + (line + 1) * SIDE,
                            left : left + LANES,
                        ]
                        before, after = column_shifts(row, first_column, last_column)
                        sums = [
                            before * kernel[3 * a]
                            + row * kernel[3 * a + 1]
                            + after * kernel[3 * a + 2]
                            for a in range(3)
                        ]
                    if line > 0:
                        convolved = above + sums[2] if line < SIDE else above
                        gate = jax.nn.sigmoid(convolved)
                        lit = convolved * gate
                        place = slice(base + (line - 1) * SIDE, base + line * SIDE)
                        active[place, inner] = lit.astype(BF16)
                        slope[place, inner] = (gate + lit * (1.0 - gate)).astype(BF16)
                    if line < SIDE:
                        above = (here if line > 0 else bias) + sums[1]
                        here = bias + sums[0]
        later[2 * number].wait()
        total = total + dot_nn(active[:, part], contract[part, :])
    projected[...] = total
    scaled, _ = norm_parts(total)
    sent[...] = (local_in.astype(F32) + scaled * across(gain) + across(shift)).astype(BF16)


def head_lanes(width):
    return lax.broadcasted_iota(jnp.int32, (1, width), 1)


def attend_ahead_kernel(
    inside, sent, gain, shift, mixing_in, mixing_out, mixing_bias,
    qkv, weights, context, middle,
):
    rows, width = sent.shape
    images = rows // SLOTS
    head = width // HEADS
    factor = 1.0 / math.sqrt(head)
    entering = sent[...].astype(F32)
    scaled, _ = norm_parts(entering)
    normed = (scaled * across(gain) + across(shift)).astype(BF16)
    for start in range(0, 3 * width, width):
        part = slice(start, start + width)
        qkv[:, part] = dot_nn(normed, mixing_in[:, part]).astype(BF16)
    pair = 2 * head
    lane = head_lanes(pair)
    valid = [inside[image * SLOTS : (image + 1) * SLOTS, :] > 0.5 for image in range(images)]
    order = [(image, number) for image in range(images) for number in range(HEADS)]

    def where_of(image, number):
        at = number // 2 * pair
        return slice(image * SLOTS, (image + 1) * SLOTS), at

    def scores_of(image, number):
        place, at = where_of(image, number)
        low, high = number % 2 * head, (number % 2 + 1) * head
        keys = qkv[place, width + at : width + at + pair]
        own = jnp.where((lane >= low) & (lane < high), keys, jnp.zeros_like(keys))
        return dot_nt(own, qkv[place, at : at + pair])

    ahead = scores_of(*order[0])
    gathered = []
    for turn, (image, number) in enumerate(order):
        scores = ahead
        if turn + 1 < len(order):
            ahead = scores_of(*order[turn + 1])
        scores = jnp.where(valid[image], scores * factor, BLOCKED)
        powers = jnp.exp(scores - jnp.max(scores, axis=0, keepdims=True))
        low = (powers * (1.0 / jnp.sum(powers, axis=0, keepdims=True))).astype(BF16)
        weights[image * HEADS + number] = low
        place, at = where_of(image, number)
        gathered.append(dot_tn(low, qkv[place, 2 * width + at : 2 * width + at + pair]))
        if number % 2:
            context[place, at : at + pair] = jnp.where(lane < head, *gathered).astype(BF16)
            gathered = []
    middle[...] = entering + dot_nn(context[...], mixing_out[...]) + across(mixing_bias)


def place_tall(pieces, grad, first_row, offset):
    for low in range(first_row, first_row + grad.shape[0], 16):
        piece, inside = low // HEIGHT, low % HEIGHT
        core, square, row = piece // (SQUARE * ROW), piece // ROW % SQUARE, piece % ROW
        for lane in range(ACROSS):
            at = offset + lane * HEIGHT + inside
            pieces[core, square, row, at : at + 16, :] = grad[
                low - first_row : low - first_row + 16, lane * LANES : (lane + 1) * LANES
            ]


def place_wide(pieces, grad, first_lane, offset, first_row=0):
    for block in range(grad.shape[0] // HEIGHT):
        for lane in range(grad.shape[1] // LANES):
            row, inside = (first_lane + lane) // ACROSS, (first_lane + lane) % ACROSS
            at = offset + inside * HEIGHT
            pieces[block // SQUARE, block % SQUARE, row - first_row, at : at + HEIGHT, :] = grad[
                block * HEIGHT : (block + 1) * HEIGHT, lane * LANES : (lane + 1) * LANES
            ]


def square_at(here, core, step):
    return here.square ^ jnp.where(core == 0, step, SWAPPED[step])


def row_at(here, step):
    return step % 2 * 2 + (here.row % 2 ^ step // 2)


def mlp_kernel(
    inside, middle, sensitivity, gain, shift, enlarge, enlarge_bias, contract,
    lit, grad_middle, blocks, send, small, wide_small,
):
    rows, width = middle.shape
    images = rows // SLOTS
    hidden_width = enlarge.shape[1]
    valid = inside[...]
    center = middle[...]
    scaled, inverse = norm_parts(center)
    hidden = (scaled * across(gain) + across(shift)).astype(BF16)
    grad_out = own_share(sensitivity, rows).astype(F32) * valid
    out_low = grad_out.astype(BF16)
    grad_hidden = jnp.zeros((rows, width), F32)
    out_turned, hidden_turned = out_low.T, hidden.T

    def products(start):
        part = slice(start, start + WIDE)
        return dot_nn(hidden, enlarge[:, part]), dot_nt(out_low, contract[part, :])

    ahead = products(0)
    for start in range(0, hidden_width, WIDE):
        part = slice(start, start + WIDE)
        widened, grad_wide = ahead
        if start + WIDE < hidden_width:
            ahead = products(start + WIDE)
        widened = widened + enlarge_bias[part].reshape(1, -1)
        normal_cdf = 0.5 * (1.0 + lax.erf(widened * (1.0 / math.sqrt(2.0))))
        normal_pdf = jnp.exp(-0.5 * widened * widened) * (1.0 / math.sqrt(2.0 * math.pi))
        activated = (widened * normal_cdf).astype(BF16)
        lit[:, part] = activated
        grad_wide = grad_wide * (normal_cdf + widened * normal_pdf)
        wide_small[:, part] = total_rows(grad_wide)
        wide_low = grad_wide.astype(BF16)
        place_tall(blocks, dot_nn(out_turned, activated).astype(BF16).T, start, 0)
        place_wide(blocks, dot_nn(hidden_turned, wide_low).astype(BF16), start // LANES, PIECE)
        grad_hidden = grad_hidden + dot_nt(wide_low, enlarge[:, part])
    gradient = grad_out + norm_reverse(grad_hidden, scaled, inverse, across(gain))
    grad_middle[...] = gradient
    small[0:1, :] = total_rows(grad_out)
    small[1:2, :] = total_rows(grad_hidden * scaled)
    small[2:3, :] = total_rows(grad_hidden)
    small[3:4, :] = total_rows(gradient)
    send[...] = blocks[1 - Here().core]


def heads_back_kernel(
    grad_middle, qkv, weights, mixing_out, grad_qkv,
):
    rows, width = grad_middle.shape
    images = rows // SLOTS
    head = width // HEADS
    factor = 1.0 / math.sqrt(head)
    grad_context = dot_nt(grad_middle[...].astype(BF16), mixing_out[...]).astype(BF16)
    pair = 2 * head
    lane = head_lanes(pair)
    order = [(image, number) for image in range(images) for number in range(HEADS)]

    def where_of(image, number):
        at = number // 2 * pair
        return slice(image * SLOTS, (image + 1) * SLOTS), at

    def weights_of(image, number):
        place, at = where_of(image, number)
        low, high = number % 2 * head, (number % 2 + 1) * head
        values = qkv[place, 2 * width + at : 2 * width + at + pair]
        own = jnp.where((lane >= low) & (lane < high), values, jnp.zeros_like(values))
        return dot_nt(own, grad_context[place, at : at + pair])

    ahead = weights_of(*order[0])
    parts = []
    for turn, (image, number) in enumerate(order):
        grad_weights = ahead
        if turn + 1 < len(order):
            ahead = weights_of(*order[turn + 1])
        place, at = where_of(image, number)
        low = weights[image * HEADS + number]
        grad_values = dot_nn(low, grad_context[place, at : at + pair])
        soft = low.astype(F32)
        lifted = soft * grad_weights
        scores_low = (lifted - soft * jnp.sum(lifted, axis=0, keepdims=True)).astype(BF16)
        queries = qkv[place, at : at + pair]
        keys = qkv[place, width + at : width + at + pair]
        if number % 2 == 0:
            keys_turned = keys.T
        mine = slice(number % 2 * head, (number % 2 + 1) * head)
        parts.append(
            (
                dot_nn(keys_turned[mine], scores_low) * factor,
                dot_nn(scores_low, queries) * factor,
                grad_values,
            )
        )
        if number % 2:
            for which in range(3):
                if which:
                    merged = jnp.where(lane < head, parts[0][which], parts[1][which])
                else:
                    merged = jnp.concatenate([parts[0][0], parts[1][0]], axis=0).T
                grad_qkv[place, which * width + at : which * width + at + pair] = merged.astype(
                    BF16
                )
            parts = []


def sent_back_kernel(
    sent, grad_middle, grad_qkv, context, projected, active, gain, shift, mixing_in,
    conv_gain, grad_sent, proj_low, blocks, send, small,
):
    rows, width = sent.shape
    gradient = grad_middle[...]
    entering = sent[...].astype(F32)
    scaled, inverse = norm_parts(entering)
    normed = (scaled * across(gain) + across(shift)).astype(BF16)
    place_wide(blocks, dot_tn(normed, grad_qkv[...]).astype(BF16), 0, 0)
    lifted = dot_nt(grad_qkv[...], mixing_in[...])
    mixing = dot_tn(context[...], gradient.astype(BF16)).astype(BF16)
    place_wide(blocks, mixing, 3 * width // LANES, 0)
    grad_low = (gradient + norm_reverse(lifted, scaled, inverse, across(gain))).astype(BF16)
    grad_sent[...] = grad_low
    small[0:1, :] = total_rows(lifted * scaled)
    small[1:2, :] = total_rows(lifted)
    incoming = grad_low.astype(F32)
    scaled, inverse = norm_parts(projected[...])
    low = norm_reverse(incoming, scaled, inverse, across(conv_gain)).astype(BF16)
    proj_low[...] = low
    small[2:3, :] = total_rows(incoming * scaled)
    small[3:4, :] = total_rows(incoming)
    turned = low.T
    for start in range(0, active.shape[1], WIDE):
        grad = dot_nn(turned, active[:, start : start + WIDE]).astype(BF16).T
        place_tall(blocks, grad, start, PIECE)
    send[...] = blocks[1 - Here().core]


def conv_part(
    inside, local_in, proj_low, expanded, slope, taps, contract, wide_small, grad_cells, blocks,
    grad_low, first, last, first_row=0,
):
    rows = local_in.shape[0]
    images = rows // SLOTS
    valid = inside[...]
    column = lax.broadcasted_iota(jnp.int32, (SIDE, LANES), 0)
    first_column, last_column = column == 0, column == SIDE - 1
    for start in range(first, last, WIDE):
        part = slice(start, start + WIDE)
        grad_conv = dot_nt(proj_low, contract[part, :]) * slope[:, part].astype(F32)
        wide_small[9:10, part] = total_rows(grad_conv)
        grad_cells[0] = grad_conv
        pieces = []
        for lanes in range(0, WIDE, LANES):
            chans = slice(start + lanes, start + lanes + LANES)
            kernel = [taps[tap : tap + 1, chans] for tap in range(9)]
            sums = [jnp.zeros((SIDE, LANES), F32) for _ in range(9)]
            outcome = []
            for image in range(images):
                base = image * SLOTS
                shifted = {}
                for line in range(SIDE):
                    for ahead in (line, line + 1):
                        if ahead < SIDE and ahead not in shifted:
                            row = grad_cells[
                                0,
                                base + ahead * SIDE : base + (ahead + 1) * SIDE,
                                lanes : lanes + LANES,
                            ]
                            before, after = column_shifts(row, first_column, last_column)
                            shifted[ahead] = (after, row, before)
                    place = slice(base + line * SIDE, base + (line + 1) * SIDE)
                    cells = expanded[place, chans].astype(F32)
                    grid = jnp.zeros((SIDE, LANES), F32)
                    for a in range(3):
                        if 0 <= line + 1 - a < SIDE:
                            for b in range(3):
                                moved = shifted[line + 1 - a][b]
                                sums[3 * a + b] = sums[3 * a + b] + cells * moved
                                grid = grid + moved * kernel[3 * a + b]
                    outcome.append(grid)
            for tap in range(9):
                wide_small[tap : tap + 1, chans] = total_rows(sums[tap])
            pieces.append(jnp.concatenate(outcome, axis=0) * valid)
        grad_expanded = jnp.concatenate(pieces, axis=1)
        wide_small[10:11, part] = total_rows(grad_expanded)
        expanded_low = grad_expanded.astype(BF16)
        place_wide(
            blocks, dot_tn(local_in, expanded_low).astype(BF16), start // LANES, 0, first_row
        )
        grad_low[:, start - first : start - first + WIDE] = expanded_low


def conv_back_kernel(
    inside, tokens, proj_low, expanded, slope, taps, contract,
    grad_low, early, early_wide, grad_cells,
):
    conv_part(
        inside, own_share(tokens, proj_low.shape[0]), proj_low[...], expanded, slope, taps,
        contract, early_wide, grad_cells, early, grad_low, 0, expanded.shape[1] // 2,
    )


def small_rows(small, wide):
    mlp, sent = small
    mlp_wide, conv_wide = wide
    found = []
    for source, rows in ((mlp, 4), (sent, 4), (mlp_wide, 1), (conv_wide, 11)):
        for row in range(rows):
            for at in range(0, source.shape[1], LANES):
                found.append((source, row, at))
    return found


def conv_end_kernel(
    inside, tokens, proj_low, expanded, slope, taps, contract, early, early_wide,
    mlp_small, sent_small, mlp_wide, grad_low, pieces, send, conv_wide, grad_cells, short,
):
    channels = expanded.shape[1]
    half = channels // 2
    conv_wide[:, 0:half] = early_wide[:, 0:half]
    pieces[:, :, 0 : ROW // 2, 0:PIECE, :] = early[...]
    conv_part(
        inside, own_share(tokens, proj_low.shape[0]), proj_low[...], expanded, slope, taps,
        contract, conv_wide, grad_cells, pieces, grad_low, half, channels,
    )
    short[...] = jnp.zeros_like(short)
    places = small_rows((mlp_small, sent_small), (mlp_wide, conv_wide))
    for number, (source, row, at) in enumerate(places):
        piece, inside = number // 8, number % 8
        short[piece, inside : inside + 1, :] = source[row : row + 1, at : at + LANES]
    for piece in range(2 * SQUARE * ROW):
        value = short[piece]
        high = value.astype(BF16).astype(F32)
        pair = jnp.concatenate([high, value - high], axis=0).astype(BF16)
        core, square, row = piece // (SQUARE * ROW), piece // ROW % SQUARE, piece % ROW
        pieces[core, square, row, PIECE : PIECE + 16, :] = pair
    send[...] = pieces[1 - Here().core]


def summed(parts, short):
    total = parts[0].astype(F32)
    for part in parts[1:]:
        total = total + part.astype(F32)
    if not short:
        return total.astype(BF16)
    main = total.shape[0] - short
    value = total[main : main + 8] + total[main + 8 : main + 16]
    high = value.astype(BF16).astype(F32)
    return jnp.concatenate([total[:main], high, value - high], axis=0).astype(BF16)


def add_kernel(short, count, *refs):
    parts, outs = refs[:count], refs[count:]
    at = 0
    for out in outs:
        for step in range(out.shape[0]):
            out[step] = summed([part[at + step] for part in parts], short)
        at += out.shape[0]


def first_kernel(short, pieces, arrived, kept, send):
    here = Here()
    half = kept.shape[0]
    for step in range(2 * half):
        square, row = square_at(here, here.core, step // ROW), row_at(here, step % ROW)
        parts = (pieces[here.core, square, row], arrived[square, row])
        (kept, send)[step // half][step % half] = summed(parts, short)


def join_kernel(short, own, arrived, out):
    half = own.shape[0]
    out[0:half] = own[...]
    out[half:] = arrived[...]


def pieces_of(parts, begin=0):
    half = len(parts) // 2
    here = Here()
    for side in range(2):
        core = here.core if side == 0 else 1 - here.core
        step = begin
        for part in parts[side * half : (side + 1) * half]:
            for inside in range(part.shape[0]):
                square = square_at(here, core, step // ROW)
                yield core * SQUARE + square, row_at(here, step % ROW), part, inside
                step += 1


class Leaving:
    def __init__(self, stage, semaphores):
        self.stage, self.semaphores, self.copies = stage, semaphores, []

    def put(self, part, step, offset):
        slot = len(self.copies)
        for lane in range(ACROSS):
            low = offset + lane * HEIGHT
            self.stage[slot, :, lane * LANES : (lane + 1) * LANES] = part[
                step, low : low + HEIGHT, :
            ].astype(F32)
        return self.stage.at[slot], self.semaphores.at[slot]

    def tall(self, target, block, row, part, step, offset):
        source, semaphore = self.put(part, step, offset)
        at = pl.multiple_of((block * ROW + row) * HEIGHT, 16)
        self.copies.append(
            pltpu.make_async_copy(source, target.at[pl.ds(at, HEIGHT)], semaphore)
        )
        self.copies[-1].start()

    def wide(self, targets, block, row, part, step, offset):
        source, semaphore = self.put(part, step, offset)
        at = pl.multiple_of(block * HEIGHT, 16)
        span = ACROSS * LANES
        if len(targets) == 1:
            lanes = pl.ds(pl.multiple_of(row * span, LANES), span)
            self.copies.append(
                pltpu.make_async_copy(source, targets[0].at[pl.ds(at, HEIGHT), lanes], semaphore)
            )
            self.copies[-1].start()
            return
        last = pltpu.make_async_copy(source, targets[1].at[pl.ds(at, HEIGHT)], semaphore)
        self.copies.append(last)
        lanes = pl.ds(pl.multiple_of(jnp.minimum(row, ROW - 2) * span, LANES), span)
        others = pltpu.make_async_copy(source, targets[0].at[pl.ds(at, HEIGHT), lanes], semaphore)
        pl.when(row == ROW - 1)(last.start)
        pl.when(row < ROW - 1)(others.start)

    def wait(self):
        for copy in self.copies:
            copy.wait()


def mlp_end_kernel(*refs):
    (narrower, widener, stage, semaphores), parts = refs[-4:], refs[:-4]
    leaving = Leaving(stage, semaphores)
    for block, row, part, step in pieces_of(parts):
        leaving.tall(narrower, block, row, part, step, 0)
        leaving.wide((widener,), block, row, part, step, PIECE)
    leaving.wait()


def sent_end_kernel(*refs):
    (attention, mixing, projector, stage, semaphores), parts = refs[-5:], refs[:-5]
    leaving = Leaving(stage, semaphores)
    for block, row, part, step in pieces_of(parts):
        leaving.wide((attention, mixing), block, row, part, step, 0)
        leaving.tall(projector, block, row, part, step, PIECE)
    leaving.wait()


def conv_all_kernel(*refs):
    (*shorts, short, stage, semaphores), (expander, *parts) = refs[-15:], refs[-16:-15] + refs[:-16]
    leaving = Leaving(stage, semaphores)
    for block, row, part, step in pieces_of(parts):
        leaving.wide((expander,), block, row, part, step, 0)
        pair = part[step, PIECE : PIECE + 16, :].astype(F32)
        short[pl.ds(pl.multiple_of((block * ROW + row) * 8, 8), 8), :] = pair[0:8] + pair[8:16]
    (upshift, depthwise, depthshift, postgain, postshift, pregain, preshift, mixshift, midgain,
     midshift, wideshift, narrowshift) = shorts
    lanes = narrowshift.shape[0] // LANES
    wide_lanes = upshift.shape[0] // LANES
    number = 0
    for target in (narrowshift, midgain, midshift, mixshift, pregain, preshift, postgain, postshift):
        for lane in range(lanes):
            target[lane * LANES : (lane + 1) * LANES] = short[number, :]
            number += 1
    for target in (wideshift,) + (depthwise,) * 9 + (depthshift, upshift):
        for lane in range(wide_lanes):
            value = short[number : number + 1, :]
            if target is depthwise:
                tap = number // wide_lanes - 3
                target[tap : tap + 1, lane * LANES : (lane + 1) * LANES] = value
            else:
                target[lane * LANES : (lane + 1) * LANES] = value.reshape(LANES)
            number += 1
    leaving.wait()


def give_kernel(
    inside, middle, lit, contract, contract_bias, grad_sent, early_low, late_low, enlarge,
    own, give,
):
    half = early_low.shape[1]
    total = middle[...] + dot_nn(lit[...], contract[...]) + across(contract_bias)
    output = (total * inside[...]).astype(BF16)
    gradient = grad_sent[...].astype(F32) + dot_nt(early_low[...], enlarge[:, 0:half])
    gradient = (gradient + dot_nt(late_low[...], enlarge[:, half:])).astype(BF16)
    first = Here().section == 0
    own[...] = jnp.where(first, gradient, output)
    give[...] = jnp.where(first, output, gradient)


def ends_kernel(filled, own, arrived, ends, means, semaphores):
    share = ends.shape[0] // 2
    local, slots, width = ends.shape[1:]
    first = Here().section
    copies = []
    for source, section in ((own, first), (arrived, 1 - first)):
        for number in range(share * local):
            copies.append(
                pltpu.make_async_copy(
                    source.at[pl.ds(number * slots, slots)],
                    ends.at[section * share + number // local, number % local],
                    semaphores.at[len(copies)],
                )
            )
            copies[-1].start()
    micro = lax.broadcasted_iota(jnp.int32, (1, ends.shape[0]), 1)
    rows = [jnp.zeros((1, ends.shape[0]), F32) for _ in range(local)]
    for source, section in ((own, first), (arrived, 1 - first)):
        for number in range(share * local):
            value = source[number * slots : (number + 1) * slots, :].astype(F32)
            square = jnp.sum(value * value, axis=0, keepdims=True)
            image = (section * share + number // local) * local + number % local
            mean = jnp.sum(square, axis=1, keepdims=True) / filled[pl.ds(image, 1), 0:1]
            held = micro == section * share + number // local
            rows[number % local] = jnp.where(held, jnp.sqrt(mean), rows[number % local])
    for image in range(local):
        means[0, image : image + 1, :] = rows[image]
    for copy in copies:
        copy.wait()


WHOLE = pl.BlockSpec(memory_space=pltpu.VMEM)
ANYWHERE = pl.BlockSpec(memory_space=pl.ANY)
REMOTE = pl.BlockSpec(memory_space=pltpu.HBM)
COST = 30
ORDER = (
    "mlp.near", "conv.first", "inner.second", "mlp.far", "conv.second", "swap_ends", "inner.near",
    "conv.near", "mlp.total", "inner.far", "conv.far", "mlp.join_row", "put_ends", "inner.total",
    "conv.total", "inner.join_row", "mlp.join_square", "conv.join_row", "inner.join_square",
    "mlp.join_cores", "conv.join_square", "put_mlp", "inner.join_cores", "conv.join_cores",
    "put_inner", "put_conv",
)
COSTS = {
    "conv_first": 0, "conv_second": 30, "conv_far": 0, "conv_join_square": 30, "give": 0,
    "mlp_cores": 0, "conv_cores": 30, "conv_all": 0, "inner_cores": 30, "conv_total": 30,
    "inner_join_square": 0, "mlp_end": 0, "mlp_far": 0, "conv_near": 30, "mlp_total": 0,
}
BOTH = ("section", "dp")


def shape(dims, kind):
    return jax.ShapeDtypeStruct(dims, kind)


class Calls:
    def __init__(self):
        self.last = None

    def __call__(self, kernel, name, ins, outs, scratch=(), mb=8, us=0, hbm=(), hbm_outs=()):
        count = len(ins)
        after = () if self.last is None else (self.last,)

        def body(*refs):
            token = refs[count + len(after)]
            token[...] = jnp.zeros_like(token)
            kernel(*refs[:count], *refs[count + len(after) + 1 :])

        ins = [
            pltpu.with_memory_space_constraint(value, pltpu.HBM) if place in hbm else value
            for place, value in enumerate(ins)
        ]
        outs = [
            pltpu.HBM(out.shape, out.dtype) if place in hbm_outs else out
            for place, out in enumerate(outs)
        ]
        self.last, *result = pl.pallas_call(
            body,
            out_shape=[shape((8, LANES), F32)] + outs,
            in_specs=[
                REMOTE if place in hbm else WHOLE
                for place in range(count)
            ]
            + [ANYWHERE] * len(after),
            out_specs=[WHOLE]
            + [REMOTE if place in hbm_outs else WHOLE for place in range(len(outs))],
            scratch_shapes=list(scratch),
            cost_estimate=pl.CostEstimate(
                flops=1 + int(COSTS.get(name, us) * 1e9), bytes_accessed=1, transcendentals=0
            ),
            compiler_params=pltpu.CompilerParams(vmem_limit_bytes=mb * 1024 * 1024),
            name=name,
        )(*ins, *after)
        return result


    def fence(self, value, name):
        def body(after, value, token, out):
            token[...] = jnp.zeros_like(token)

        self.last, value = pl.pallas_call(
            body,
            out_shape=[shape((8, LANES), F32), shape(value.shape, value.dtype)],
            in_specs=[ANYWHERE] * 2,
            out_specs=[WHOLE, ANYWHERE],
            input_output_aliases={1: 1},
            cost_estimate=pl.CostEstimate(
                flops=1 + int(COSTS.get(name, 0) * 1e9), bytes_accessed=1, transcendentals=0
            ),
            compiler_params=pltpu.CompilerParams(vmem_limit_bytes=1024 * 1024),
            name=name,
        )(self.last, value)
        return value


def swapped(value, digit, step=0):
    sections, members = (lax.axis_size(axis) for axis in BOTH)
    pairs = []
    for section in range(sections):
        for member in range(members):
            if digit == "first" or digit == "second":
                across = 2 if digit == "first" else 1
            else:
                across = step if digit == "square" else 0
            if member % 2:
                across = SWAPPED[across]
            along = {"near": 4}.get(digit, digit if isinstance(digit, int) else 0)
            other = (section ^ across // 2) * members + (member ^ (across % 2 * 2 + along))
            pairs.append((section * members + member, other))
    return lax.ppermute(value, BOTH, pairs)


class Group:
    def __init__(self, name, calls, keep, send, short=0, cost=COST):
        self.name, self.calls, self.short, self.cost = name, calls, short, cost
        self.rows = keep.shape[3]
        self.parts = [keep, swapped(send, 1)]

    def call(self, kernel, what, ins, outs):
        return self.calls(
            functools.partial(kernel, self.short), f"{self.name}_{what}", ins,
            [shape((count, self.rows, LANES), BF16) for count in outs], us=self.cost,
        )

    def add(self, what, outs=1):
        pieces = [self.parts[0].shape[0] // outs] * outs
        kernel = lambda short, *refs: add_kernel(short, len(self.parts), *refs)
        return self.call(kernel, what, self.parts, pieces)

    def halve(self, what):
        keep, send = self.add(what, 2)
        self.parts = [keep, swapped(send, what)]

    def first(self):
        half = SQUARE * ROW // 2
        keep, send = self.call(first_kernel, "first", self.parts, [half] * 2)
        self.parts = [keep, swapped(send, "first")]

    def second(self):
        self.halve("second")

    def square(self):
        keep, *send = self.add("square", SQUARE)
        self.parts = [keep] + [swapped(part, "square", 1 + at) for at, part in enumerate(send)]

    def near(self):
        self.halve("near")

    def far(self):
        stride, what = 4, "far"
        while stride < lax.axis_size("dp") // 2:
            stride *= 2
            (own,) = self.add(what)
            self.parts, what = [own, swapped(own, stride)], f"over_{stride}"

    def total(self):
        (own,) = self.add("total")
        self.parts = [own, swapped(own, "near")]

    def join(self, what):
        (own,) = self.call(join_kernel, what, self.parts, [2 * self.parts[0].shape[0]])
        return own

    def join_row(self):
        own = self.join("join_row")
        self.parts = [own, swapped(own, "second")]

    def join_square(self):
        own = self.join("join_square")
        self.parts = [own, swapped(own, "first")]
        self.near_half = swapped(own, 1)

    def join_cores(self):
        far_half = self.calls.fence(self.parts[1], f"{self.name}_cores")
        self.blocks = [self.parts[0], far_half, self.near_half, swapped(far_half, 1)]

    def early(self):
        return [self.parts[0], self.near_half]

    def late(self):
        return self.blocks[1::2]

    def join_all(self):
        own = self.join("join_row")
        self.parts = [own] + [swapped(own, "square", step) for step in range(1, SQUARE)]
        self.blocks = self.parts + [swapped(part, 1) for part in self.parts]


def shards(
    entering_tokens,
    output_sensitivity,
    picture_tile_extents,
    pointwise_enlarge,
    enlarge_bias,
    channelwise_kernel,
    channelwise_conv_bias,
    pointwise_contract,
    convblock_scale,
    convblock_offset,
    attend_scale,
    attend_offset,
    query_key_proj,
    heads_output_proj,
    heads_output_bias,
    feedforward_scale,
    feedforward_offset,
    feedforward_enlarge,
    feedforward_enlarge_bias,
    feedforward_contract,
    contract_bias,
):
    micro_count, local_images, slots, width = entering_tokens.shape
    channels = pointwise_enlarge.shape[1]
    share = micro_count // 2
    images = share * local_images
    rows = images * slots
    call = Calls()
    extents = jnp.transpose(picture_tile_extents, (1, 2, 0))
    sent, expanded, slope, active, projected, inside, filled = call(
        conv_ahead_kernel, "conv_ahead",
        (extents, entering_tokens, pointwise_enlarge, enlarge_bias, channelwise_kernel,
         channelwise_conv_bias, pointwise_contract, convblock_scale, convblock_offset),
        [shape((rows, width), BF16), shape((rows, channels), BF16), shape((rows, channels), BF16),
         shape((rows, channels), BF16), shape((rows, width), F32), shape((rows, 1), F32),
         shape((micro_count * local_images, LANES), F32)],
        [pltpu.VMEM((2, rows, BLOCK), F32), pltpu.VMEM((share, local_images, slots, width), BF16)]
        + [pltpu.VMEM(value.shape, value.dtype) for value in
           (pointwise_enlarge, enlarge_bias, channelwise_kernel, channelwise_conv_bias,
            pointwise_contract, convblock_scale, convblock_offset)]
        + [pltpu.SMEM(extents.shape, jnp.int32), pltpu.SemaphoreType.DMA((6 + 2 * share + 2 * channels // BLOCK,))],
        mb=14, hbm=range(9),
    )
    qkv, weights, context, middle = call(
        attend_ahead_kernel, "attend_ahead",
        (inside, sent, attend_scale, attend_offset, query_key_proj, heads_output_proj,
         heads_output_bias),
        [shape((rows, 3 * width), BF16), shape((images * HEADS, slots, slots), BF16),
         shape((rows, width), BF16), shape((rows, width), F32)], mb=10,
    )
    halves = [shape((cores, SQUARE, ROW, 2 * PIECE, LANES), BF16) for cores in (2, 1)]
    halves[1] = shape(halves[1].shape[1:], BF16)
    lit, grad_middle, keep, send, mlp_small, mlp_wide = call(
        mlp_kernel, "mlp",
        (inside, middle, output_sensitivity, feedforward_scale, feedforward_offset, feedforward_enlarge,
         feedforward_enlarge_bias, feedforward_contract),
        [shape((rows, channels), BF16), shape((rows, width), F32)] + halves
        + [shape((8, width), F32), shape((1, channels), F32)],
        mb=18,
    )
    mlp = Group("mlp", call, keep, send)
    (grad_qkv,) = call(
        heads_back_kernel, "heads_back", (grad_middle, qkv, weights, heads_output_proj),
        [shape((rows, 3 * width), BF16)], mb=10,
    )
    mlp.first()
    grad_sent, proj_low, keep, send, sent_small = call(
        sent_back_kernel, "sent_back",
        (sent, grad_middle, grad_qkv, context, projected, active, attend_scale, attend_offset,
         query_key_proj, convblock_scale),
        [shape((rows, width), BF16), shape((rows, width), BF16)] + halves
        + [shape((8, width), F32)],
        mb=14,
    )
    inner = Group("inner", call, keep, send)
    early_pieces = shape((2, SQUARE, ROW // 2, PIECE, LANES), BF16)
    early_low, early, early_wide = call(
        conv_back_kernel, "conv_back",
        (inside, entering_tokens, proj_low, expanded, slope, channelwise_kernel,
         pointwise_contract),
        [shape((rows, channels // 2), BF16), early_pieces, shape((16, channels), F32)],
        [pltpu.VMEM((1, rows, WIDE), F32)], mb=12,
    )
    mlp.second()
    inner.first()
    halves = [shape((cores, SQUARE, ROW, PIECE + 16, LANES), BF16) for cores in (2, 1)]
    halves[1] = shape(halves[1].shape[1:], BF16)
    late_low, keep, send = call(
        conv_end_kernel, "conv_end",
        (inside, entering_tokens, proj_low, expanded, slope, channelwise_kernel,
         pointwise_contract, early, early_wide, mlp_small, sent_small, mlp_wide),
        [shape((rows, channels // 2), BF16)] + halves,
        [pltpu.VMEM((16, channels), F32), pltpu.VMEM((1, rows, WIDE), F32),
         pltpu.VMEM((2 * SQUARE * ROW, 8, LANES), F32)],
        mb=14,
    )
    conv = Group("conv", call, keep, send, 16)
    line, wide_line = shape((width,), F32), shape((channels,), F32)
    tall, wide = shape((channels, width), F32), shape((width, channels), F32)
    pieces = 2 * SQUARE * ROW

    def leaving(count):
        return [pltpu.VMEM((count, HEIGHT, ACROSS * LANES), F32), pltpu.SemaphoreType.DMA((count,))]

    def swap_ends():
        own, give = call(
            give_kernel, "give",
            (inside, middle, lit, feedforward_contract, contract_bias, grad_sent, early_low,
             late_low, pointwise_enlarge),
            [shape((rows, width), BF16)] * 2, mb=10, us=COST,
        )
        return own, lax.ppermute(give, "section", [(0, 1), (1, 0)])

    def put_ends(own, arrived):
        return call(
            ends_kernel, "ends", (filled, own, arrived),
            [shape(entering_tokens.shape, BF16), shape((1, local_images, micro_count), F32)],
            [pltpu.SemaphoreType.DMA((micro_count * local_images,))], hbm_outs=(0,), us=COST,
        )

    def put_mlp():
        return call(
            mlp_end_kernel, "mlp_end", mlp.blocks, [tall, wide], leaving(2 * pieces), mb=12,
            hbm_outs=(0, 1), us=COST,
        )

    def put_inner():
        return call(
            sent_end_kernel, "sent_end", inner.blocks,
            [shape((width, 3 * width), F32), shape((width, width), F32), tall],
            leaving(2 * pieces), mb=12, hbm_outs=(0, 1, 2), us=COST,
        )

    def put_conv():
        return call(
            conv_all_kernel, "conv_all", conv.blocks,
            [wide, wide_line, shape((9, channels), F32), wide_line] + [line] * 7
            + [wide_line, line],
            [pltpu.VMEM((pieces * 8, LANES), F32)] + leaving(pieces), hbm_outs=(0,), us=COST,
        )

    done = {}
    for step in ORDER:
        name, _, what = step.partition(".")
        if what:
            getattr({"mlp": mlp, "inner": inner, "conv": conv}[name], what)()
        elif name == "swap_ends":
            done[name] = swap_ends()
        elif name == "put_ends":
            done[name] = put_ends(*done["swap_ends"])
        else:
            done[name] = {"put_mlp": put_mlp, "put_inner": put_inner, "put_conv": put_conv}[name]()
    narrower, widener = done["put_mlp"]
    attention, mixing, projector = done["put_inner"]
    (expander, upshift, depthwise, depthshift, postgain, postshift, pregain, preshift, mixshift,
     midgain, midshift, wideshift, narrowshift) = done["put_conv"]
    ends, means = done["put_ends"]
    means = jnp.transpose(means, (0, 2, 1))
    return (
        ends[None], means, expander, upshift, depthwise, depthshift, projector, postgain,
        postshift, pregain, preshift, attention, mixing, mixshift, midgain, midshift, widener,
        wideshift, narrower, narrowshift,
    )


def solution(mesh):
    tokens = P(None, "dp", None, None)
    placed = (tokens, tokens, P(None, "dp", None)) + (P(),) * 18
    return jax.shard_map(
        shards,
        mesh=mesh,
        in_specs=placed,
        out_specs=(P("section", None, "dp", None, None), P("section", None, "dp")) + (P(),) * 18,
        check_vma=False,
    )
```
